32 devices in a mesh: replica: 2 (over x), fsdp: 16 (over z, y, core).
Axes of the slice: x: 2, y: 2, z: 4, core: 2. Of those that a mesh axis runs over, the one named last changes fastest.
Arguments:
- tokens: bfloat16 [4096, 2048], P(('replica', 'fsdp')), may hold values from -6 to 6
- w_qkv: bfloat16 [2048, 6144], P('fsdp'), may hold values from -0.125 to 0.125
- w_out: bfloat16 [2048, 2048], P('fsdp'), may hold values from -0.125 to 0.125
- w_gate_up: bfloat16 [2048, 16384], P('fsdp'), may hold values from -0.125 to 0.125
- w_down_t: bfloat16 [2048, 8192], P('fsdp'), may hold values from -0.0625 to 0.0625
- gains: bfloat16 [2048, 4], P('fsdp'), may hold values from 0.25 to 1.75
- starts: int32 [4096], P(('replica', 'fsdp')), may hold values from 0 to 1, as said below
- cotangent: bfloat16 [4096, 2048], P(('replica', 'fsdp')), may hold values from -6 to 6
Outputs:
- mixed: bfloat16 [4096, 2048], P(('replica', 'fsdp'))
- grad_tokens: float32 [4096, 2048], P(('replica', 'fsdp'))
- grad_qkv: float32 [2048, 6144], P('fsdp')
- grad_out: float32 [2048, 2048], P('fsdp')
- grad_gate_up: float32 [2048, 16384], P('fsdp')
- grad_down_t: float32 [2048, 8192], P('fsdp')
- grad_gains: float32 [2048, 4], P('fsdp')
The draws below stay inside these ranges and needn't reach their ends.
Inputs may be any that keep to these rules, and one draw needn't show every extreme that they name: `starts`: the first row of each block of 128 rows is 1, so sequences lie whole on a device; in some block no other row is 1, so one sequence fills all 128 rows.
All inputs are finite; a program needn't handle non-finite values.
Results may differ from the reference program's by a relative error of at most 0.017.
Values may be sent and summed in bfloat16 or wider, within the bound.
A program may use at most 1 GiB of HBM per device.

```python
import math
import jax
import jax.numpy as jnp
from jax import lax

D = 2048
HEADS = 16
HD = 128
FF = 8192
ROWS = 128
TOKENS = 4096


def draw_starts(key, part):
    key = jax.random.fold_in(key, 11)
    first_key, second_key = jax.random.split(key)
    row_index = jnp.arange(TOKENS, dtype=jnp.int32)
    cut_marks = (jax.random.randint(first_key, (TOKENS,), 0, max(2, ROWS // 3)) == 0).astype(jnp.int32)
    whole_block = jax.random.randint(second_key, (), 0, TOKENS // ROWS)
    start_marks = jnp.where(row_index % ROWS == 0, 1, jnp.where(row_index // ROWS == whole_block, 0, cut_marks))
    return start_marks.astype(jnp.int32)


def spiked(values, key, source, target, blocks, factor):
    owner, partner = [(jnp.arange(values.shape[dim]) // (values.shape[dim] // blocks)).reshape([-1 if axis == dim else 1 for axis in range(values.ndim)]) for dim in (source, target)]
    chosen = jax.random.permutation(key, blocks)[partner]
    strong = (owner == chosen) | (owner == (partner + blocks // 2) % blocks)
    return jnp.where(strong, factor * values, values)


def levels(key, dims, cuts, smallest, top_value):
    gain = 1.0
    for dim, parts in cuts:
        heights = jax.random.uniform(jax.random.fold_in(jax.random.fold_in(key, 6), dim), (parts,), jnp.float32, smallest / len(cuts), top_value / len(cuts))
        gain = gain * jnp.repeat(jnp.exp(heights), dims[dim] // parts).reshape((-1,) + (1,) * (len(dims) - 1 - dim))
    return gain


def scatter_about(own_key, shape, deviation, reach, pieces=(), kind=jnp.bfloat16):
    result = jax.random.normal(own_key, shape, jnp.float32) * deviation
    if len(pieces) > 0:
        result = levels(own_key, shape, pieces, -0.22, 0.18) * result
    return jnp.clip(result, min=-reach, max=reach).astype(kind)


def bell_draw_with(stream_key, extent, scale, reach, shards, heavy, kind=jnp.bfloat16):
    drawn = scale * jax.random.normal(stream_key, extent, jnp.float32)
    if shards:
        drawn = drawn * levels(stream_key, extent, shards, -0.22, 0.18)
    return jnp.clip(spiked(drawn, jax.random.fold_in(stream_key, 3), *heavy), -reach, reach).astype(kind)


def setup_inputs(seed: int = 0) -> dict:
    splits = jax.random.split(jax.random.key(seed), 9)
    tokens = bell_draw_with(splits[0], (TOKENS, D), 1.0, 6.0, ((0, 32),), (0, 1, 32, 2.75))
    w_qkv = scatter_about(splits[1], (D, 3 * D), D ** -0.5, 0.125, ((0, 16),))
    w_out = scatter_about(splits[2], (D, D), D ** -0.5, 0.125, ((0, 16),))
    w_gate_up = scatter_about(splits[3], (D, 2 * FF), D ** -0.5, 0.125, ((0, 16),))
    w_down_t = scatter_about(splits[4], (D, FF), FF ** -0.5, 0.0625, ((0, 16),))
    gains = jnp.clip(1.0 + 0.15 * jax.random.normal(splits[5], (D, 4), jnp.float32), 0.25, 1.75).astype(jnp.bfloat16)
    starts = draw_starts(jax.random.fold_in(splits[8], 71), 0)
    cotangent = bell_draw_with(splits[7], (TOKENS, D), 1.0, 6.0, ((0, 32),), (0, 1, 32, 2.75))
    return dict(tokens=tokens, w_qkv=w_qkv, w_out=w_out, w_gate_up=w_gate_up, w_down_t=w_down_t, gains=gains, starts=starts, cotangent=cotangent)


epsilon = 1e-06
theta_base = 500000.0

@jax.custom_vjp
def low(v):
    return lax.optimization_barrier(v.astype(jnp.bfloat16)).astype(jnp.float32)

@jax.custom_vjp
def low_back(v):
    return v

def low_keep(v):
    return (low(v), None)

def low_pass(kept, grad):
    return (grad,)

def back_keep(v):
    return (v, None)

def back_low(kept, grad):
    return (low(grad),)
low.defvjp(low_keep, low_pass)
low_back.defvjp(back_keep, back_low)

def product(operand, matrix):
    return jnp.dot(operand, matrix, precision=lax.Precision.HIGHEST)

def rms_norm(values, scales):
    return values * lax.rsqrt(lax.optimization_barrier(jnp.mean(values * values, axis=-1, keepdims=True)) + epsilon) * scales

def rope_tables(positions):
    frequency = theta_base ** (-2.0 * jnp.arange(HD // 2).astype(jnp.float32) / HD)
    angles = positions[:, None] * frequency[None, :]
    return (jnp.cos(angles)[:, None, :], jnp.sin(angles)[:, None, :])

def rotate(values, cos_table, sin_table):
    half_width = values.shape[-1] // 2
    former = values[..., :half_width]
    latter = values[..., half_width:]
    return jnp.concatenate([former * cos_table - latter * sin_table, latter * cos_table + former * sin_table], axis=-1)

def attend(block_inputs):
    queries, keys_in, values, seq_begin = block_inputs
    local_rows = jnp.arange(ROWS, dtype=jnp.int32)
    allowed = (local_rows[None, :] <= local_rows[:, None]) & (local_rows[None, :] >= seq_begin[:, None])
    scores = jnp.einsum('qhd,khd->hqk', queries.reshape(ROWS, HEADS, HD), keys_in.reshape(ROWS, HEADS, HD), precision=lax.Precision.HIGHEST) / math.sqrt(HD)
    scores = low_back(scores)
    scores = jnp.where(allowed[None, :, :], scores, -1e+30)
    peaks = lax.optimization_barrier(jnp.max(scores, axis=-1, keepdims=True))
    exponent = jnp.exp(scores - peaks)
    attention = exponent / lax.optimization_barrier(jnp.sum(exponent, axis=-1, keepdims=True))
    attention = low(attention)
    mixed_heads = jnp.einsum('hqk,khd->qhd', attention, values.reshape(ROWS, HEADS, HD), precision=lax.Precision.HIGHEST)
    return mixed_heads.reshape(ROWS, D)

def block_forward(layer_input, w_qkv, w_out, w_gate_up, w_down_t, gains, cos_table, sin_table, seq_begin):
    count_rows = layer_input.shape[0]
    projected = low_back(product(layer_input, w_qkv))
    queries = rms_norm(projected[:, :D], gains[:, 0])
    keys_in = rms_norm(projected[:, D:2 * D], gains[:, 1])
    values = low(projected[:, 2 * D:])
    queries = low(rotate(queries.reshape(count_rows, HEADS, HD), cos_table, sin_table).reshape(count_rows, D))
    keys_in = low(rotate(keys_in.reshape(count_rows, HEADS, HD), cos_table, sin_table).reshape(count_rows, D))
    blocks = count_rows // ROWS
    attended = lax.map(jax.checkpoint(attend), (queries.reshape(blocks, ROWS, D), keys_in.reshape(blocks, ROWS, D), values.reshape(blocks, ROWS, D), seq_begin.reshape(blocks, ROWS)))
    attended = low(low_back(attended.reshape(count_rows, D)))
    branch = low_back(product(attended, w_out))
    middle = layer_input + rms_norm(branch, gains[:, 2])
    gate_up = low_back(product(low(middle), w_gate_up))
    hidden = low(jax.nn.silu(gate_up[:, :FF]) * gate_up[:, FF:])
    feed_out = low_back(product(hidden, w_down_t.T))
    return middle + rms_norm(feed_out, gains[:, 3])

def reference(tokens, w_qkv, w_out, w_gate_up, w_down_t, gains, starts, cotangent):
    weights = (w_qkv.astype(jnp.float32), w_out.astype(jnp.float32), w_gate_up.astype(jnp.float32), w_down_t.astype(jnp.float32), gains.astype(jnp.float32))
    blocks = TOKENS // ROWS
    group_blocks = math.gcd(blocks, max(1, 4096 // ROWS))
    groups = blocks // group_blocks
    group_rows = group_blocks * ROWS
    local_rows = jnp.arange(ROWS, dtype=jnp.int32)
    start_marks = starts.reshape(blocks, ROWS)
    seq_begin = lax.cummax(jnp.where(start_marks == 1, local_rows[None, :], 0), axis=1)
    positions = (local_rows[None, :] - seq_begin).astype(jnp.float32)
    inputs_all = tokens.astype(jnp.float32).reshape(groups, group_rows, D)
    cotangents = cotangent.astype(jnp.float32).reshape(groups, group_rows, D)

    def advance(running, slices):
        group_inputs, group_cotangent, group_begin, group_positions = slices
        cos_table, sin_table = rope_tables(group_positions)

        def forward(layer_input, weight_qkv, weight_out, weight_gate_up, weight_down, weight_gains):
            return block_forward(layer_input, weight_qkv, weight_out, weight_gate_up, weight_down, weight_gains, cos_table, sin_table, group_begin)
        outputs, pullback = jax.vjp(forward, group_inputs, *weights)
        gradients = pullback(group_cotangent)
        running = tuple((earlier + increment for earlier, increment in zip(running, gradients[1:])))
        return (running, (outputs, gradients[0]))
    initial = tuple((jnp.zeros_like(matrix) for matrix in weights))
    running, (outputs, input_grads) = lax.scan(advance, initial, (inputs_all, cotangents, seq_begin.reshape(groups, group_rows), positions.reshape(groups, group_rows)))
    mixed = outputs.reshape(TOKENS, D).astype(jnp.bfloat16)
    return (mixed, input_grads.reshape(TOKENS, D), running[0], running[1], running[2], running[3], running[4])
```

```python
import math

import jax
import jax.numpy as jnp
from jax import lax
from jax.sharding import Mesh, PartitionSpec as P

HD = 128

epsilon = 1e-06
theta_base = 500000.0

CUBE = ("x", "zl", "y", "c")
SIDE = ("zl", "y", "c")
OWNERS = ("zh", "zl", "y", "c")
EVERY = ("x", "zh", "zl", "y", "c")
MEMBERS = 16
SIDES = 8


def normalize(values, scales):
    inverse = lax.rsqrt(jnp.mean(values * values, axis=-1, keepdims=True) + epsilon)
    return (values * inverse * scales, inverse)


def norm_back(upstream, values, inverse, scales):
    unit_rows = values * inverse
    scaled = upstream * scales
    value_grad = inverse * (
        scaled - unit_rows * jnp.mean(scaled * unit_rows, axis=-1, keepdims=True)
    )
    return (value_grad, jnp.sum(upstream * unit_rows, axis=0))


def rope_tables(positions):
    frequency = theta_base ** (-2.0 * jnp.arange(HD // 2).astype(jnp.float32) / HD)
    angles = positions[:, None] * frequency[None, :]
    return (jnp.cos(angles)[:, None, :], jnp.sin(angles)[:, None, :])


def rotate(values, cos_table, sin_table):
    half_width = values.shape[-1] // 2
    former = values[..., :half_width]
    latter = values[..., half_width:]
    return jnp.concatenate(
        [former * cos_table - latter * sin_table, latter * cos_table + former * sin_table], axis=-1
    )


def contract_last(operand, matrix):
    return lax.dot_general(
        operand, matrix, (((1,), (1,)), ((), ())), preferred_element_type=jnp.float32
    )


def contract_first(operand, matrix):
    return lax.dot_general(
        operand, matrix, (((0,), (0,)), ((), ())), preferred_element_type=jnp.float32
    )


def masked_scores(query_bf, key_bf, allowed, score_scale):
    scores = (
        jnp.einsum("qhd,khd->hqk", query_bf, key_bf, preferred_element_type=jnp.float32)
        * score_scale
    )
    return jnp.where(allowed[None, :, :], scores, -1e30)


def gather_cube(block):
    return lax.all_gather(block, CUBE, axis=0, tiled=True)


def scatter_cube(partial):
    return lax.psum_scatter(
        partial.astype(jnp.bfloat16), CUBE, scatter_dimension=0, tiled=True
    ).astype(jnp.float32)


def swap_groups(blocks):
    groups = lax.axis_size("zh")
    if groups == 2:
        mine = lax.axis_index("zh")
        away = lax.dynamic_index_in_dim(blocks, 1 - mine, 0, keepdims=False)
        came = lax.ppermute(away, "zh", [(0, 1), (1, 0)])
        kept = lax.dynamic_index_in_dim(blocks, mine, 0, keepdims=False)
        return jnp.where(mine == 0, jnp.stack([kept, came]), jnp.stack([came, kept]))
    return lax.all_to_all(blocks, "zh", 0, 0, tiled=True)


def columns_of(weight, parts):
    rows, width = weight.shape
    piece = width // (parts * MEMBERS)
    groups = lax.axis_size("zh")
    half = lax.dynamic_index_in_dim(
        weight.reshape(rows, parts, 2, SIDES * piece), lax.axis_index("x"), 2, keepdims=False
    )
    if groups == 2:
        came = lax.ppermute(half, "zh", [(0, 1), (1, 0)])
        both = jnp.where(lax.axis_index("zh") == 0, jnp.stack([half, came]), jnp.stack([came, half]))
    else:
        both = lax.all_gather(half, "zh", axis=0)
    blocks = both.reshape(groups, rows, parts, SIDES, piece).transpose(3, 0, 1, 2, 4)
    came = lax.all_to_all(blocks, SIDE, 0, 0, tiled=True)
    return came.transpose(1, 0, 2, 3, 4).reshape(groups * SIDES * rows, parts * piece)


def owners_sum(grad_columns, parts):
    depth, width = grad_columns.shape
    piece = width // parts
    groups = lax.axis_size("zh")
    rows = depth // (groups * SIDES)
    blocks = grad_columns.astype(jnp.bfloat16).reshape(groups, SIDES, rows, parts, piece)
    came = lax.all_to_all(blocks, SIDE, 1, 1, tiled=True)
    terms = swap_groups(came)
    total = jnp.sum(terms.astype(jnp.float32), axis=0).astype(jnp.bfloat16)
    both = lax.all_gather(total, "x", axis=0)
    return (
        both.transpose(2, 3, 0, 1, 4).reshape(rows, parts * MEMBERS * piece).astype(jnp.float32)
    )


def shards(tokens, w_qkv, w_out, w_gate_up, w_down_t, gains, starts, cotangent):
    count_rows, width = tokens.shape
    head_count = width // HD
    score_scale = 1.0 / math.sqrt(HD)
    local_rows = jnp.arange(count_rows, dtype=jnp.int32)
    seq_begin = lax.cummax(jnp.where(starts == 1, local_rows, 0), axis=0)
    positions = (local_rows - seq_begin).astype(jnp.float32)
    cos_table, sin_table = rope_tables(positions)
    allowed = (local_rows[None, :] <= local_rows[:, None]) & (
        local_rows[None, :] >= seq_begin[:, None]
    )
    full_gains = lax.all_gather(gains, OWNERS, axis=0, tiled=True)
    gain_cols = full_gains.astype(jnp.float32)
    tokens_all = gather_cube(tokens)
    qkv_cols = columns_of(w_qkv, 3)
    full_out = lax.all_gather(w_out, OWNERS, axis=0, tiled=True)
    gate_up_cols = columns_of(w_gate_up, 2)
    down_cols = columns_of(w_down_t, 1)
    hidden_width = down_cols.shape[1]

    projected_cols = jnp.dot(
        tokens_all, qkv_cols, preferred_element_type=jnp.float32
    ).astype(jnp.bfloat16)
    projected = lax.all_to_all(
        projected_cols.reshape(MEMBERS, count_rows, 3, width // MEMBERS), CUBE, 0, 0, tiled=True
    )
    projected = projected.transpose(1, 2, 0, 3).reshape(count_rows, 3, width)
    query_raw = projected[:, 0].astype(jnp.float32)
    key_raw = projected[:, 1].astype(jnp.float32)
    value_bf = projected[:, 2].reshape(count_rows, head_count, HD)
    query_norm, query_inv = normalize(query_raw, gain_cols[:, 0])
    key_norm, key_inv = normalize(key_raw, gain_cols[:, 1])
    query_bf = rotate(query_norm.reshape(count_rows, head_count, HD), cos_table, sin_table).astype(
        jnp.bfloat16
    )
    key_bf = rotate(key_norm.reshape(count_rows, head_count, HD), cos_table, sin_table).astype(
        jnp.bfloat16
    )
    scores = masked_scores(query_bf, key_bf, allowed, score_scale)
    peaks = jnp.max(scores, axis=-1, keepdims=True)
    exponent = jnp.exp(scores - peaks)
    attention_f32 = exponent / jnp.sum(exponent, axis=-1, keepdims=True)
    attention = attention_f32.astype(jnp.bfloat16)
    attended = (
        jnp.einsum("hqk,khd->qhd", attention, value_bf, preferred_element_type=jnp.float32)
        .reshape(count_rows, width)
        .astype(jnp.bfloat16)
    )
    attended_all = gather_cube(attended)
    branch = jnp.dot(attended, full_out, preferred_element_type=jnp.float32)
    branch_norm, branch_inv = normalize(branch, gain_cols[:, 2])
    middle = tokens.astype(jnp.float32) + branch_norm
    middle_all = gather_cube(middle.astype(jnp.bfloat16))
    gate_up = jnp.dot(middle_all, gate_up_cols, preferred_element_type=jnp.float32)
    gate_part = gate_up[:, :hidden_width]
    up_part = gate_up[:, hidden_width:]
    sigmoid_gate = jax.nn.sigmoid(gate_part)
    hidden_bf = (gate_part * sigmoid_gate * up_part).astype(jnp.bfloat16)
    feed_out = scatter_cube(contract_last(hidden_bf, down_cols))
    feed_norm, feed_inv = normalize(feed_out, gain_cols[:, 3])
    mixed = (middle + feed_norm).astype(jnp.bfloat16)

    upstream = cotangent.astype(jnp.float32)
    feed_grad, gain_feed = norm_back(upstream, feed_out, feed_inv, gain_cols[:, 3])
    feed_all = gather_cube(feed_grad.astype(jnp.bfloat16))
    grad_down_t = owners_sum(contract_first(feed_all, hidden_bf), 1)
    hidden_grad = jnp.dot(feed_all, down_cols, preferred_element_type=jnp.float32)
    gate_grad = hidden_grad * up_part * sigmoid_gate * (1.0 + gate_part * (1.0 - sigmoid_gate))
    up_grad = hidden_grad * gate_part * sigmoid_gate
    gate_up_bf = jnp.concatenate([gate_grad, up_grad], axis=1).astype(jnp.bfloat16)
    grad_gate_up = owners_sum(contract_first(middle_all, gate_up_bf), 2)
    middle_grad = upstream + scatter_cube(contract_last(gate_up_bf, gate_up_cols))
    branch_grad, gain_branch = norm_back(middle_grad, branch, branch_inv, gain_cols[:, 2])
    branch_bf = branch_grad.astype(jnp.bfloat16)
    branch_cols = lax.all_to_all(
        branch_bf.reshape(count_rows, MEMBERS, width // MEMBERS), CUBE, 1, 0, tiled=True
    ).reshape(MEMBERS * count_rows, width // MEMBERS)
    grad_out = owners_sum(contract_first(attended_all, branch_cols), 1)
    attended_grad = (
        contract_last(branch_bf, full_out).astype(jnp.bfloat16).reshape(count_rows, head_count, HD)
    )
    prob_grad = jnp.einsum(
        "qhd,khd->hqk", attended_grad, value_bf, preferred_element_type=jnp.float32
    )
    score_bf = (
        attention_f32 * (prob_grad - jnp.sum(attention_f32 * prob_grad, axis=-1, keepdims=True))
    ).astype(jnp.bfloat16)
    value_grad = jnp.einsum(
        "hqk,qhd->khd", attention, attended_grad, preferred_element_type=jnp.float32
    )
    query_grad = (
        jnp.einsum("hqk,khd->qhd", score_bf, key_bf, preferred_element_type=jnp.float32)
        * score_scale
    )
    key_grad = (
        jnp.einsum("hqk,qhd->khd", score_bf, query_bf, preferred_element_type=jnp.float32)
        * score_scale
    )
    query_grad = rotate(query_grad, cos_table, -sin_table).reshape(count_rows, width)
    key_grad = rotate(key_grad, cos_table, -sin_table).reshape(count_rows, width)
    query_raw_grad, gain_query = norm_back(query_grad, query_raw, query_inv, gain_cols[:, 0])
    key_raw_grad, gain_key = norm_back(key_grad, key_raw, key_inv, gain_cols[:, 1])
    projected_bf = jnp.stack(
        [query_raw_grad, key_raw_grad, value_grad.reshape(count_rows, width)], axis=1
    ).astype(jnp.bfloat16)
    projected_cols_grad = lax.all_to_all(
        projected_bf.reshape(count_rows, 3, MEMBERS, width // MEMBERS).transpose(2, 0, 1, 3),
        CUBE, 0, 0, tiled=True,
    ).reshape(MEMBERS * count_rows, 3 * width // MEMBERS)
    grad_qkv = owners_sum(contract_first(tokens_all, projected_cols_grad), 3)
    grad_tokens = middle_grad + scatter_cube(contract_last(projected_cols_grad, qkv_cols))
    gain_terms = jnp.stack([gain_query, gain_key, gain_branch, gain_feed], axis=0)
    gain_sums = lax.psum(gain_terms, EVERY)
    owner = lax.axis_index(OWNERS)
    grad_gains = lax.dynamic_slice_in_dim(
        gain_sums, owner * gains.shape[0], gains.shape[0], axis=1
    ).T
    return (mixed, grad_tokens, grad_qkv, grad_out, grad_gate_up, grad_down_t, grad_gains)


def solution(mesh):
    sizes = dict(mesh.shape)
    groups = sizes["fsdp"] // SIDES
    finer = Mesh(mesh.devices.reshape(2, groups, 2, 2, 2), EVERY)
    return jax.shard_map(
        shards,
        mesh=finer,
        in_specs=(
            P(EVERY, None),
            P(OWNERS, None),
            P(OWNERS, None),
            P(OWNERS, None),
            P(OWNERS, None),
            P(OWNERS, None),
            P(EVERY),
            P(EVERY, None),
        ),
        out_specs=(
            P(EVERY, None),
            P(EVERY, None),
            P(OWNERS, None),
            P(OWNERS, None),
            P(OWNERS, None),
            P(OWNERS, None),
            P(OWNERS, None),
        ),
        check_vma=False,
    )
```

```python
import functools
import math

import jax
import jax.numpy as jnp
from jax import lax
from jax.experimental import pallas as pl
from jax.experimental.pallas import tpu as pltpu
from jax.sharding import Mesh, PartitionSpec as P

HD = 128

epsilon = 1e-06
theta_base = 500000.0

OWNERS = ("zh", "zl", "y", "c")
EVERY = ("x", "zh", "zl", "y", "c")
MEMBERS = 16
SIDES = 8
SIDE_BITS = {"zl": 4, "y": 2, "c": 1}
BITS = {"x": 8, "zl": 4, "y": 2, "c": 1}
MESH = pl.DeviceIdType.MESH
MIB = 1 << 20


def thirds(rows):
    unit = rows // 8
    return (
        (("x", "y", "zl"), 0, 3 * unit),
        (("y", "zl", "x"), 3 * unit, 3 * unit),
        (("zl", "x", "y"), 6 * unit, 2 * unit),
    )


def halves(rows, *order):
    return ((order, 0, rows // 2), (order, rows // 2, rows // 2))


PEERS = [tuple(n for n in BITS if m & BITS[n]) for m in range(1, MEMBERS)]
SIDE_PEERS = [tuple(n for n in SIDE_BITS if m & SIDE_BITS[n]) for m in range(SIDES)]


def place():
    return {name: lax.axis_index(name) for name in EVERY}


def flip(here, *names):
    return {name: 1 - here[name] for name in names}


def with_bits(here, names, bits=BITS):
    index = 0
    for name, bit in bits.items():
        index = index + bit * ((1 - here[name]) if name in names else here[name])
    return index


def subset(order, mask):
    return tuple(name for k, name in enumerate(order) if mask >> k & 1)


def greet(devices):
    barrier = pltpu.get_barrier_semaphore()
    for device in devices:
        pl.semaphore_signal(barrier, inc=1, device_id=device, device_id_type=MESH)
    pl.semaphore_wait(barrier, len(devices))


def owner_at(here, groups, step, names):
    device = flip(here, *names)
    if step:
        device["zh"] = lax.rem(here["zh"] + step, groups)
    return device


class Load:
    def __init__(self, kind, source, parts=1):
        self.kind = kind
        self.source = source
        self.parts = parts
        groups = self.groups = lax.axis_size("zh")
        shape, kept = source.shape, source.dtype
        if kind == "columns":
            self.rows = shape[0]
            self.piece = shape[1] // (parts * MEMBERS)
            shape = (groups * SIDES * shape[0], parts * self.piece)
        elif kind == "owners":
            self.rows = shape[0] // (groups * SIDES)
            self.piece = shape[1] // parts
            shape = (groups, self.rows, parts * SIDES * self.piece)
        elif kind == "plane":
            shape = (groups * SIDES,) + shape
        elif kind == "cube":
            shape = (MEMBERS,) + shape
        self.out = jax.ShapeDtypeStruct(shape, kept)
        self.space = pltpu.VMEM if kind in ("plane", "cube") else pl.ANY
        self.count = len(self.moves(None))

    def moves(self, here):
        if self.kind == "zh":
            return [((1, ()), 0)]
        if self.kind == "x":
            return [((0, ("x",)), 0)]
        if self.kind == "cube":
            return [((0, names), 0) for names in [()] + PEERS]
        return [
            ((step, names), part)
            for step in range(self.groups)
            for names in SIDE_PEERS
            for part in range(self.parts)
        ]

    def scratch(self):
        return [pltpu.SemaphoreType.DMA((self.count,)), pltpu.SemaphoreType.DMA((self.count,))]

    def devices(self, here):
        return [
            (step, names) for (step, names), part in self.moves(here) if part == 0 and (step or names)
        ]

    def views(self, here, src, dst, step, names, part):
        if self.kind in ("zh", "x"):
            return src, dst, dst
        if self.kind == "cube":
            return src, dst.at[with_bits(here, ())], dst.at[with_bits(here, names)]
        groups, side = self.groups, with_bits(here, (), SIDE_BITS)
        other = with_bits(here, names, SIDE_BITS)
        there = lax.rem(here["zh"] + step, groups)
        whence = lax.rem(here["zh"] + groups - step, groups)
        me, he = here["zh"] * SIDES + side, whence * SIDES + other
        if self.kind == "plane":
            return src, dst.at[me], dst.at[he]
        rows, piece = self.rows, self.piece

        def at(start, size):
            return pl.ds(pl.multiple_of(start, size), size)

        if self.kind == "columns":
            first = part * MEMBERS + here["x"] * SIDES + other
            columns = pl.ds(part * piece, piece)
            return (
                src.at[:, at(first * piece, piece)],
                dst.at[at(me * rows, rows), columns],
                dst.at[at(he * rows, rows), columns],
            )
        target = there * SIDES + other
        return (
            src.at[at(target * rows, rows), pl.ds(part * piece, piece)],
            dst.at[here["zh"], :, at((part * SIDES + side) * piece, piece)],
            dst.at[whence, :, at((part * SIDES + other) * piece, piece)],
        )

    def copies(self, here, src, dst, send, recv):
        result = []
        for index, ((step, names), part) in enumerate(self.moves(here)):
            source, target, landing = self.views(here, src, dst, step, names, part)
            if not step and not names:
                copy = pltpu.make_async_copy(source, target, send.at[index])
                result.append((copy, None))
                continue
            copy = pltpu.make_async_remote_copy(
                src_ref=source, dst_ref=target, send_sem=send.at[index], recv_sem=recv.at[index],
                device_id=owner_at(here, self.groups, step, names), device_id_type=MESH,
            )
            result.append((copy, pltpu.make_async_copy(landing, landing, recv.at[index])))
        return result


class Cargo:
    def __init__(self, loads):
        self.loads = loads
        self.n = len(loads)
        self.sources = [load.source for load in loads]
        self.specs = [pl.BlockSpec(memory_space=load.space) for load in loads]
        self.outs = [load.out for load in loads]
        self.scratch = [s for load in loads for s in load.scratch()]

    def greet(self, here, names):
        reached = {(0, n) for n in names}
        for load in self.loads:
            reached |= set(load.devices(here))
        groups = lax.axis_size("zh")
        greet([owner_at(here, groups, step, n) for step, n in sorted(reached)])

    def start(self, here, sources, targets, semaphores):
        self.copies = []
        for k, load in enumerate(self.loads):
            self.copies += load.copies(
                here, sources[k], targets[k], semaphores[2 * k], semaphores[2 * k + 1]
            )
        for copy, _ in self.copies:
            copy.start()

    def wait(self):
        for copy, landing in self.copies:
            if landing is None:
                copy.wait()
            else:
                landing.wait()
        for copy, landing in self.copies:
            if landing is not None:
                copy.wait_send()


NEAR = [("x",), ("zl",), ("y",), ("c",)]


def call(body, name, ident, cargo, operand, out, out_space, scratch, vmem=32):
    return pl.pallas_call(
        body,
        out_shape=[out] + cargo.outs,
        in_specs=[pl.BlockSpec(memory_space=pl.ANY)] + cargo.specs,
        out_specs=[pl.BlockSpec(memory_space=out_space)] + cargo.specs,
        scratch_shapes=scratch + cargo.scratch,
        compiler_params=pltpu.CompilerParams(
            collective_id=ident, has_side_effects=True, vmem_limit_bytes=vmem * MIB
        ),
        cost_estimate=pl.CostEstimate(flops=0, bytes_accessed=100 * MIB, transcendentals=0),
        name=name,
    )(operand, *cargo.sources)


def gather_kernel(orders, cargo, x_ref, *refs):
    n = cargo.n
    sources, o_ref, targets = refs[:n], refs[n], refs[n + 1 : 2 * n + 1]
    send_sem, recv_sem, core_send, core_recv, own_sem = refs[2 * n + 1 : 2 * n + 6]
    here = place()
    spans = [pl.ds(r0, size) for _, r0, size in orders]
    orders = [o for o, _, _ in orders]
    pieces = range(len(orders))
    cargo.greet(here, NEAR)
    own = pltpu.make_async_copy(x_ref, o_ref.at[with_bits(here, ())], own_sem)

    def piece_of(p, mask):
        spot = o_ref.at[with_bits(here, subset(orders[p], mask)), spans[p]]
        return (x_ref.at[spans[p]] if mask == 0 else spot), spot

    def over(p, mask, k):
        source, spot = piece_of(p, mask)
        return pltpu.make_async_remote_copy(
            src_ref=source, dst_ref=spot,
            send_sem=send_sem.at[p, mask | 1 << k], recv_sem=recv_sem.at[p, mask | 1 << k],
            device_id=flip(here, orders[p][k]), device_id_type=MESH,
        )

    def across(p, mask):
        source, spot = piece_of(p, mask)
        return pltpu.make_async_remote_copy(
            src_ref=source, dst_ref=spot,
            send_sem=core_send.at[p, mask], recv_sem=core_recv.at[p, mask],
            device_id=flip(here, "c"), device_id_type=MESH,
        )

    sent = []
    for mask in range(8):
        for p in pieces:
            if mask:
                _, spot = piece_of(p, mask)
                pltpu.make_async_copy(spot, spot, recv_sem.at[p, mask]).wait()
            for k in range(mask.bit_length(), 3):
                sent.append(over(p, mask, k))
                sent[-1].start()
        for p in pieces:
            sent.append(across(p, mask))
            sent[-1].start()
        if mask == 0:
            own.start()
            cargo.start(here, sources, targets, refs[2 * n + 6 :])
    for mask in range(8):
        for p in pieces:
            spot = o_ref.at[with_bits(here, subset(orders[p], mask) + ("c",)), spans[p]]
            pltpu.make_async_copy(spot, spot, core_recv.at[p, mask]).wait()
    for copy in sent:
        copy.wait_send()
    own.wait()
    cargo.wait()


def gather_cube(block, ident, loads=(), orders=None):
    rows, width = block.shape
    orders = orders or thirds(rows)
    cargo = Cargo(list(loads))
    out = call(
        functools.partial(gather_kernel, orders, cargo),
        "gather_cube", ident, cargo, block,
        jax.ShapeDtypeStruct((MEMBERS, rows, width), block.dtype), pl.ANY,
        [pltpu.SemaphoreType.DMA((len(orders), 8))] * 4 + [pltpu.SemaphoreType.DMA(())],
    )
    return [out[0].reshape(MEMBERS * rows, width)] + list(out[1:])


def scatter_kernel(orders, cargo, p_ref, *refs):
    n = cargo.n
    sources, o_ref, targets = refs[:n], refs[n], refs[n + 1 : 2 * n + 1]
    acc, rcore, came, load_sem, core_send, core_recv, send_sem, recv_sem = refs[
        2 * n + 1 : 2 * n + 9
    ]
    here = place()
    spans = [pl.ds(r0, size) for _, r0, size in orders]
    orders = [o for o, _, _ in orders]
    pieces = range(len(orders))
    cargo.greet(here, NEAR)

    def away(p, mask):
        names = subset(orders[p], mask)
        return pltpu.make_async_remote_copy(
            src_ref=p_ref.at[with_bits(here, names + ("c",)), spans[p]],
            dst_ref=rcore.at[mask, spans[p]],
            send_sem=core_send.at[p, mask], recv_sem=core_recv.at[p, mask],
            device_id=flip(here, "c"), device_id_type=MESH,
        )

    def fetch(p, mask):
        names = subset(orders[p], mask)
        return pltpu.make_async_copy(
            p_ref.at[with_bits(here, names), spans[p]], acc.at[mask, spans[p]], load_sem.at[p, mask]
        )

    sequence = [7, 3, 5, 1, 6, 2, 4, 0]
    sent = []
    for mask in sequence:
        for p in pieces:
            sent.append(away(p, mask))
            sent[-1].start()
            fetch(p, mask).start()
    cargo.start(here, sources, targets, refs[2 * n + 9 :])

    def over(p, mask):
        k = (mask & -mask).bit_length() - 1
        return pltpu.make_async_remote_copy(
            src_ref=acc.at[mask, spans[p]], dst_ref=came.at[mask, spans[p]],
            send_sem=send_sem.at[p, mask], recv_sem=recv_sem.at[p, mask],
            device_id=flip(here, orders[p][k]), device_id_type=MESH,
        )

    def add(p, mask, other):
        acc[mask, spans[p]] = acc[mask, spans[p]] + other[...]

    for mask in sequence:
        for p in pieces:
            fetch(p, mask).wait()
            away(p, mask).wait_recv()
            add(p, mask, rcore.at[mask, spans[p]])
            if mask & 1:
                sent.append(over(p, mask))
                sent[-1].start()
    for k in range(3):
        low = 1 << k
        for mask in [m for m in (6, 2, 4, 0) if m & (2 * low - 1) == 0]:
            for p in pieces:
                over(p, mask | low).wait_recv()
                if mask == 0 and k == 2:
                    o_ref[spans[p]] = acc[0, spans[p]].astype(jnp.float32) + came[
                        4, spans[p]
                    ].astype(jnp.float32)
                    continue
                add(p, mask, came.at[mask | low, spans[p]])
                if mask & (2 * low):
                    sent.append(over(p, mask))
                    sent[-1].start()
    for copy in sent:
        copy.wait_send()
    cargo.wait()


def scatter_cube(partial, ident, loads=(), orders=None):
    total, width = partial.shape
    rows = total // MEMBERS
    orders = orders or thirds(rows)
    cargo = Cargo(list(loads))
    return call(
        functools.partial(scatter_kernel, orders, cargo),
        "scatter_cube", ident, cargo, partial.astype(jnp.bfloat16).reshape(MEMBERS, rows, width),
        jax.ShapeDtypeStruct((rows, width), jnp.float32), pltpu.VMEM,
        [pltpu.VMEM((8, rows, width), jnp.bfloat16)] * 3
        + [pltpu.SemaphoreType.DMA((len(orders), 8))] * 5,
    )


def carry_kernel(cargo, *refs):
    n = cargo.n
    here = place()
    cargo.greet(here, [])
    cargo.start(here, refs[:n], refs[n : 2 * n], refs[2 * n :])
    cargo.wait()


def carry(ident, loads):
    cargo = Cargo(list(loads))
    return pl.pallas_call(
        functools.partial(carry_kernel, cargo),
        out_shape=cargo.outs,
        in_specs=cargo.specs,
        out_specs=cargo.specs,
        scratch_shapes=cargo.scratch,
        compiler_params=pltpu.CompilerParams(collective_id=ident, has_side_effects=True),
        cost_estimate=pl.CostEstimate(flops=0, bytes_accessed=50 * MIB, transcendentals=0),
        name="carry",
    )(*cargo.sources)


def exchange_kernel(v_ref, o_ref, slots, send_sem, recv_sem):
    here = place()
    greet([flip(here, *names) for names in PEERS])
    copies = []
    for m in range(1, MEMBERS):
        copies.append(pltpu.make_async_remote_copy(
            src_ref=v_ref, dst_ref=slots.at[m], send_sem=send_sem.at[m], recv_sem=recv_sem.at[m],
            device_id=flip(here, *PEERS[m - 1]), device_id_type=MESH,
        ))
        copies[-1].start()
    for copy in copies:
        copy.wait_recv()
    slots[0] = v_ref[...]
    terms = [slots[m] for m in range(MEMBERS)]
    while len(terms) > 1:
        terms = [terms[2 * i] + terms[2 * i + 1] for i in range(len(terms) // 2)]
    o_ref[...] = terms[0]
    for copy in copies:
        copy.wait_send()


def sum_cube(values, ident):
    shape = values.shape
    return pl.pallas_call(
        exchange_kernel,
        out_shape=jax.ShapeDtypeStruct(shape, jnp.float32),
        in_specs=[pl.BlockSpec(memory_space=pltpu.VMEM)],
        out_specs=pl.BlockSpec(memory_space=pltpu.VMEM),
        scratch_shapes=[
            pltpu.VMEM((MEMBERS,) + shape, jnp.float32),
            pltpu.SemaphoreType.DMA((MEMBERS,)),
            pltpu.SemaphoreType.DMA((MEMBERS,)),
        ],
        compiler_params=pltpu.CompilerParams(collective_id=ident, has_side_effects=True),
        cost_estimate=pl.CostEstimate(flops=0, bytes_accessed=20 * MIB, transcendentals=0),
        name="sum_cube",
    )(values)


def rope_tables(positions):
    frequency = theta_base ** (-2.0 * jnp.arange(HD // 2).astype(jnp.float32) / HD)
    angles = positions[:, None] * frequency[None, :]
    return (jnp.cos(angles), jnp.sin(angles))


def rotate(values, cos_table, sin_table):
    half_width = values.shape[-1] // 2
    former = values[..., :half_width]
    latter = values[..., half_width:]
    return jnp.concatenate(
        [former * cos_table - latter * sin_table, latter * cos_table + former * sin_table], axis=-1
    )


def normalize(values, scales):
    inverse = lax.rsqrt(jnp.mean(values * values, axis=-1, keepdims=True) + epsilon)
    return (values * inverse * scales, inverse)


def norm_back(upstream, values, inverse, scales):
    unit_rows = values * inverse
    scaled = upstream * scales
    value_grad = inverse * (
        scaled - unit_rows * jnp.mean(scaled * unit_rows, axis=-1, keepdims=True)
    )
    return (value_grad, jnp.sum(upstream * unit_rows, axis=0))


def contract_last(operand, matrix):
    return lax.dot_general(
        operand, matrix, (((1,), (1,)), ((), ())), preferred_element_type=jnp.float32
    )


def contract_first(operand, matrix):
    return lax.dot_general(
        operand, matrix, (((0,), (0,)), ((), ())), preferred_element_type=jnp.float32
    )


def row_sums(pair, ident):
    total = pair[0].shape[0]
    flat = jnp.concatenate([v.reshape(total // 128, 128) for v in pair], axis=0)
    summed = sum_cube(flat, ident).reshape(2, total, 1)
    return summed[0], summed[1]


def owned_sum(terms):
    return jnp.sum(terms.astype(jnp.float32), axis=0).astype(jnp.bfloat16)


def whole_rows(mine, came, parts):
    rows = mine.shape[0]
    first = lax.axis_index("x") == 0
    mine, came = (v.reshape(rows, parts, -1) for v in (mine, came))
    both = [jnp.where(first, mine, came), jnp.where(first, came, mine)]
    return jnp.stack(both, axis=2).reshape(rows, -1).astype(jnp.float32)


def heads_are_owners(rows):
    return lax.axis_size("zh") == 2 and rows == HD


def gathered_head_rows(weight):
    full = lax.all_gather(weight, OWNERS, axis=0, tiled=True)
    head = lax.axis_index(("x", "zl", "y", "c"))
    return lax.dynamic_slice_in_dim(full, head * HD, HD, axis=0)


def summed_head_rows(grad_rows, rows):
    head = lax.axis_index(("x", "zl", "y", "c"))
    full = jnp.zeros((MEMBERS * HD, grad_rows.shape[1]), jnp.float32)
    full = lax.dynamic_update_slice_in_dim(full, grad_rows, head * HD, axis=0)
    full = lax.psum(full, EVERY)
    return lax.dynamic_slice_in_dim(full, lax.axis_index(OWNERS) * rows, rows, axis=0)


def silu_grads(hidden_grad, gate_part, up_part):
    sigmoid_gate = jax.nn.sigmoid(gate_part)
    gate_grad = hidden_grad * up_part * sigmoid_gate * (1.0 + gate_part * (1.0 - sigmoid_gate))
    up_grad = hidden_grad * gate_part * sigmoid_gate
    return gate_grad.astype(jnp.bfloat16), up_grad.astype(jnp.bfloat16)


def shards(tokens, w_qkv, w_out, w_gate_up, w_down_t, gains, starts, cotangent):
    count_rows, width = tokens.shape
    owned = gains.shape[0]
    groups = lax.axis_size("zh")
    total = MEMBERS * count_rows
    score_scale = 1.0 / math.sqrt(HD)
    direct = heads_are_owners(owned)
    local_rows = jnp.arange(count_rows, dtype=jnp.int32)
    seq_begin = lax.cummax(jnp.where(starts == 1, local_rows, 0), axis=0)

    gain_part = jnp.pad(gains.astype(jnp.float32).T, ((0, 4), (0, 0)))
    begin_part = jnp.broadcast_to(seq_begin.astype(jnp.float32)[None, :], (8, count_rows))
    loads = [Load("plane", gain_part), Load("cube", begin_part), Load("columns", w_qkv, 3)]
    if direct:
        loads.append(Load("zh", w_out))
    tokens_all, gain_all, begin_all, qkv_cols, *out_other = gather_cube(
        tokens, 1, loads, halves(count_rows, "zl", "y", "x")
    )
    same = lax.axis_index("x") == lax.axis_index("zh")
    if direct:
        out_rows = jnp.where(same, w_out, out_other[0])
    else:
        out_rows = gathered_head_rows(w_out)
    gain_rows = gain_all[:, :4].transpose(1, 0, 2).reshape(4, width)
    begin_all = begin_all[:, 0]
    head = lax.axis_index(("x", "zl", "y", "c"))
    head_gains = lax.dynamic_slice_in_dim(gain_rows, head * HD, HD, axis=1)
    rows_f32 = local_rows.astype(jnp.float32)
    positions = (rows_f32[None, :] - begin_all).reshape(total)
    cos_table, sin_table = rope_tables(positions)
    allowed = (rows_f32[None, None, :] <= rows_f32[None, :, None]) & (
        rows_f32[None, None, :] >= begin_all[:, :, None]
    )

    def blocks(values):
        return values.reshape(MEMBERS, count_rows, HD)

    projected = jnp.dot(tokens_all, qkv_cols, preferred_element_type=jnp.float32)
    query_raw = projected[:, :HD]
    key_raw = projected[:, HD : 2 * HD]
    value_bf = blocks(projected[:, 2 * HD :].astype(jnp.bfloat16))
    query_sq, key_sq = row_sums(
        (jnp.sum(query_raw * query_raw, axis=1), jnp.sum(key_raw * key_raw, axis=1)), 2
    )
    query_inv = lax.rsqrt(query_sq / width + epsilon)
    key_inv = lax.rsqrt(key_sq / width + epsilon)
    query_unit = query_raw * query_inv
    key_unit = key_raw * key_inv
    query_bf = blocks(rotate(query_unit * head_gains[0], cos_table, sin_table).astype(jnp.bfloat16))
    key_bf = blocks(rotate(key_unit * head_gains[1], cos_table, sin_table).astype(jnp.bfloat16))
    scores = (
        jnp.einsum("bqd,bkd->bqk", query_bf, key_bf, preferred_element_type=jnp.float32)
        * score_scale
    )
    scores = jnp.where(allowed, scores, -1e30)
    exponent = jnp.exp(scores - jnp.max(scores, axis=-1, keepdims=True))
    attention_f32 = exponent / jnp.sum(exponent, axis=-1, keepdims=True)
    attention = attention_f32.astype(jnp.bfloat16)
    attended = (
        jnp.einsum("bqk,bkd->bqd", attention, value_bf, preferred_element_type=jnp.float32)
        .reshape(total, HD)
        .astype(jnp.bfloat16)
    )
    feed_width = w_down_t.shape[1]
    x_most = halves(count_rows, "x", "y", "zl")
    x_last = halves(count_rows, "zl", "y", "x")
    y_last = halves(count_rows, "zl", "x", "y")
    branch, gate_cols = scatter_cube(
        jnp.dot(attended, out_rows, preferred_element_type=jnp.float32),
        3, [Load("columns", w_gate_up[:, :feed_width])], x_most,
    )
    branch_norm, branch_inv = normalize(branch, gain_rows[2])
    middle = tokens.astype(jnp.float32) + branch_norm
    middle_all, up_cols, down_cols = gather_cube(
        middle.astype(jnp.bfloat16), 4,
        [Load("columns", w_gate_up[:, feed_width:]), Load("columns", w_down_t)], x_last,
    )
    gate_part = jnp.dot(middle_all, gate_cols, preferred_element_type=jnp.float32)
    up_part = jnp.dot(middle_all, up_cols, preferred_element_type=jnp.float32)
    hidden_bf = (gate_part * jax.nn.sigmoid(gate_part) * up_part).astype(jnp.bfloat16)
    (feed_out,) = scatter_cube(contract_last(hidden_bf, down_cols), 5)
    feed_norm, feed_inv = normalize(feed_out, gain_rows[3])
    mixed = (middle + feed_norm).astype(jnp.bfloat16)

    upstream = cotangent.astype(jnp.float32)
    feed_grad, gain_feed = norm_back(upstream, feed_out, feed_inv, gain_rows[3])
    (feed_all,) = gather_cube(feed_grad.astype(jnp.bfloat16), 6)
    down_grad = contract_first(feed_all, hidden_bf).astype(jnp.bfloat16)
    hidden_grad = jnp.dot(feed_all, down_cols, preferred_element_type=jnp.float32)
    gate_bf, up_bf = silu_grads(hidden_grad, gate_part, up_part)
    gate_grad = contract_first(middle_all, gate_bf).astype(jnp.bfloat16)
    up_grad = contract_first(middle_all, up_bf).astype(jnp.bfloat16)
    middle_part = contract_last(gate_bf, gate_cols) + contract_last(up_bf, up_cols)
    middle_sum, down_terms, gate_terms = scatter_cube(
        middle_part, 7, [Load("owners", down_grad), Load("owners", gate_grad)], x_most
    )
    middle_grad = upstream + middle_sum
    branch_grad, gain_branch = norm_back(middle_grad, branch, branch_inv, gain_rows[2])
    down_sum = owned_sum(down_terms)
    gate_sum = owned_sum(gate_terms)
    branch_all, up_terms, down_other, gate_other = gather_cube(
        branch_grad.astype(jnp.bfloat16), 8,
        [Load("owners", up_grad), Load("x", down_sum), Load("x", gate_sum)], y_last,
    )
    up_sum = owned_sum(up_terms)
    out_grad = contract_first(attended, branch_all)
    attended_grad = blocks(contract_last(branch_all, out_rows).astype(jnp.bfloat16))
    prob_grad = jnp.einsum(
        "bqd,bkd->bqk", attended_grad, value_bf, preferred_element_type=jnp.float32
    )
    score_bf = (
        attention_f32 * (prob_grad - jnp.sum(attention_f32 * prob_grad, axis=-1, keepdims=True))
    ).astype(jnp.bfloat16)
    value_grad = jnp.einsum(
        "bqk,bqd->bkd", attention, attended_grad, preferred_element_type=jnp.float32
    ).reshape(total, HD)
    query_grad = (
        jnp.einsum("bqk,bkd->bqd", score_bf, key_bf, preferred_element_type=jnp.float32)
        * score_scale
    ).reshape(total, HD)
    key_grad = (
        jnp.einsum("bqk,bqd->bkd", score_bf, query_bf, preferred_element_type=jnp.float32)
        * score_scale
    ).reshape(total, HD)
    query_grad = rotate(query_grad, cos_table, -sin_table)
    key_grad = rotate(key_grad, cos_table, -sin_table)
    query_scaled = query_grad * head_gains[0]
    key_scaled = key_grad * head_gains[1]
    query_dot, key_dot = row_sums(
        (jnp.sum(query_scaled * query_unit, axis=1), jnp.sum(key_scaled * key_unit, axis=1)), 9
    )
    query_raw_grad = query_inv * (query_scaled - query_unit * (query_dot / width))
    key_raw_grad = key_inv * (key_scaled - key_unit * (key_dot / width))
    projected_bf = jnp.concatenate([query_raw_grad, key_raw_grad, value_grad], axis=1).astype(
        jnp.bfloat16
    )
    qkv_grad = contract_first(tokens_all, projected_bf).astype(jnp.bfloat16)

    gain_head = jnp.stack(
        [jnp.sum(query_grad * query_unit, axis=0), jnp.sum(key_grad * key_unit, axis=0)]
    )
    gain_terms = jnp.concatenate(
        [
            lax.dynamic_update_slice_in_dim(
                jnp.zeros((2, width), jnp.float32), gain_head, head * HD, axis=1
            ),
            jnp.stack([gain_branch, gain_feed]),
        ]
    )
    lanes = -(-owned // 128) * 128
    gain_terms = jnp.pad(
        gain_terms.reshape(4, groups * SIDES, owned).transpose(1, 0, 2),
        ((0, 0), (0, 4), (0, lanes - owned)),
    ).reshape(groups * SIDES * 8, lanes)
    loads = [Load("owners", qkv_grad, 3), Load("x", up_sum), Load("owners", gain_terms)]
    if direct:
        out_bf = out_grad.astype(jnp.bfloat16)
        loads.append(Load("zh", out_bf))
    tokens_sum, qkv_terms, up_other, gain_came, *out_came = scatter_cube(
        contract_last(projected_bf, qkv_cols), 10, loads, x_most
    )
    grad_tokens = middle_grad + tokens_sum
    qkv_sum = owned_sum(qkv_terms)
    gain_sum = jnp.sum(gain_came.reshape(groups, 8, SIDES, lanes), axis=(0, 2))
    loads = [Load("x", qkv_sum), Load("x", gain_sum)]
    if direct:
        out_sum = (out_bf.astype(jnp.float32) + out_came[0].astype(jnp.float32)).astype(
            jnp.bfloat16
        )
        loads.append(Load("x", out_sum))
    qkv_other, gain_other, *out_other = carry(11, loads)
    if direct:
        grad_out = jnp.where(same, out_sum, out_other[0]).astype(jnp.float32)
    else:
        grad_out = summed_head_rows(out_grad, owned)
    grad_qkv = whole_rows(qkv_sum, qkv_other, 3)
    grad_gate_up = jnp.concatenate(
        [whole_rows(gate_sum, gate_other, 1), whole_rows(up_sum, up_other, 1)], axis=1
    )
    grad_down_t = whole_rows(down_sum, down_other, 1)
    grad_gains = (gain_sum + gain_other)[:4, :owned].T
    return (mixed, grad_tokens, grad_qkv, grad_out, grad_gate_up, grad_down_t, grad_gains)


def solution(mesh):
    sizes = dict(mesh.shape)
    groups = sizes["fsdp"] // SIDES
    finer = Mesh(mesh.devices.reshape(2, groups, 2, 2, 2), EVERY)
    return jax.shard_map(
        shards,
        mesh=finer,
        in_specs=(
            P(EVERY, None),
            P(OWNERS, None),
            P(OWNERS, None),
            P(OWNERS, None),
            P(OWNERS, None),
            P(OWNERS, None),
            P(EVERY),
            P(EVERY, None),
        ),
        out_specs=(
            P(EVERY, None),
            P(EVERY, None),
            P(OWNERS, None),
            P(OWNERS, None),
            P(OWNERS, None),
            P(OWNERS, None),
            P(OWNERS, None),
        ),
        check_vma=False,
    )
```

```python
import functools
import math

import jax
import jax.numpy as jnp
from jax import lax
from jax.experimental import pallas as pl
from jax.experimental.pallas import tpu as pltpu
from jax.sharding import Mesh, PartitionSpec as P

HD = 128

epsilon = 1e-06
theta_base = 500000.0

OWNERS = ("zh", "zl", "y", "c")
EVERY = ("x", "zh", "zl", "y", "c")
MEMBERS = 16
SIDES = 8
SIDE_BITS = {"zl": 4, "y": 2, "c": 1}
BITS = {"x": 8, "zl": 4, "y": 2, "c": 1}
MESH = pl.DeviceIdType.MESH
MIB = 1 << 20


def thirds(rows):
    unit = rows // 8
    return (
        (("x", "y", "zl"), 0, 3 * unit),
        (("y", "zl", "x"), 3 * unit, 3 * unit),
        (("zl", "x", "y"), 6 * unit, 2 * unit),
    )


def halves(rows, *order):
    return ((order, 0, rows // 2), (order, rows // 2, rows // 2))


PEERS = [tuple(n for n in BITS if m & BITS[n]) for m in range(1, MEMBERS)]
SIDE_PEERS = [tuple(n for n in SIDE_BITS if m & SIDE_BITS[n]) for m in range(SIDES)]


def place():
    return {name: lax.axis_index(name) for name in EVERY}


def flip(here, *names):
    return {name: 1 - here[name] for name in names}


def with_bits(here, names, bits=BITS):
    index = 0
    for name, bit in bits.items():
        index = index + bit * ((1 - here[name]) if name in names else here[name])
    return index


def subset(order, mask):
    return tuple(name for k, name in enumerate(order) if mask >> k & 1)


def greet(devices):
    barrier = pltpu.get_barrier_semaphore()
    for device in devices:
        pl.semaphore_signal(barrier, inc=1, device_id=device, device_id_type=MESH)
    pl.semaphore_wait(barrier, len(devices))


def owner_at(here, groups, step, names):
    device = flip(here, *names)
    if step:
        device["zh"] = lax.rem(here["zh"] + step, groups)
    return device


class Load:
    def __init__(self, kind, source, parts=1, far=0, near=0):
        self.kind = kind
        self.stages = (near, far)
        self.source = source
        self.parts = parts
        groups = self.groups = lax.axis_size("zh")
        shape, kept = source.shape, source.dtype
        if kind == "columns":
            self.rows = shape[0]
            self.piece = shape[1] // (parts * MEMBERS)
            shape = (groups * SIDES * shape[0], parts * self.piece)
        elif kind == "owners":
            self.rows = shape[0] // (groups * SIDES)
            self.piece = shape[1] // parts
            shape = (groups, self.rows, parts * SIDES * self.piece)
        elif kind == "plane":
            shape = (groups * SIDES,) + shape
        elif kind == "cube":
            shape = (MEMBERS,) + shape
        self.out = jax.ShapeDtypeStruct(shape, kept)
        self.space = pltpu.VMEM if kind in ("plane", "cube") else pl.ANY
        self.count = len(self.moves(None))

    def moves(self, here):
        if self.kind == "zh":
            return [((1, ()), 0)]
        if self.kind == "x":
            return [((0, ("x",)), 0)]
        if self.kind == "cube":
            return [((0, names), 0) for names in [()] + PEERS]
        return [
            ((step, names), part)
            for step in range(self.groups)
            for names in SIDE_PEERS
            for part in range(self.parts)
        ]

    def scratch(self):
        return [pltpu.SemaphoreType.DMA((self.count,)), pltpu.SemaphoreType.DMA((self.count,))]

    def devices(self, here):
        return [
            (step, names) for (step, names), part in self.moves(here) if part == 0 and (step or names)
        ]

    def views(self, here, src, dst, step, names, part):
        if self.kind in ("zh", "x"):
            return src, dst, dst
        if self.kind == "cube":
            return src, dst.at[with_bits(here, ())], dst.at[with_bits(here, names)]
        groups, side = self.groups, with_bits(here, (), SIDE_BITS)
        other = with_bits(here, names, SIDE_BITS)
        there = lax.rem(here["zh"] + step, groups)
        whence = lax.rem(here["zh"] + groups - step, groups)
        me, he = here["zh"] * SIDES + side, whence * SIDES + other
        if self.kind == "plane":
            return src, dst.at[me], dst.at[he]
        rows, piece = self.rows, self.piece

        def at(start, size):
            return pl.ds(pl.multiple_of(start, size), size)

        if self.kind == "columns":
            first = part * MEMBERS + here["x"] * SIDES + other
            columns = pl.ds(part * piece, piece)
            return (
                src.at[:, at(first * piece, piece)],
                dst.at[at(me * rows, rows), columns],
                dst.at[at(he * rows, rows), columns],
            )
        target = there * SIDES + other
        return (
            src.at[at(target * rows, rows), pl.ds(part * piece, piece)],
            dst.at[here["zh"], :, at((part * SIDES + side) * piece, piece)],
            dst.at[whence, :, at((part * SIDES + other) * piece, piece)],
        )

    def copies(self, here, src, dst, send, recv):
        result = []
        for index, ((step, names), part) in enumerate(self.moves(here)):
            source, target, landing = self.views(here, src, dst, step, names, part)
            stage = self.stages[1 if step else 0]
            if not step and not names:
                copy = pltpu.make_async_copy(source, target, send.at[index])
                result.append((stage, copy, None))
                continue
            copy = pltpu.make_async_remote_copy(
                src_ref=source, dst_ref=target, send_sem=send.at[index], recv_sem=recv.at[index],
                device_id=owner_at(here, self.groups, step, names), device_id_type=MESH,
            )
            landed = pltpu.make_async_copy(landing, landing, recv.at[index])
            result.append((stage, copy, landed))
        return result


class Cargo:
    def __init__(self, loads):
        self.loads = loads
        self.n = len(loads)
        self.sources = [load.source for load in loads]
        self.specs = [pl.BlockSpec(memory_space=load.space) for load in loads]
        self.outs = [load.out for load in loads]
        self.scratch = [s for load in loads for s in load.scratch()]

    def greet(self, here, names):
        reached = {(0, n) for n in names}
        for load in self.loads:
            reached |= set(load.devices(here))
        groups = lax.axis_size("zh")
        greet([owner_at(here, groups, step, n) for step, n in sorted(reached)])

    def prepare(self, here, sources, targets, semaphores):
        self.copies = []
        for k, load in enumerate(self.loads):
            self.copies += load.copies(
                here, sources[k], targets[k], semaphores[2 * k], semaphores[2 * k + 1]
            )

    def start(self, stage):
        for when, copy, _ in self.copies:
            if when == stage:
                copy.start()

    def wait(self):
        for _, copy, landing in self.copies:
            if landing is None:
                copy.wait()
            else:
                landing.wait()
        for _, copy, landing in self.copies:
            if landing is not None:
                copy.wait_send()


GATHER_STAGES = (0, 1, 2, 3)
NEAR = [("x",), ("zl",), ("y",), ("c",)]


def call(body, name, ident, cargo, operand, space, out, out_space, scratch, vmem=40):
    return pl.pallas_call(
        body,
        out_shape=[out] + cargo.outs,
        in_specs=[pl.BlockSpec(memory_space=space)] + cargo.specs,
        out_specs=[pl.BlockSpec(memory_space=out_space)] + cargo.specs,
        scratch_shapes=scratch + cargo.scratch,
        compiler_params=pltpu.CompilerParams(
            collective_id=ident, has_side_effects=True, vmem_limit_bytes=vmem * MIB
        ),
        cost_estimate=pl.CostEstimate(flops=0, bytes_accessed=100 * MIB, transcendentals=0),
        name=name,
    )(operand, *cargo.sources)


def gather_kernel(orders, cargo, x_ref, *refs):
    n = cargo.n
    sources, o_ref, targets = refs[:n], refs[n], refs[n + 1 : 2 * n + 1]
    send_sem, recv_sem, core_send, core_recv, own_sem = refs[2 * n + 1 : 2 * n + 6]
    here = place()
    spans = [pl.ds(r0, size) for _, r0, size in orders]
    orders = [o for o, _, _ in orders]
    pieces = range(len(orders))
    cargo.prepare(here, sources, targets, refs[2 * n + 6 :])
    cargo.greet(here, NEAR)
    own = pltpu.make_async_copy(x_ref, o_ref.at[with_bits(here, ())], own_sem)

    def piece_of(p, mask):
        spot = o_ref.at[with_bits(here, subset(orders[p], mask)), spans[p]]
        return (x_ref.at[spans[p]] if mask == 0 else spot), spot

    def over(p, mask, k):
        source, spot = piece_of(p, mask)
        return pltpu.make_async_remote_copy(
            src_ref=source, dst_ref=spot,
            send_sem=send_sem.at[p, mask | 1 << k], recv_sem=recv_sem.at[p, mask | 1 << k],
            device_id=flip(here, orders[p][k]), device_id_type=MESH,
        )

    def across(p, mask):
        source, spot = piece_of(p, mask)
        return pltpu.make_async_remote_copy(
            src_ref=source, dst_ref=spot,
            send_sem=core_send.at[p, mask], recv_sem=core_recv.at[p, mask],
            device_id=flip(here, "c"), device_id_type=MESH,
        )

    sent = []
    for mask in range(8):
        for p in pieces:
            if mask:
                _, spot = piece_of(p, mask)
                pltpu.make_async_copy(spot, spot, recv_sem.at[p, mask]).wait()
            for k in range(mask.bit_length(), 3):
                sent.append(over(p, mask, k))
                sent[-1].start()
        for p in pieces:
            sent.append(across(p, mask))
            sent[-1].start()
        if mask == 0:
            own.start()
        if mask in GATHER_STAGES:
            cargo.start(GATHER_STAGES.index(mask))
    for mask in range(8):
        for p in pieces:
            spot = o_ref.at[with_bits(here, subset(orders[p], mask) + ("c",)), spans[p]]
            pltpu.make_async_copy(spot, spot, core_recv.at[p, mask]).wait()
    for copy in sent:
        copy.wait_send()
    own.wait()
    cargo.wait()


def gather_cube(block, ident, loads=(), orders=None):
    rows, width = block.shape
    orders = orders or thirds(rows)
    cargo = Cargo(list(loads))
    out = call(
        functools.partial(gather_kernel, orders, cargo),
        "gather_cube", ident, cargo, block, pl.ANY,
        jax.ShapeDtypeStruct((MEMBERS, rows, width), block.dtype), pl.ANY,
        [pltpu.SemaphoreType.DMA((len(orders), 8))] * 4 + [pltpu.SemaphoreType.DMA(())],
    )
    return [out[0].reshape(MEMBERS * rows, width)] + list(out[1:])


def scatter_kernel(orders, cargo, p_ref, *refs):
    n = cargo.n
    sources, o_ref, targets = refs[:n], refs[n], refs[n + 1 : 2 * n + 1]
    acc, rcore, came, core_send, core_recv, send_sem, recv_sem = refs[2 * n + 1 : 2 * n + 8]
    here = place()
    spans = [pl.ds(r0, size) for _, r0, size in orders]
    orders = [o for o, _, _ in orders]
    pieces = range(len(orders))
    cargo.prepare(here, sources, targets, refs[2 * n + 8 :])
    cargo.greet(here, NEAR)

    def away(p, mask):
        names = subset(orders[p], mask)
        return pltpu.make_async_remote_copy(
            src_ref=p_ref.at[with_bits(here, names + ("c",)), spans[p]],
            dst_ref=rcore.at[mask, spans[p]],
            send_sem=core_send.at[p, mask], recv_sem=core_recv.at[p, mask],
            device_id=flip(here, "c"), device_id_type=MESH,
        )

    sequence = [7, 3, 5, 1, 6, 2, 4, 0]
    sent = []
    for mask in sequence:
        for p in pieces:
            sent.append(away(p, mask))
            sent[-1].start()
    cargo.start(0)

    def over(p, mask):
        k = (mask & -mask).bit_length() - 1
        return pltpu.make_async_remote_copy(
            src_ref=acc.at[mask, spans[p]], dst_ref=came.at[mask, spans[p]],
            send_sem=send_sem.at[p, mask], recv_sem=recv_sem.at[p, mask],
            device_id=flip(here, orders[p][k]), device_id_type=MESH,
        )

    def add(p, mask, other):
        acc[mask, spans[p]] = acc[mask, spans[p]] + other[...]

    def first_sum(p, mask):
        own = with_bits(here, subset(orders[p], mask))
        acc[mask, spans[p]] = p_ref[own, spans[p]] + rcore[mask, spans[p]]

    for mask in sequence:
        for p in pieces:
            away(p, mask).wait_recv()
            first_sum(p, mask)
            if mask & 1:
                sent.append(over(p, mask))
                sent[-1].start()
    cargo.start(1)
    for k in range(3):
        low = 1 << k
        for mask in [m for m in (6, 2, 4, 0) if m & (2 * low - 1) == 0]:
            for p in pieces:
                over(p, mask | low).wait_recv()
                if mask == 0 and k == 2:
                    o_ref[spans[p]] = acc[0, spans[p]].astype(jnp.float32) + came[
                        4, spans[p]
                    ].astype(jnp.float32)
                    continue
                add(p, mask, came.at[mask | low, spans[p]])
                if mask & (2 * low):
                    sent.append(over(p, mask))
                    sent[-1].start()
        if k < 2:
            cargo.start(2 + k)
    for copy in sent:
        copy.wait_send()
    cargo.wait()


def scatter_cube(partial, ident, loads=(), orders=None):
    total, width = partial.shape
    rows = total // MEMBERS
    orders = orders or thirds(rows)
    cargo = Cargo(list(loads))
    return call(
        functools.partial(scatter_kernel, orders, cargo),
        "scatter_cube", ident, cargo, partial.astype(jnp.bfloat16).reshape(MEMBERS, rows, width),
        pltpu.VMEM,
        jax.ShapeDtypeStruct((rows, width), jnp.float32), pltpu.VMEM,
        [pltpu.VMEM((8, rows, width), jnp.bfloat16)] * 3
        + [pltpu.SemaphoreType.DMA((len(orders), 8))] * 4,
    )


def carry_kernel(cargo, *refs):
    n = cargo.n
    here = place()
    cargo.prepare(here, refs[:n], refs[n : 2 * n], refs[2 * n :])
    cargo.greet(here, [])
    cargo.start(0)
    cargo.wait()


def carry(ident, loads):
    cargo = Cargo(list(loads))
    return pl.pallas_call(
        functools.partial(carry_kernel, cargo),
        out_shape=cargo.outs,
        in_specs=cargo.specs,
        out_specs=cargo.specs,
        scratch_shapes=cargo.scratch,
        compiler_params=pltpu.CompilerParams(collective_id=ident, has_side_effects=True),
        cost_estimate=pl.CostEstimate(flops=0, bytes_accessed=50 * MIB, transcendentals=0),
        name="carry",
    )(*cargo.sources)


def exchange_kernel(v_ref, o_ref, slots, send_sem, recv_sem):
    here = place()
    greet([flip(here, *names) for names in PEERS])
    copies = []
    for m in range(1, MEMBERS):
        copies.append(pltpu.make_async_remote_copy(
            src_ref=v_ref, dst_ref=slots.at[m], send_sem=send_sem.at[m], recv_sem=recv_sem.at[m],
            device_id=flip(here, *PEERS[m - 1]), device_id_type=MESH,
        ))
        copies[-1].start()
    for copy in copies:
        copy.wait_recv()
    slots[0] = v_ref[...]
    terms = [slots[m] for m in range(MEMBERS)]
    while len(terms) > 1:
        terms = [terms[2 * i] + terms[2 * i + 1] for i in range(len(terms) // 2)]
    o_ref[...] = terms[0]
    for copy in copies:
        copy.wait_send()


def sum_cube(values, ident):
    shape = values.shape
    return pl.pallas_call(
        exchange_kernel,
        out_shape=jax.ShapeDtypeStruct(shape, jnp.float32),
        in_specs=[pl.BlockSpec(memory_space=pltpu.VMEM)],
        out_specs=pl.BlockSpec(memory_space=pltpu.VMEM),
        scratch_shapes=[
            pltpu.VMEM((MEMBERS,) + shape, jnp.float32),
            pltpu.SemaphoreType.DMA((MEMBERS,)),
            pltpu.SemaphoreType.DMA((MEMBERS,)),
        ],
        compiler_params=pltpu.CompilerParams(collective_id=ident, has_side_effects=True),
        cost_estimate=pl.CostEstimate(flops=0, bytes_accessed=20 * MIB, transcendentals=0),
        name="sum_cube",
    )(values)


def rope_tables(positions):
    frequency = theta_base ** (-2.0 * jnp.arange(HD // 2).astype(jnp.float32) / HD)
    angles = positions[:, None] * frequency[None, :]
    return (jnp.cos(angles), jnp.sin(angles))


def rotate(values, cos_table, sin_table):
    half_width = values.shape[-1] // 2
    former = values[..., :half_width]
    latter = values[..., half_width:]
    return jnp.concatenate(
        [former * cos_table - latter * sin_table, latter * cos_table + former * sin_table], axis=-1
    )


def normalize(values, scales):
    inverse = lax.rsqrt(jnp.mean(values * values, axis=-1, keepdims=True) + epsilon)
    return (values * inverse * scales, inverse)


def norm_back(upstream, values, inverse, scales):
    unit_rows = values * inverse
    scaled = upstream * scales
    value_grad = inverse * (
        scaled - unit_rows * jnp.mean(scaled * unit_rows, axis=-1, keepdims=True)
    )
    return (value_grad, jnp.sum(upstream * unit_rows, axis=0))


def contract_last(operand, matrix):
    return lax.dot_general(
        operand, matrix, (((1,), (1,)), ((), ())), preferred_element_type=jnp.float32
    )


def contract_first(operand, matrix):
    return lax.dot_general(
        operand, matrix, (((0,), (0,)), ((), ())), preferred_element_type=jnp.float32
    )


def row_sums(pair, ident):
    total = pair[0].shape[0]
    flat = jnp.concatenate([v.reshape(total // 128, 128) for v in pair], axis=0)
    summed = sum_cube(flat, ident).reshape(2, total, 1)
    return summed[0], summed[1]


def owned_sum(terms):
    return jnp.sum(terms.astype(jnp.float32), axis=0).astype(jnp.bfloat16)


def finish_kernel(mine_ref, came_ref, o_ref):
    own = pl.program_id(1) == lax.axis_index("x")
    o_ref[...] = jnp.where(own, mine_ref[...], came_ref[...]).astype(jnp.float32)


def whole_rows(mine, came, parts):
    rows, width = mine.shape
    step = min(2048, width // parts)
    steps = width // parts // step
    half = pl.BlockSpec((rows, step), lambda p, x, k: (0, p * steps + k))
    return pl.pallas_call(
        finish_kernel,
        grid=(parts, 2, steps),
        out_shape=jax.ShapeDtypeStruct((rows, 2 * width), jnp.float32),
        in_specs=[half, half],
        out_specs=pl.BlockSpec((rows, step), lambda p, x, k: (0, (2 * p + x) * steps + k)),
        compiler_params=pltpu.CompilerParams(vmem_limit_bytes=32 * MIB),
        cost_estimate=pl.CostEstimate(
            flops=0, bytes_accessed=16 * rows * width, transcendentals=0
        ),
        name="whole_rows",
    )(mine, came)


def heads_are_owners(rows):
    return lax.axis_size("zh") == 2 and rows == HD


def gathered_head_rows(weight):
    full = lax.all_gather(weight, OWNERS, axis=0, tiled=True)
    head = lax.axis_index(("x", "zl", "y", "c"))
    return lax.dynamic_slice_in_dim(full, head * HD, HD, axis=0)


def summed_head_rows(grad_rows, rows):
    head = lax.axis_index(("x", "zl", "y", "c"))
    full = jnp.zeros((MEMBERS * HD, grad_rows.shape[1]), jnp.float32)
    full = lax.dynamic_update_slice_in_dim(full, grad_rows, head * HD, axis=0)
    full = lax.psum(full, EVERY)
    return lax.dynamic_slice_in_dim(full, lax.axis_index(OWNERS) * rows, rows, axis=0)


def silu_grads(hidden_grad, gate_part, up_part):
    sigmoid_gate = jax.nn.sigmoid(gate_part)
    gate_grad = hidden_grad * up_part * sigmoid_gate * (1.0 + gate_part * (1.0 - sigmoid_gate))
    up_grad = hidden_grad * gate_part * sigmoid_gate
    return gate_grad.astype(jnp.bfloat16), up_grad.astype(jnp.bfloat16)


def shards(tokens, w_qkv, w_out, w_gate_up, w_down_t, gains, starts, cotangent):
    count_rows, width = tokens.shape
    owned = gains.shape[0]
    groups = lax.axis_size("zh")
    total = MEMBERS * count_rows
    score_scale = 1.0 / math.sqrt(HD)
    direct = heads_are_owners(owned)
    local_rows = jnp.arange(count_rows, dtype=jnp.int32)
    seq_begin = lax.cummax(jnp.where(starts == 1, local_rows, 0), axis=0)

    gain_part = jnp.pad(gains.astype(jnp.float32).T, ((0, 4), (0, 0)))
    begin_part = jnp.broadcast_to(seq_begin.astype(jnp.float32)[None, :], (8, count_rows))
    loads = [Load("plane", gain_part), Load("cube", begin_part), Load("columns", w_qkv, 3)]
    if direct:
        loads.append(Load("zh", w_out))
    tokens_all, gain_all, begin_all, qkv_cols, *out_other = gather_cube(
        tokens, 1, loads, halves(count_rows, "zl", "y", "x")
    )
    same = lax.axis_index("x") == lax.axis_index("zh")
    if direct:
        out_rows = jnp.where(same, w_out, out_other[0])
    else:
        out_rows = gathered_head_rows(w_out)
    gain_rows = gain_all[:, :4].transpose(1, 0, 2).reshape(4, width)
    begin_all = begin_all[:, 0]
    head = lax.axis_index(("x", "zl", "y", "c"))
    head_gains = lax.dynamic_slice_in_dim(gain_rows, head * HD, HD, axis=1)
    rows_f32 = local_rows.astype(jnp.float32)
    positions = (rows_f32[None, :] - begin_all).reshape(total)
    cos_table, sin_table = rope_tables(positions)
    allowed = (rows_f32[None, None, :] <= rows_f32[None, :, None]) & (
        rows_f32[None, None, :] >= begin_all[:, :, None]
    )

    def blocks(values):
        return values.reshape(MEMBERS, count_rows, HD)

    projected = jnp.dot(tokens_all, qkv_cols, preferred_element_type=jnp.float32)
    query_raw = projected[:, :HD]
    key_raw = projected[:, HD : 2 * HD]
    value_bf = blocks(projected[:, 2 * HD :].astype(jnp.bfloat16))
    query_sq, key_sq = row_sums(
        (jnp.sum(query_raw * query_raw, axis=1), jnp.sum(key_raw * key_raw, axis=1)), 2
    )
    query_inv = lax.rsqrt(query_sq / width + epsilon)
    key_inv = lax.rsqrt(key_sq / width + epsilon)
    query_unit = query_raw * query_inv
    key_unit = key_raw * key_inv
    query_bf = blocks(rotate(query_unit * head_gains[0], cos_table, sin_table).astype(jnp.bfloat16))
    key_bf = blocks(rotate(key_unit * head_gains[1], cos_table, sin_table).astype(jnp.bfloat16))
    scores = (
        jnp.einsum("bqd,bkd->bqk", query_bf, key_bf, preferred_element_type=jnp.float32)
        * score_scale
    )
    scores = jnp.where(allowed, scores, -1e30)
    exponent = jnp.exp(scores - jnp.max(scores, axis=-1, keepdims=True))
    attention_f32 = exponent / jnp.sum(exponent, axis=-1, keepdims=True)
    attention = attention_f32.astype(jnp.bfloat16)
    attended = (
        jnp.einsum("bqk,bkd->bqd", attention, value_bf, preferred_element_type=jnp.float32)
        .reshape(total, HD)
        .astype(jnp.bfloat16)
    )
    x_most = halves(count_rows, "x", "y", "zl")
    x_last = halves(count_rows, "zl", "y", "x")
    x_or_y = (
        (("x", "y", "zl"), 0, count_rows // 2),
        (("y", "x", "zl"), count_rows // 2, count_rows // 2),
    )
    y_last = halves(count_rows, "zl", "x", "y")
    branch, down_cols = scatter_cube(
        jnp.dot(attended, out_rows, preferred_element_type=jnp.float32),
        3, [Load("columns", w_down_t, near=1)], x_most,
    )
    branch_norm, branch_inv = normalize(branch, gain_rows[2])
    middle = tokens.astype(jnp.float32) + branch_norm
    middle_all, gate_up_cols = gather_cube(
        middle.astype(jnp.bfloat16), 4, [Load("columns", w_gate_up, 2, near=3)], x_last
    )
    gate_up = jnp.dot(middle_all, gate_up_cols, preferred_element_type=jnp.float32)
    gate_part, up_part = jnp.split(gate_up, 2, axis=1)
    hidden_bf = (gate_part * jax.nn.sigmoid(gate_part) * up_part).astype(jnp.bfloat16)
    (feed_out,) = scatter_cube(contract_last(hidden_bf, down_cols), 5)
    feed_norm, feed_inv = normalize(feed_out, gain_rows[3])
    mixed = (middle + feed_norm).astype(jnp.bfloat16)

    upstream = cotangent.astype(jnp.float32)
    feed_grad, gain_feed = norm_back(upstream, feed_out, feed_inv, gain_rows[3])
    (feed_all,) = gather_cube(feed_grad.astype(jnp.bfloat16), 6)
    down_grad = contract_first(feed_all, hidden_bf).astype(jnp.bfloat16)
    hidden_grad = jnp.dot(feed_all, down_cols, preferred_element_type=jnp.float32)
    gate_up_bf = jnp.concatenate(silu_grads(hidden_grad, gate_part, up_part), axis=1)
    gate_up_grad = contract_first(middle_all, gate_up_bf).astype(jnp.bfloat16)
    middle_part = contract_last(gate_up_bf, gate_up_cols)
    middle_sum, gate_up_terms = scatter_cube(
        middle_part, 7, [Load("owners", gate_up_grad, 2)], x_most
    )
    middle_grad = upstream + middle_sum
    branch_grad, gain_branch = norm_back(middle_grad, branch, branch_inv, gain_rows[2])
    gate_up_sum = owned_sum(gate_up_terms)
    branch_all, down_terms, gate_up_other = gather_cube(
        branch_grad.astype(jnp.bfloat16), 8,
        [Load("owners", down_grad, far=1, near=3), Load("x", gate_up_sum, near=1)], y_last,
    )
    down_sum = owned_sum(down_terms)
    out_grad = contract_first(attended, branch_all)
    attended_grad = blocks(contract_last(branch_all, out_rows).astype(jnp.bfloat16))
    prob_grad = jnp.einsum(
        "bqd,bkd->bqk", attended_grad, value_bf, preferred_element_type=jnp.float32
    )
    score_bf = (
        attention_f32 * (prob_grad - jnp.sum(attention_f32 * prob_grad, axis=-1, keepdims=True))
    ).astype(jnp.bfloat16)
    value_grad = jnp.einsum(
        "bqk,bqd->bkd", attention, attended_grad, preferred_element_type=jnp.float32
    ).reshape(total, HD)
    query_grad = (
        jnp.einsum("bqk,bkd->bqd", score_bf, key_bf, preferred_element_type=jnp.float32)
        * score_scale
    ).reshape(total, HD)
    key_grad = (
        jnp.einsum("bqk,bqd->bkd", score_bf, query_bf, preferred_element_type=jnp.float32)
        * score_scale
    ).reshape(total, HD)
    query_grad = rotate(query_grad, cos_table, -sin_table)
    key_grad = rotate(key_grad, cos_table, -sin_table)
    query_scaled = query_grad * head_gains[0]
    key_scaled = key_grad * head_gains[1]
    query_dot, key_dot = row_sums(
        (jnp.sum(query_scaled * query_unit, axis=1), jnp.sum(key_scaled * key_unit, axis=1)), 9
    )
    query_raw_grad = query_inv * (query_scaled - query_unit * (query_dot / width))
    key_raw_grad = key_inv * (key_scaled - key_unit * (key_dot / width))
    projected_bf = jnp.concatenate([query_raw_grad, key_raw_grad, value_grad], axis=1).astype(
        jnp.bfloat16
    )
    qkv_grad = contract_first(tokens_all, projected_bf).astype(jnp.bfloat16)

    gain_head = jnp.stack(
        [jnp.sum(query_grad * query_unit, axis=0), jnp.sum(key_grad * key_unit, axis=0)]
    )
    gain_terms = jnp.concatenate(
        [
            lax.dynamic_update_slice_in_dim(
                jnp.zeros((2, width), jnp.float32), gain_head, head * HD, axis=1
            ),
            jnp.stack([gain_branch, gain_feed]),
        ]
    )
    lanes = -(-owned // 128) * 128
    gain_terms = jnp.pad(
        gain_terms.reshape(4, groups * SIDES, owned).transpose(1, 0, 2),
        ((0, 0), (0, 4), (0, lanes - owned)),
    ).reshape(groups * SIDES * 8, lanes)
    loads = [Load("owners", qkv_grad, 3), Load("x", down_sum, near=2), Load("owners", gain_terms)]
    if direct:
        out_bf = out_grad.astype(jnp.bfloat16)
        loads.append(Load("zh", out_bf))
    tokens_sum, qkv_terms, down_other, gain_came, *out_came = scatter_cube(
        contract_last(projected_bf, qkv_cols), 10, loads, x_or_y
    )
    grad_tokens = middle_grad + tokens_sum
    qkv_sum = owned_sum(qkv_terms)
    gain_sum = jnp.sum(gain_came.reshape(groups, 8, SIDES, lanes), axis=(0, 2))
    loads = [Load("x", qkv_sum), Load("x", gain_sum)]
    if direct:
        out_sum = (out_bf.astype(jnp.float32) + out_came[0].astype(jnp.float32)).astype(
            jnp.bfloat16
        )
        loads.append(Load("x", out_sum))
    qkv_other, gain_other, *out_other = carry(11, loads)
    if direct:
        grad_out = jnp.where(same, out_sum, out_other[0]).astype(jnp.float32)
    else:
        grad_out = summed_head_rows(out_grad, owned)
    grad_qkv = whole_rows(qkv_sum, qkv_other, 3)
    grad_gate_up = whole_rows(gate_up_sum, gate_up_other, 2)
    grad_down_t = whole_rows(down_sum, down_other, 1)
    grad_gains = (gain_sum + gain_other)[:4, :owned].T
    return (mixed, grad_tokens, grad_qkv, grad_out, grad_gate_up, grad_down_t, grad_gains)


def solution(mesh):
    sizes = dict(mesh.shape)
    groups = sizes["fsdp"] // SIDES
    finer = Mesh(mesh.devices.reshape(2, groups, 2, 2, 2), EVERY)
    return jax.shard_map(
        shards,
        mesh=finer,
        in_specs=(
            P(EVERY, None),
            P(OWNERS, None),
            P(OWNERS, None),
            P(OWNERS, None),
            P(OWNERS, None),
            P(OWNERS, None),
            P(EVERY),
            P(EVERY, None),
        ),
        out_specs=(
            P(EVERY, None),
            P(EVERY, None),
            P(OWNERS, None),
            P(OWNERS, None),
            P(OWNERS, None),
            P(OWNERS, None),
            P(OWNERS, None),
        ),
        check_vma=False,
    )
```

```python
import functools
import math

import jax
import jax.numpy as jnp
from jax import lax
from jax.experimental import pallas as pl
from jax.experimental.pallas import tpu as pltpu
from jax.sharding import Mesh, PartitionSpec as P

HD = 128

epsilon = 1e-06
theta_base = 500000.0

OWNERS = ("zh", "zl", "y", "c")
EVERY = ("x", "zh", "zl", "y", "c")
MEMBERS = 16
SIDES = 8
SIDE_BITS = {"zl": 4, "y": 2, "c": 1}
BITS = {"x": 8, "zl": 4, "y": 2, "c": 1}
SLOTS = [
    frozenset(names + core)
    for names in (
        (), ("x",), ("y",), ("zl",), ("x", "y"), ("x", "zl"), ("y", "zl"), ("x", "y", "zl"),
    )
    for core in ((), ("c",))
]
SLOT = {names: k for k, names in enumerate(SLOTS)}
MESH = pl.DeviceIdType.MESH
MIB = 1 << 20


def thirds(rows):
    unit = rows // 8
    return (
        (("x", "y", "zl"), 0, 3 * unit),
        (("y", "zl", "x"), 3 * unit, 3 * unit),
        (("zl", "x", "y"), 6 * unit, 2 * unit),
    )


def halves(rows, *order):
    return ((order, 0, rows // 2), (order, rows // 2, rows // 2))


PEERS = [tuple(n for n in BITS if m & BITS[n]) for m in range(1, MEMBERS)]
SIDE_PEERS = [tuple(n for n in SIDE_BITS if m & SIDE_BITS[n]) for m in range(SIDES)]


def slot(*names):
    return SLOT[frozenset(names)]


def place():
    return {name: lax.axis_index(name) for name in EVERY}


def flip(here, *names):
    return {name: 1 - here[name] for name in names}


def with_bits(here, names, bits):
    index = 0
    for name, bit in bits.items():
        index = index + bit * ((1 - here[name]) if name in names else here[name])
    return index


def subset(order, mask):
    return tuple(name for k, name in enumerate(order) if mask >> k & 1)


def greet(devices):
    barrier = pltpu.get_barrier_semaphore()
    for device in devices:
        pl.semaphore_signal(barrier, inc=1, device_id=device, device_id_type=MESH)
    pl.semaphore_wait(barrier, len(devices))


def owner_at(here, groups, step, names):
    device = flip(here, *names)
    if step:
        device["zh"] = lax.rem(here["zh"] + step, groups)
    return device


def at(start, size):
    return pl.ds(pl.multiple_of(start, size), size)


class Load:
    space = pl.ANY
    parts = 1

    def __init__(self, source, far=0, near=0, early=False):
        self.sources = [source]
        self.stages = (near, far)
        self.early = early
        self.groups = lax.axis_size("zh")

    def spaces(self):
        return [self.space] * len(self.sources), [self.space] * len(self.outs)

    def semaphores(self):
        count = len(self.moves())
        return [pltpu.SemaphoreType.DMA((count,)), pltpu.SemaphoreType.DMA((count,))]

    def scratch(self):
        return self.semaphores()

    def moves(self):
        return [
            ((step, names), part)
            for step in range(self.groups)
            for names in SIDE_PEERS
            for part in range(self.parts)
        ]

    def reached(self):
        return {peer for peer, _ in self.moves() if peer != (0, ())}

    def around(self, here, step, names):
        there = lax.rem(here["zh"] + step, self.groups)
        whence = lax.rem(here["zh"] + self.groups - step, self.groups)
        mine, other = with_bits(here, (), SIDE_BITS), with_bits(here, names, SIDE_BITS)
        return mine, other, there, whence

    def bind(self, here, sources, targets, scratch):
        self.here, self.src, self.dst = here, sources, targets
        self.send, self.recv, *self.more = scratch
        self.copies = []
        for index, ((step, names), part) in enumerate(self.moves()):
            source, target, landing = self.views(here, step, names, part)
            stage = self.stages[1 if step else 0]
            if not step and not names:
                copy = pltpu.make_async_copy(source, target, self.send.at[index])
                self.copies.append((stage, copy, None, (step, names)))
                continue
            copy = pltpu.make_async_remote_copy(
                src_ref=source, dst_ref=target,
                send_sem=self.send.at[index], recv_sem=self.recv.at[index],
                device_id=owner_at(here, self.groups, step, names), device_id_type=MESH,
            )
            landed = pltpu.make_async_copy(landing, landing, self.recv.at[index])
            self.copies.append((stage, copy, landed, (step, names)))

    def start(self, stage):
        for when, copy, _, _ in self.copies:
            if when == stage:
                copy.start()

    def land(self):
        for _, copy, landed, _ in self.copies:
            (copy if landed is None else landed).wait()

    def finish(self):
        pass

    def leave(self):
        for _, copy, landed, _ in self.copies:
            if landed is not None:
                copy.wait_send()


class Columns(Load):
    def __init__(self, source, parts=1, **stages):
        super().__init__(source, **stages)
        self.parts = parts
        self.rows = source.shape[0]
        self.piece = source.shape[1] // (parts * MEMBERS)
        shape = (self.groups * SIDES * self.rows, parts * self.piece)
        self.outs = [jax.ShapeDtypeStruct(shape, source.dtype)]

    def views(self, here, step, names, part):
        mine, other, _, whence = self.around(here, step, names)
        first = part * MEMBERS + here["x"] * SIDES + other
        columns = pl.ds(part * self.piece, self.piece)
        return (
            self.src[0].at[:, at(first * self.piece, self.piece)],
            self.dst[0].at[at((here["zh"] * SIDES + mine) * self.rows, self.rows), columns],
            self.dst[0].at[at((whence * SIDES + other) * self.rows, self.rows), columns],
        )


class Few(Load):
    space = pltpu.VMEM

    def __init__(self, source, cube):
        super().__init__(source)
        self.cube = cube
        count = MEMBERS if cube else self.groups * SIDES
        self.outs = [jax.ShapeDtypeStruct((count,) + source.shape, source.dtype)]

    def moves(self):
        if self.cube:
            return [((0, names), 0) for names in [()] + PEERS]
        return super().moves()

    def views(self, here, step, names, part):
        if self.cube:
            spot = self.dst[0].at[slot(*names)]
            return self.src[0], spot, spot
        mine, other, _, whence = self.around(here, step, names)
        return (
            self.src[0],
            self.dst[0].at[here["zh"] * SIDES + mine],
            self.dst[0].at[whence * SIDES + other],
        )


class Whole(Load):
    def __init__(self, source, axis, **stages):
        super().__init__(source, **stages)
        self.axis = axis
        self.outs = [jax.ShapeDtypeStruct(source.shape, source.dtype)]

    def moves(self):
        return [((0, ("x",)) if self.axis == "x" else (1, ()), 0)]

    def views(self, here, step, names, part):
        return self.src[0], self.dst[0], self.dst[0]


class Swap:
    def swap_scratch(self):
        return [pltpu.SemaphoreType.DMA((3,))]

    def give(self, total, sems):
        self.kept = pltpu.make_async_copy(total, self.dst[0], sems.at[0])
        self.kept.start()
        self.given = None
        if len(self.outs) > 1:
            self.given = pltpu.make_async_remote_copy(
                src_ref=total, dst_ref=self.dst[1], send_sem=sems.at[1], recv_sem=sems.at[2],
                device_id=flip(self.here, "x"), device_id_type=MESH,
            )
            self.given.start()

    def given_wait(self):
        self.kept.wait()
        if self.given is not None:
            self.given.wait()


class Owners(Load, Swap):
    def __init__(self, source, parts=1, swap=False, fold=False, **stages):
        super().__init__(source, **stages)
        self.setup(source.shape[0], source.shape[1], source.dtype, parts, swap, fold)

    def setup(self, depth, width, kind, parts, swap, fold):
        self.parts = parts
        self.fold = fold
        self.kind = kind
        self.rows = depth // (self.groups * SIDES)
        self.piece = width // parts
        self.wide = parts * SIDES * self.piece
        total = (self.rows, self.piece if fold else self.wide)
        self.total = total
        self.outs = [jax.ShapeDtypeStruct(total, kind)] * (1 + swap)
        self.swap = swap

    def reached(self):
        return super().reached() | ({(0, ("x",))} if self.swap else set())

    def spaces(self):
        return [pltpu.VMEM if self.fold else pl.ANY] * len(self.sources), [pl.ANY] * len(self.outs)

    def scratch(self):
        return self.semaphores() + self.swap_scratch() + [
            pltpu.VMEM((self.groups, self.rows, self.wide), self.kind),
            pltpu.VMEM(self.total, self.kind),
        ]

    def views(self, here, step, names, part):
        mine, other, there, whence = self.around(here, step, names)
        terms = self.more[1]
        return (
            self.slice_of(there * SIDES + other, part),
            terms.at[here["zh"], :, at((part * SIDES + mine) * self.piece, self.piece)],
            terms.at[whence, :, at((part * SIDES + other) * self.piece, self.piece)],
        )

    def slice_of(self, target, part):
        return self.src[0].at[
            at(target * self.rows, self.rows), pl.ds(part * self.piece, self.piece)
        ]

    def finish(self):
        sems, terms, total = self.more[:3]
        step = self.piece if self.fold else min(512, self.wide)

        def add(start):
            value = terms[0, :, pl.ds(start, step)].astype(jnp.float32)
            for group in range(1, self.groups):
                value = value + terms[group, :, pl.ds(start, step)].astype(jnp.float32)
            return value

        if self.fold:
            value = add(0)
            for side in range(1, SIDES):
                value = value + add(side * step)
            total[...] = value
        else:

            @pl.loop(0, self.wide // step)
            def _(k):
                start = pl.multiple_of(k * step, step)
                total[:, pl.ds(start, step)] = add(start).astype(total.dtype)

        self.give(total, sems)

    def leave(self):
        super().leave()
        self.given_wait()


class Product(Owners):
    def __init__(self, left, right, parts=1, swap=False, **stages):
        Load.__init__(self, left, **stages)
        self.sources = [left, right]
        self.setup(left.shape[1], right.shape[1], jnp.bfloat16, parts, swap, False)

    def scratch(self):
        depth, width = self.sources[0].shape[0], self.sources[1].shape[1]
        return super().scratch() + [
            pltpu.VMEM((2, depth, 2 * self.rows), jnp.bfloat16),
            pltpu.VMEM((depth, width), jnp.bfloat16),
            pltpu.VMEM((self.groups * SIDES * self.rows, width), jnp.bfloat16),
            pltpu.SemaphoreType.DMA((3,)),
        ]

    def slice_of(self, target, part):
        return self.more[5].at[
            at(target * self.rows, self.rows), pl.ds(part * self.piece, self.piece)
        ]

    def tiles(self):
        order = [
            (step, names)
            for step in reversed(range(self.groups))
            for names in SIDE_PEERS
            if "c" not in names
        ]
        return order

    def first_row(self, step, names):
        _, other, there, _ = self.around(self.here, step, names)
        return (there * SIDES + (other // 2) * 2) * self.rows

    def fetch(self, k):
        step, names = self.tiles()[k]
        left = self.src[0].at[:, at(self.first_row(step, names), 2 * self.rows)]
        return pltpu.make_async_copy(left, self.more[3].at[k % 2], self.more[6].at[k % 2])

    def begin(self):
        self.right = pltpu.make_async_copy(self.src[1], self.more[4], self.more[6].at[2])
        self.right.start()
        self.fetch(0).start()
        self.fetch(1).start()

    def start(self, stage):
        tiles = self.tiles()
        _, _, _, lefts, right, result, _ = self.more
        for k, (step, names) in enumerate(tiles):
            if self.stages[1 if step else 0] != stage:
                continue
            if k == 0:
                self.right.wait()
            self.fetch(k).wait()
            rows = at(self.first_row(step, names), 2 * self.rows)
            wide = min(256, self.sources[1].shape[1])
            left = lefts[k % 2]
            for column in range(0, self.sources[1].shape[1], wide):
                columns = pl.ds(column, min(wide, self.sources[1].shape[1] - column))
                result[rows, columns] = lax.dot_general(
                    left, right[:, columns], (((0,), (0,)), ((), ())),
                    preferred_element_type=jnp.float32,
                ).astype(jnp.bfloat16)
            if k + 2 < len(tiles):
                self.fetch(k + 2).start()
            for _, copy, _, peer in self.copies:
                if peer in ((step, names), (step, names + ("c",))):
                    copy.start()


class Pair(Load, Swap):
    def __init__(self, source, **stages):
        super().__init__(source, **stages)
        self.outs = [jax.ShapeDtypeStruct(source.shape, source.dtype)] * 2

    def spaces(self):
        return [pltpu.VMEM], [pl.ANY] * 2

    def moves(self):
        return [((1, ()), 0)]

    def reached(self):
        return {(1, ()), (0, ("x",))}

    def scratch(self):
        shape = self.outs[0].shape
        return self.semaphores() + self.swap_scratch() + [
            pltpu.VMEM(shape, jnp.bfloat16), pltpu.VMEM(shape, jnp.bfloat16)
        ]

    def views(self, here, step, names, part):
        return self.src[0], self.more[1], self.more[1]

    def finish(self):
        sems, came, total = self.more
        total[...] = (
            self.src[0][...].astype(jnp.float32) + came[...].astype(jnp.float32)
        ).astype(jnp.bfloat16)
        self.give(total, sems)

    def leave(self):
        super().leave()
        self.given_wait()


class Cargo:
    def __init__(self, loads):
        self.loads = loads
        self.sources = [s for load in loads for s in load.sources]
        self.outs = [o for load in loads for o in load.outs]
        self.in_specs = [pl.BlockSpec(memory_space=s) for load in loads for s in load.spaces()[0]]
        self.out_specs = [pl.BlockSpec(memory_space=s) for load in loads for s in load.spaces()[1]]
        self.scratch = [s for load in loads for s in load.scratch()]

    def bind(self, here, sources, targets, scratch):
        sources, targets, scratch = list(sources), list(targets), list(scratch)

        def take(refs, count):
            taken = refs[:count]
            del refs[:count]
            return taken

        for load in self.loads:
            load.bind(
                here,
                take(sources, len(load.sources)),
                take(targets, len(load.outs)),
                take(scratch, len(load.scratch())),
            )
            if hasattr(load, "begin"):
                load.begin()

    def greet(self, here, names):
        reached = {(0, n) for n in names}
        for load in self.loads:
            reached |= load.reached()
        groups = lax.axis_size("zh")
        greet([owner_at(here, groups, step, n) for step, n in sorted(reached)])

    def start(self, stage):
        for load in self.loads:
            load.start(stage)

    def finish(self, early=False):
        for load in self.loads:
            if load.early == early:
                load.land()
                load.finish()
        if not early:
            for load in self.loads:
                load.leave()


GATHER_STAGES = (0, 1, 2, 3)
NEAR = [("x",), ("zl",), ("y",), ("c",)]


def call(body, name, ident, cargo, operand, space, out, out_space, scratch):
    held = [out] * (out_space == pltpu.VMEM) + [operand] * (space == pltpu.VMEM)
    held += [s for s in scratch + cargo.scratch if s.memory_space == pltpu.VMEM]
    held += [s for load in cargo.loads if load.spaces()[0][0] == pltpu.VMEM for s in load.sources]
    vmem = sum(math.prod(s.shape) * jnp.dtype(s.dtype).itemsize for s in held) + 6 * MIB
    return pl.pallas_call(
        functools.partial(body, cargo),
        out_shape=[out] + cargo.outs,
        in_specs=[pl.BlockSpec(memory_space=space)] + cargo.in_specs,
        out_specs=[pl.BlockSpec(memory_space=out_space)] + cargo.out_specs,
        scratch_shapes=scratch + cargo.scratch,
        compiler_params=pltpu.CompilerParams(
            collective_id=ident, has_side_effects=True, vmem_limit_bytes=vmem
        ),
        cost_estimate=pl.CostEstimate(flops=0, bytes_accessed=100 * MIB, transcendentals=0),
        name=name,
    )(operand, *cargo.sources)


def gather_kernel(orders, cargo, x_ref, *refs):
    n, m = len(cargo.sources), len(cargo.outs)
    sources, o_ref, targets = refs[:n], refs[n], refs[n + 1 : n + 1 + m]
    send_sem, recv_sem, core_send, core_recv, own_sem = refs[n + m + 1 : n + m + 6]
    here = place()
    spans = [pl.ds(r0, size) for _, r0, size in orders]
    orders = [o for o, _, _ in orders]
    pieces = range(len(orders))
    cargo.bind(here, sources, targets, refs[n + m + 6 :])
    cargo.greet(here, NEAR)
    own = pltpu.make_async_copy(x_ref, o_ref.at[0], own_sem)

    def spot(p, *names):
        return o_ref.at[slot(*names), spans[p]]

    def source(p, mask):
        return spot(p, *subset(orders[p], mask)) if mask else x_ref.at[spans[p]]

    def over(p, mask, k):
        whole = mask | 1 << k
        return pltpu.make_async_remote_copy(
            src_ref=source(p, mask), dst_ref=spot(p, *subset(orders[p], whole)),
            send_sem=send_sem.at[p, whole], recv_sem=recv_sem.at[p, whole],
            device_id=flip(here, orders[p][k]), device_id_type=MESH,
        )

    def across(p, mask):
        return pltpu.make_async_remote_copy(
            src_ref=source(p, mask), dst_ref=spot(p, "c", *subset(orders[p], mask)),
            send_sem=core_send.at[p, mask], recv_sem=core_recv.at[p, mask],
            device_id=flip(here, "c"), device_id_type=MESH,
        )

    sent = []
    for mask in range(8):
        for p in pieces:
            if mask:
                landing = spot(p, *subset(orders[p], mask))
                pltpu.make_async_copy(landing, landing, recv_sem.at[p, mask]).wait()
            for k in range(mask.bit_length(), 3):
                sent.append(over(p, mask, k))
                sent[-1].start()
        for p in pieces:
            sent.append(across(p, mask))
            sent[-1].start()
        if mask == 0:
            own.start()
        if mask in GATHER_STAGES:
            cargo.start(GATHER_STAGES.index(mask))
    for mask in range(8):
        for p in pieces:
            landing = spot(p, "c", *subset(orders[p], mask))
            pltpu.make_async_copy(landing, landing, core_recv.at[p, mask]).wait()
    for copy in sent:
        copy.wait_send()
    own.wait()
    cargo.finish()


def gather_cube(block, ident, loads=(), orders=None):
    rows, width = block.shape
    orders = orders or thirds(rows)
    out = call(
        functools.partial(gather_kernel, orders),
        "gather_cube", ident, Cargo(list(loads)), block, pl.ANY,
        jax.ShapeDtypeStruct((MEMBERS, rows, width), block.dtype), pl.ANY,
        [pltpu.SemaphoreType.DMA((len(orders), 8))] * 4 + [pltpu.SemaphoreType.DMA(())],
    )
    return [out[0].reshape(MEMBERS * rows, width)] + list(out[1:])


def scatter_kernel(orders, cargo, p_ref, *refs):
    n, m = len(cargo.sources), len(cargo.outs)
    sources, o_ref, targets = refs[:n], refs[n], refs[n + 1 : n + 1 + m]
    acc, rcore, came, core_send, core_recv, send_sem, recv_sem = refs[n + m + 1 : n + m + 8]
    here = place()
    spans = [pl.ds(r0, size) for _, r0, size in orders]
    orders = [o for o, _, _ in orders]
    pieces = range(len(orders))
    cargo.bind(here, sources, targets, refs[n + m + 8 :])
    cargo.greet(here, NEAR)

    def away(p, mask):
        return pltpu.make_async_remote_copy(
            src_ref=p_ref.at[slot("c", *subset(orders[p], mask)), spans[p]],
            dst_ref=rcore.at[mask, spans[p]],
            send_sem=core_send.at[p, mask], recv_sem=core_recv.at[p, mask],
            device_id=flip(here, "c"), device_id_type=MESH,
        )

    sequence = [7, 3, 5, 1, 6, 2, 4, 0]
    sent = []
    for mask in sequence:
        for p in pieces:
            sent.append(away(p, mask))
            sent[-1].start()
    cargo.start(0)

    def over(p, mask):
        k = (mask & -mask).bit_length() - 1
        return pltpu.make_async_remote_copy(
            src_ref=acc.at[mask, spans[p]], dst_ref=came.at[mask, spans[p]],
            send_sem=send_sem.at[p, mask], recv_sem=recv_sem.at[p, mask],
            device_id=flip(here, orders[p][k]), device_id_type=MESH,
        )

    for mask in sequence:
        for p in pieces:
            away(p, mask).wait_recv()
            own = slot(*subset(orders[p], mask))
            acc[mask, spans[p]] = p_ref[own, spans[p]] + rcore[mask, spans[p]]
            if mask & 1:
                sent.append(over(p, mask))
                sent[-1].start()
    cargo.start(1)
    for k in range(3):
        low = 1 << k
        for mask in [b for b in (6, 2, 4, 0) if b & (2 * low - 1) == 0]:
            for p in pieces:
                over(p, mask | low).wait_recv()
                if mask == 0 and k == 2:
                    o_ref[spans[p]] = acc[0, spans[p]].astype(jnp.float32) + came[
                        4, spans[p]
                    ].astype(jnp.float32)
                    continue
                acc[mask, spans[p]] = acc[mask, spans[p]] + came[mask | low, spans[p]]
                if mask & (2 * low):
                    sent.append(over(p, mask))
                    sent[-1].start()
        if k < 2:
            cargo.start(2 + k)
        if k == 1:
            cargo.finish(early=True)
    for copy in sent:
        copy.wait_send()
    cargo.finish()


def scatter_cube(partial, ident, loads=(), orders=None):
    total, width = partial.shape
    rows = total // MEMBERS
    orders = orders or thirds(rows)
    return call(
        functools.partial(scatter_kernel, orders),
        "scatter_cube", ident, Cargo(list(loads)),
        partial.astype(jnp.bfloat16).reshape(MEMBERS, rows, width), pltpu.VMEM,
        jax.ShapeDtypeStruct((rows, width), jnp.float32), pltpu.VMEM,
        [pltpu.VMEM((8, rows, width), jnp.bfloat16)] * 3
        + [pltpu.SemaphoreType.DMA((len(orders), 8))] * 4,
    )


def exchange_kernel(v_ref, o_ref, slots, send_sem, recv_sem):
    here = place()
    greet([flip(here, *names) for names in PEERS])
    copies = []
    for names in PEERS:
        k = slot(*names)
        copies.append(pltpu.make_async_remote_copy(
            src_ref=v_ref, dst_ref=slots.at[k], send_sem=send_sem.at[k], recv_sem=recv_sem.at[k],
            device_id=flip(here, *names), device_id_type=MESH,
        ))
        copies[-1].start()
    for copy in copies:
        copy.wait_recv()
    slots[0] = v_ref[...]
    for row in range(v_ref.shape[0]):
        kind, mine = divmod(row, MEMBERS)
        terms = [
            slots[k, pl.ds(kind * MEMBERS + SLOT[SLOTS[mine] ^ SLOTS[k]], 1), :]
            for k in range(MEMBERS)
        ]
        while len(terms) > 1:
            terms = [terms[2 * i] + terms[2 * i + 1] for i in range(len(terms) // 2)]
        o_ref[pl.ds(row, 1), :] = terms[0]
    for copy in copies:
        copy.wait_send()


def sum_cube(values, ident):
    shape = values.shape
    return pl.pallas_call(
        exchange_kernel,
        out_shape=jax.ShapeDtypeStruct(shape, jnp.float32),
        in_specs=[pl.BlockSpec(memory_space=pltpu.VMEM)],
        out_specs=pl.BlockSpec(memory_space=pltpu.VMEM),
        scratch_shapes=[
            pltpu.VMEM((MEMBERS,) + shape, jnp.float32),
            pltpu.SemaphoreType.DMA((MEMBERS,)),
            pltpu.SemaphoreType.DMA((MEMBERS,)),
        ],
        compiler_params=pltpu.CompilerParams(collective_id=ident, has_side_effects=True),
        cost_estimate=pl.CostEstimate(flops=0, bytes_accessed=20 * MIB, transcendentals=0),
        name="sum_cube",
    )(values)


def rope_tables(positions):
    frequency = theta_base ** (-2.0 * jnp.arange(HD // 2).astype(jnp.float32) / HD)
    angles = positions[:, None] * frequency[None, :]
    return (jnp.cos(angles), jnp.sin(angles))


def rotate(values, cos_table, sin_table):
    half_width = values.shape[-1] // 2
    former = values[..., :half_width]
    latter = values[..., half_width:]
    return jnp.concatenate(
        [former * cos_table - latter * sin_table, latter * cos_table + former * sin_table], axis=-1
    )


def normalize(values, scales):
    inverse = lax.rsqrt(jnp.mean(values * values, axis=-1, keepdims=True) + epsilon)
    return (values * inverse * scales, inverse)


def norm_back(upstream, values, inverse, scales):
    unit_rows = values * inverse
    scaled = upstream * scales
    value_grad = inverse * (
        scaled - unit_rows * jnp.mean(scaled * unit_rows, axis=-1, keepdims=True)
    )
    return (value_grad, jnp.sum(upstream * unit_rows, axis=0))


def contract_last(operand, matrix):
    return lax.dot_general(
        operand, matrix, (((1,), (1,)), ((), ())), preferred_element_type=jnp.float32
    )


def contract_first(operand, matrix):
    return lax.dot_general(
        operand, matrix, (((0,), (0,)), ((), ())), preferred_element_type=jnp.float32
    )


def row_sums(pair, ident):
    total = pair[0].shape[0]
    flat = jnp.concatenate([v.reshape(MEMBERS, total // MEMBERS) for v in pair], axis=0)
    summed = sum_cube(flat, ident).reshape(2, total, 1)
    return summed[0], summed[1]


def finish_kernel(mine_ref, came_ref, o_ref):
    own = pl.program_id(1) == lax.axis_index("x")
    o_ref[...] = jnp.where(own, mine_ref[...], came_ref[...]).astype(jnp.float32)


def whole_rows(mine, came, parts):
    rows, width = mine.shape
    step = min(2048, width // parts)
    steps = width // parts // step
    half = pl.BlockSpec((rows, step), lambda p, x, k: (0, p * steps + k))
    return pl.pallas_call(
        finish_kernel,
        grid=(parts, 2, steps),
        out_shape=jax.ShapeDtypeStruct((rows, 2 * width), jnp.float32),
        in_specs=[half, half],
        out_specs=pl.BlockSpec((rows, step), lambda p, x, k: (0, (2 * p + x) * steps + k)),
        compiler_params=pltpu.CompilerParams(vmem_limit_bytes=32 * MIB),
        cost_estimate=pl.CostEstimate(
            flops=0, bytes_accessed=16 * rows * width, transcendentals=0
        ),
        name="whole_rows",
    )(mine, came)


def owners_product(left, right, parts=1, **options):
    if left.shape[1] // (lax.axis_size("zh") * SIDES) % 128 == 0:
        return Product(left, right, parts, **options)
    return Owners(contract_first(left, right).astype(jnp.bfloat16), parts, **options)


def heads_are_owners(rows):
    return lax.axis_size("zh") == 2 and rows == HD


def gathered_head_rows(weight):
    full = lax.all_gather(weight, OWNERS, axis=0, tiled=True)
    head = lax.axis_index(("x", "zl", "y", "c"))
    return lax.dynamic_slice_in_dim(full, head * HD, HD, axis=0)


def summed_head_rows(grad_rows, rows):
    head = lax.axis_index(("x", "zl", "y", "c"))
    full = jnp.zeros((MEMBERS * HD, grad_rows.shape[1]), jnp.float32)
    full = lax.dynamic_update_slice_in_dim(full, grad_rows, head * HD, axis=0)
    full = lax.psum(full, EVERY)
    return lax.dynamic_slice_in_dim(full, lax.axis_index(OWNERS) * rows, rows, axis=0)


def silu_grads(hidden_grad, gate_part, up_part):
    sigmoid_gate = jax.nn.sigmoid(gate_part)
    gate_grad = hidden_grad * up_part * sigmoid_gate * (1.0 + gate_part * (1.0 - sigmoid_gate))
    up_grad = hidden_grad * gate_part * sigmoid_gate
    return gate_grad.astype(jnp.bfloat16), up_grad.astype(jnp.bfloat16)


def shards(tokens, w_qkv, w_out, w_gate_up, w_down_t, gains, starts, cotangent):
    count_rows, width = tokens.shape
    owned = gains.shape[0]
    groups = lax.axis_size("zh")
    total = MEMBERS * count_rows
    score_scale = 1.0 / math.sqrt(HD)
    direct = heads_are_owners(owned)
    local_rows = jnp.arange(count_rows, dtype=jnp.int32)
    seq_begin = lax.cummax(jnp.where(starts == 1, local_rows, 0), axis=0)

    gain_part = jnp.pad(gains.astype(jnp.float32).T, ((0, 4), (0, 0)))
    begin_part = jnp.broadcast_to(seq_begin.astype(jnp.float32)[None, :], (8, count_rows))
    loads = [Few(gain_part, False), Few(begin_part, True), Columns(w_qkv, 3)]
    if direct:
        loads.append(Whole(w_out, "zh"))
    tokens_all, gain_all, begin_all, qkv_cols, *out_other = gather_cube(
        tokens, 1, loads, halves(count_rows, "zl", "y", "x")
    )
    same = lax.axis_index("x") == lax.axis_index("zh")
    if direct:
        out_rows = jnp.where(same, w_out, out_other[0])
    else:
        out_rows = gathered_head_rows(w_out)
    gain_rows = gain_all[:, :4].transpose(1, 0, 2).reshape(4, width)
    begin_all = begin_all[:, 0]
    head = lax.axis_index(("x", "zl", "y", "c"))
    head_gains = lax.dynamic_slice_in_dim(gain_rows, head * HD, HD, axis=1)
    rows_f32 = local_rows.astype(jnp.float32)
    positions = (rows_f32[None, :] - begin_all).reshape(total)
    cos_table, sin_table = rope_tables(positions)
    allowed = (rows_f32[None, None, :] <= rows_f32[None, :, None]) & (
        rows_f32[None, None, :] >= begin_all[:, :, None]
    )

    def blocks(values):
        return values.reshape(MEMBERS, count_rows, HD)

    projected = jnp.dot(tokens_all, qkv_cols, preferred_element_type=jnp.float32)
    query_raw = projected[:, :HD]
    key_raw = projected[:, HD : 2 * HD]
    value_bf = blocks(projected[:, 2 * HD :].astype(jnp.bfloat16))
    query_sq, key_sq = row_sums(
        (jnp.sum(query_raw * query_raw, axis=1), jnp.sum(key_raw * key_raw, axis=1)), 2
    )
    query_inv = lax.rsqrt(query_sq / width + epsilon)
    key_inv = lax.rsqrt(key_sq / width + epsilon)
    query_unit = query_raw * query_inv
    key_unit = key_raw * key_inv
    query_bf = blocks(rotate(query_unit * head_gains[0], cos_table, sin_table).astype(jnp.bfloat16))
    key_bf = blocks(rotate(key_unit * head_gains[1], cos_table, sin_table).astype(jnp.bfloat16))
    scores = (
        jnp.einsum("bqd,bkd->bqk", query_bf, key_bf, preferred_element_type=jnp.float32)
        * score_scale
    )
    scores = jnp.where(allowed, scores, -1e30)
    exponent = jnp.exp(scores - jnp.max(scores, axis=-1, keepdims=True))
    attention_f32 = exponent / jnp.sum(exponent, axis=-1, keepdims=True)
    attention = attention_f32.astype(jnp.bfloat16)
    attended = (
        jnp.einsum("bqk,bkd->bqd", attention, value_bf, preferred_element_type=jnp.float32)
        .reshape(total, HD)
        .astype(jnp.bfloat16)
    )
    x_most = halves(count_rows, "x", "y", "zl")
    x_last = halves(count_rows, "zl", "y", "x")
    x_or_y = (
        (("x", "y", "zl"), 0, count_rows // 2),
        (("y", "x", "zl"), count_rows // 2, count_rows // 2),
    )
    y_last = halves(count_rows, "zl", "x", "y")
    branch, down_cols = scatter_cube(
        jnp.dot(attended, out_rows, preferred_element_type=jnp.float32),
        3, [Columns(w_down_t, near=1)], x_most,
    )
    branch_norm, branch_inv = normalize(branch, gain_rows[2])
    middle = tokens.astype(jnp.float32) + branch_norm
    middle_all, gate_up_cols = gather_cube(
        middle.astype(jnp.bfloat16), 4, [Columns(w_gate_up, 2, near=3)], x_last
    )
    gate_up = jnp.dot(middle_all, gate_up_cols, preferred_element_type=jnp.float32)
    gate_part, up_part = jnp.split(gate_up, 2, axis=1)
    hidden_bf = (gate_part * jax.nn.sigmoid(gate_part) * up_part).astype(jnp.bfloat16)
    (feed_out,) = scatter_cube(contract_last(hidden_bf, down_cols), 5)
    feed_norm, feed_inv = normalize(feed_out, gain_rows[3])
    mixed = (middle + feed_norm).astype(jnp.bfloat16)

    upstream = cotangent.astype(jnp.float32)
    feed_grad, gain_feed = norm_back(upstream, feed_out, feed_inv, gain_rows[3])
    (feed_all,) = gather_cube(feed_grad.astype(jnp.bfloat16), 6)
    hidden_grad = jnp.dot(feed_all, down_cols, preferred_element_type=jnp.float32)
    gate_up_bf = jnp.concatenate(silu_grads(hidden_grad, gate_part, up_part), axis=1)
    middle_part = contract_last(gate_up_bf, gate_up_cols)
    middle_sum, gate_up_sum = scatter_cube(
        middle_part, 7, [owners_product(middle_all, gate_up_bf, 2, near=1)], x_most
    )
    middle_grad = upstream + middle_sum
    branch_grad, gain_branch = norm_back(middle_grad, branch, branch_inv, gain_rows[2])
    branch_all, down_sum, gate_up_other = gather_cube(
        branch_grad.astype(jnp.bfloat16), 8,
        [
            owners_product(feed_all, hidden_bf, far=1, near=3),
            Whole(gate_up_sum, "x", near=1),
        ], y_last,
    )
    down_other = lax.ppermute(down_sum, "x", [(0, 1), (1, 0)])
    out_grad = contract_first(attended, branch_all)
    attended_grad = blocks(contract_last(branch_all, out_rows).astype(jnp.bfloat16))
    prob_grad = jnp.einsum(
        "bqd,bkd->bqk", attended_grad, value_bf, preferred_element_type=jnp.float32
    )
    score_bf = (
        attention_f32 * (prob_grad - jnp.sum(attention_f32 * prob_grad, axis=-1, keepdims=True))
    ).astype(jnp.bfloat16)
    value_grad = jnp.einsum(
        "bqk,bqd->bkd", attention, attended_grad, preferred_element_type=jnp.float32
    ).reshape(total, HD)
    query_grad = (
        jnp.einsum("bqk,bkd->bqd", score_bf, key_bf, preferred_element_type=jnp.float32)
        * score_scale
    ).reshape(total, HD)
    key_grad = (
        jnp.einsum("bqk,bqd->bkd", score_bf, query_bf, preferred_element_type=jnp.float32)
        * score_scale
    ).reshape(total, HD)
    query_grad = rotate(query_grad, cos_table, -sin_table)
    key_grad = rotate(key_grad, cos_table, -sin_table)
    query_scaled = query_grad * head_gains[0]
    key_scaled = key_grad * head_gains[1]
    query_dot, key_dot = row_sums(
        (jnp.sum(query_scaled * query_unit, axis=1), jnp.sum(key_scaled * key_unit, axis=1)), 9
    )
    query_raw_grad = query_inv * (query_scaled - query_unit * (query_dot / width))
    key_raw_grad = key_inv * (key_scaled - key_unit * (key_dot / width))
    projected_bf = jnp.concatenate([query_raw_grad, key_raw_grad, value_grad], axis=1).astype(
        jnp.bfloat16
    )

    gain_head = jnp.stack(
        [jnp.sum(query_grad * query_unit, axis=0), jnp.sum(key_grad * key_unit, axis=0)]
    )
    gain_terms = jnp.concatenate(
        [
            lax.dynamic_update_slice_in_dim(
                jnp.zeros((2, width), jnp.float32), gain_head, head * HD, axis=1
            ),
            jnp.stack([gain_branch, gain_feed]),
        ]
    )
    lanes = -(-owned // 128) * 128
    gain_terms = jnp.pad(
        gain_terms.reshape(4, groups * SIDES, owned).transpose(1, 0, 2),
        ((0, 0), (0, 4), (0, lanes - owned)),
    ).reshape(groups * SIDES * 8, lanes)
    loads = [
        owners_product(tokens_all, projected_bf, 3, swap=True, near=1, early=True),
        Owners(gain_terms, swap=True, fold=True, early=True),
    ]
    if direct:
        loads.append(Pair(out_grad.astype(jnp.bfloat16), early=True))
    tokens_sum, qkv_sum, qkv_other, gain_sum, gain_other, *out_both = scatter_cube(
        contract_last(projected_bf, qkv_cols), 10, loads, x_most
    )
    grad_tokens = middle_grad + tokens_sum
    if direct:
        grad_out = jnp.where(same, out_both[0], out_both[1]).astype(jnp.float32)
    else:
        grad_out = summed_head_rows(out_grad, owned)
    grad_qkv = whole_rows(qkv_sum, qkv_other, 3)
    grad_gate_up = whole_rows(gate_up_sum, gate_up_other, 2)
    grad_down_t = whole_rows(down_sum, down_other, 1)
    grad_gains = (gain_sum + gain_other)[:4, :owned].T
    return (mixed, grad_tokens, grad_qkv, grad_out, grad_gate_up, grad_down_t, grad_gains)


def solution(mesh):
    sizes = dict(mesh.shape)
    groups = sizes["fsdp"] // SIDES
    finer = Mesh(mesh.devices.reshape(2, groups, 2, 2, 2), EVERY)
    return jax.shard_map(
        shards,
        mesh=finer,
        in_specs=(
            P(EVERY, None),
            P(OWNERS, None),
            P(OWNERS, None),
            P(OWNERS, None),
            P(OWNERS, None),
            P(OWNERS, None),
            P(EVERY),
            P(EVERY, None),
        ),
        out_specs=(
            P(EVERY, None),
            P(EVERY, None),
            P(OWNERS, None),
            P(OWNERS, None),
            P(OWNERS, None),
            P(OWNERS, None),
            P(OWNERS, None),
        ),
        check_vma=False,
    )
```

```python
import functools
import math

import jax
import jax.numpy as jnp
from jax import lax
from jax.experimental import pallas as pl
from jax.experimental.pallas import tpu as pltpu
from jax.sharding import Mesh, PartitionSpec as P

HD = 128

epsilon = 1e-06
theta_base = 500000.0

OWNERS = ("zh", "zl", "y", "c")
EVERY = ("x", "zh", "zl", "y", "c")
MEMBERS = 16
SIDES = 8
SIDE_BITS = {"zl": 4, "y": 2, "c": 1}
BITS = {"x": 8, "zl": 4, "y": 2, "c": 1}
SLOTS = [
    frozenset(names + core)
    for names in (
        (), ("x",), ("y",), ("zl",), ("x", "y"), ("x", "zl"), ("y", "zl"), ("x", "y", "zl"),
    )
    for core in ((), ("c",))
]
SLOT = {names: k for k, names in enumerate(SLOTS)}
MESH = pl.DeviceIdType.MESH
MIB = 1 << 20


def thirds(rows):
    unit = rows // 8
    return (
        (("x", "y", "zl"), 0, 3 * unit),
        (("y", "zl", "x"), 3 * unit, 3 * unit),
        (("zl", "x", "y"), 6 * unit, 2 * unit),
    )


def halves(rows, *order):
    return ((order, 0, rows // 2), (order, rows // 2, rows // 2))


PEERS = [tuple(n for n in BITS if m & BITS[n]) for m in range(1, MEMBERS)]
SIDE_PEERS = [tuple(n for n in SIDE_BITS if m & SIDE_BITS[n]) for m in range(SIDES)]


def slot(*names):
    return SLOT[frozenset(names)]


def place():
    return {name: lax.axis_index(name) for name in EVERY}


def flip(here, *names):
    return {name: 1 - here[name] for name in names}


def with_bits(here, names, bits):
    index = 0
    for name, bit in bits.items():
        index = index + bit * ((1 - here[name]) if name in names else here[name])
    return index


def subset(order, mask):
    return tuple(name for k, name in enumerate(order) if mask >> k & 1)


def greet(devices):
    barrier = pltpu.get_barrier_semaphore()
    for device in devices:
        pl.semaphore_signal(barrier, inc=1, device_id=device, device_id_type=MESH)
    pl.semaphore_wait(barrier, len(devices))


def owner_at(here, groups, step, names):
    device = flip(here, *names)
    if step:
        device["zh"] = lax.rem(here["zh"] + step, groups)
    return device


def at(start, size):
    return pl.ds(pl.multiple_of(start, size), size)


class Load:
    space = pltpu.HBM
    parts = 1

    def __init__(self, source, far=0, near=0, early=False):
        self.sources = [source]
        self.stages = (near, far)
        self.early = early
        self.groups = lax.axis_size("zh")

    def spaces(self):
        return [self.space] * len(self.sources), [self.space] * len(self.outs)

    def semaphores(self):
        count = len(self.moves())
        return [pltpu.SemaphoreType.DMA((count,)), pltpu.SemaphoreType.DMA((count,))]

    def scratch(self):
        return self.semaphores()

    def moves(self):
        return [
            ((step, names), part)
            for step in range(self.groups)
            for names in SIDE_PEERS
            for part in range(self.parts)
        ]

    def reached(self):
        return {peer for peer, _ in self.moves() if peer != (0, ())}

    def around(self, here, step, names):
        there = lax.rem(here["zh"] + step, self.groups)
        whence = lax.rem(here["zh"] + self.groups - step, self.groups)
        mine, other = with_bits(here, (), SIDE_BITS), with_bits(here, names, SIDE_BITS)
        return mine, other, there, whence

    def bind(self, here, sources, targets, scratch):
        self.here, self.src, self.dst = here, sources, targets
        self.send, self.recv, *self.more = scratch
        self.copies = []
        for index, ((step, names), part) in enumerate(self.moves()):
            source, target, landing = self.views(here, step, names, part)
            stage = self.stages[1 if step else 0]
            if not step and not names:
                copy = pltpu.make_async_copy(source, target, self.send.at[index])
                self.copies.append((stage, copy, None, (step, names)))
                continue
            copy = pltpu.make_async_remote_copy(
                src_ref=source, dst_ref=target,
                send_sem=self.send.at[index], recv_sem=self.recv.at[index],
                device_id=owner_at(here, self.groups, step, names), device_id_type=MESH,
            )
            landed = pltpu.make_async_copy(landing, landing, self.recv.at[index])
            self.copies.append((stage, copy, landed, (step, names)))

    def start(self, stage):
        for when, copy, _, _ in self.copies:
            if when == stage:
                copy.start()

    def land(self):
        for _, copy, landed, _ in self.copies:
            (copy if landed is None else landed).wait()

    def finish(self):
        pass

    def leave(self):
        for _, copy, landed, _ in self.copies:
            if landed is not None:
                copy.wait_send()


class Columns(Load):
    def __init__(self, source, parts=1, **stages):
        super().__init__(source, **stages)
        self.parts = parts
        self.rows = source.shape[0]
        self.piece = source.shape[1] // (parts * MEMBERS)
        shape = (self.groups * SIDES * self.rows, parts * self.piece)
        self.outs = [jax.ShapeDtypeStruct(shape, source.dtype)]

    def views(self, here, step, names, part):
        mine, other, _, whence = self.around(here, step, names)
        first = part * MEMBERS + here["x"] * SIDES + other
        columns = pl.ds(part * self.piece, self.piece)
        return (
            self.src[0].at[:, at(first * self.piece, self.piece)],
            self.dst[0].at[at((here["zh"] * SIDES + mine) * self.rows, self.rows), columns],
            self.dst[0].at[at((whence * SIDES + other) * self.rows, self.rows), columns],
        )


class Few(Load):
    space = pltpu.VMEM

    def __init__(self, source, cube):
        super().__init__(source)
        self.cube = cube
        count = MEMBERS if cube else self.groups * SIDES
        self.outs = [jax.ShapeDtypeStruct((count,) + source.shape, source.dtype)]

    def moves(self):
        if self.cube:
            return [((0, names), 0) for names in [()] + PEERS]
        return super().moves()

    def views(self, here, step, names, part):
        if self.cube:
            spot = self.dst[0].at[slot(*names)]
            return self.src[0], spot, spot
        mine, other, _, whence = self.around(here, step, names)
        return (
            self.src[0],
            self.dst[0].at[here["zh"] * SIDES + mine],
            self.dst[0].at[whence * SIDES + other],
        )


class Whole(Load):
    def __init__(self, source, axis, **stages):
        super().__init__(source, **stages)
        self.axis = axis
        self.outs = [jax.ShapeDtypeStruct(source.shape, source.dtype)]

    def moves(self):
        return [((0, ("x",)) if self.axis == "x" else (1, ()), 0)]

    def views(self, here, step, names, part):
        return self.src[0], self.dst[0], self.dst[0]


class Swap:
    def swap_scratch(self):
        return [pltpu.SemaphoreType.DMA((3,))]

    def give(self, total, sems):
        self.kept = pltpu.make_async_copy(total, self.dst[0], sems.at[0])
        self.kept.start()
        self.given = None
        if len(self.outs) > 1:
            self.given = pltpu.make_async_remote_copy(
                src_ref=total, dst_ref=self.dst[1], send_sem=sems.at[1], recv_sem=sems.at[2],
                device_id=flip(self.here, "x"), device_id_type=MESH,
            )
            self.given.start()

    def given_wait(self):
        self.kept.wait()
        if self.given is not None:
            self.given.wait()


class Owners(Load, Swap):
    def __init__(self, source, parts=1, swap=False, fold=False, **stages):
        super().__init__(source, **stages)
        self.setup(source.shape[0], source.shape[1], source.dtype, parts, swap, fold)

    def setup(self, depth, width, kind, parts, swap, fold):
        self.parts = parts
        self.fold = fold
        self.kind = kind
        self.rows = depth // (self.groups * SIDES)
        self.piece = width // parts
        self.wide = parts * SIDES * self.piece
        total = (self.rows, self.piece if fold else self.wide)
        self.total = total
        self.outs = [jax.ShapeDtypeStruct(total, kind)] * (1 + swap)
        self.swap = swap

    def reached(self):
        return super().reached() | ({(0, ("x",))} if self.swap else set())

    def spaces(self):
        return [pltpu.VMEM if self.fold else pltpu.HBM] * len(self.sources), [pltpu.HBM] * len(self.outs)

    def scratch(self):
        return self.semaphores() + self.swap_scratch() + [
            pltpu.VMEM((self.groups, self.rows, self.wide), self.kind),
            pltpu.VMEM(self.total, self.kind),
        ]

    def views(self, here, step, names, part):
        mine, other, there, whence = self.around(here, step, names)
        terms = self.more[1]
        return (
            self.slice_of(there * SIDES + other, part),
            terms.at[here["zh"], :, at((part * SIDES + mine) * self.piece, self.piece)],
            terms.at[whence, :, at((part * SIDES + other) * self.piece, self.piece)],
        )

    def slice_of(self, target, part):
        return self.src[0].at[
            at(target * self.rows, self.rows), pl.ds(part * self.piece, self.piece)
        ]

    def finish(self):
        sems, terms, total = self.more[:3]
        step = self.piece if self.fold else min(512, self.wide)

        def add(start):
            value = terms[0, :, pl.ds(start, step)].astype(jnp.float32)
            for group in range(1, self.groups):
                value = value + terms[group, :, pl.ds(start, step)].astype(jnp.float32)
            return value

        if self.fold:
            value = add(0)
            for side in range(1, SIDES):
                value = value + add(side * step)
            total[...] = value
        else:

            @pl.loop(0, self.wide // step)
            def _(k):
                start = pl.multiple_of(k * step, step)
                total[:, pl.ds(start, step)] = add(start).astype(total.dtype)

        self.give(total, sems)

    def leave(self):
        super().leave()
        self.given_wait()


class Product(Owners):
    def __init__(self, left, right, parts=1, swap=False, columns=None, **stages):
        Load.__init__(self, left, **stages)
        self.sources = [left, right]
        self.columns = columns or (0, right.shape[1])
        self.setup(left.shape[1], self.columns[1], jnp.bfloat16, parts, swap, False)

    def scratch(self):
        depth, width = self.sources[0].shape[0], self.columns[1]
        return super().scratch() + [
            pltpu.VMEM((2, depth, 2 * self.rows), jnp.bfloat16),
            pltpu.VMEM((depth, width), jnp.bfloat16),
            pltpu.VMEM((self.groups * SIDES * self.rows, width), jnp.bfloat16),
            pltpu.SemaphoreType.DMA((3,)),
        ]

    def slice_of(self, target, part):
        return self.more[5].at[
            at(target * self.rows, self.rows), pl.ds(part * self.piece, self.piece)
        ]

    def tiles(self):
        order = [
            (step, names)
            for step in reversed(range(self.groups))
            for names in SIDE_PEERS
            if "c" not in names
        ]
        return order

    def first_row(self, step, names):
        _, other, there, _ = self.around(self.here, step, names)
        return (there * SIDES + (other // 2) * 2) * self.rows

    def fetch(self, k):
        step, names = self.tiles()[k]
        left = self.src[0].at[:, at(self.first_row(step, names), 2 * self.rows)]
        return pltpu.make_async_copy(left, self.more[3].at[k % 2], self.more[6].at[k % 2])

    def begin(self):
        right = self.src[1].at[:, pl.ds(*self.columns)]
        self.right = pltpu.make_async_copy(right, self.more[4], self.more[6].at[2])
        self.right.start()
        self.fetch(0).start()
        self.fetch(1).start()

    def start(self, stage):
        tiles = self.tiles()
        _, _, _, lefts, right, result, _ = self.more
        for k, (step, names) in enumerate(tiles):
            if self.stages[1 if step else 0] != stage:
                continue
            if k == 0:
                self.right.wait()
            self.fetch(k).wait()
            rows = at(self.first_row(step, names), 2 * self.rows)
            width = self.columns[1]
            left = lefts[k % 2]
            for column in range(0, width, 256):
                columns = pl.ds(column, min(256, width - column))
                result[rows, columns] = lax.dot_general(
                    left, right[:, columns], (((0,), (0,)), ((), ())),
                    preferred_element_type=jnp.float32,
                ).astype(jnp.bfloat16)
            if k + 2 < len(tiles):
                self.fetch(k + 2).start()
            for _, copy, _, peer in self.copies:
                if peer in ((step, names), (step, names + ("c",))):
                    copy.start()


class Pair(Load, Swap):
    def __init__(self, source, **stages):
        super().__init__(source, **stages)
        self.outs = [jax.ShapeDtypeStruct(source.shape, source.dtype)] * 2

    def spaces(self):
        return [pltpu.VMEM], [pltpu.HBM] * 2

    def moves(self):
        return [((1, ()), 0)]

    def reached(self):
        return {(1, ()), (0, ("x",))}

    def scratch(self):
        shape = self.outs[0].shape
        return self.semaphores() + self.swap_scratch() + [
            pltpu.VMEM(shape, jnp.bfloat16), pltpu.VMEM(shape, jnp.bfloat16)
        ]

    def views(self, here, step, names, part):
        return self.src[0], self.more[1], self.more[1]

    def finish(self):
        sems, came, total = self.more
        total[...] = (
            self.src[0][...].astype(jnp.float32) + came[...].astype(jnp.float32)
        ).astype(jnp.bfloat16)
        self.give(total, sems)

    def leave(self):
        super().leave()
        self.given_wait()


class Cargo:
    def __init__(self, loads):
        self.loads = loads
        self.sources = [s for load in loads for s in load.sources]
        self.outs = [o for load in loads for o in load.outs]
        self.in_specs = [pl.BlockSpec(memory_space=s) for load in loads for s in load.spaces()[0]]
        self.out_specs = [pl.BlockSpec(memory_space=s) for load in loads for s in load.spaces()[1]]
        self.scratch = [s for load in loads for s in load.scratch()]

    def bind(self, here, sources, targets, scratch):
        sources, targets, scratch = list(sources), list(targets), list(scratch)

        def take(refs, count):
            taken = refs[:count]
            del refs[:count]
            return taken

        for load in self.loads:
            load.bind(
                here,
                take(sources, len(load.sources)),
                take(targets, len(load.outs)),
                take(scratch, len(load.scratch())),
            )
            if hasattr(load, "begin"):
                load.begin()

    def greet(self, here, names):
        reached = {(0, n) for n in names}
        for load in self.loads:
            reached |= load.reached()
        groups = lax.axis_size("zh")
        greet([owner_at(here, groups, step, n) for step, n in sorted(reached)])

    def start(self, stage):
        for load in self.loads:
            load.start(stage)

    def finish(self, early=False):
        for load in self.loads:
            if load.early == early:
                load.land()
                load.finish()
        if not early:
            for load in self.loads:
                load.leave()


class Work:
    operands = ()

    def __init__(self, *sources):
        self.sources = list(sources)

    def bind(self, sources, targets, scratch):
        self.src, self.dst, self.more = list(sources), list(targets), list(scratch)
        self.copies = []

    def begin(self):
        pass

    def keep(self, copy):
        self.copies.append(copy)
        copy.start()

    def close(self):
        for copy in self.copies:
            copy.wait()


class FeedForward(Work):
    def __init__(self, gate_up_cols, total):
        super().__init__(gate_up_cols)
        width, both = gate_up_cols.shape
        self.half, self.pair = both // 2, 2 * total // MEMBERS
        self.in_spaces = [pltpu.HBM]
        self.outs = [
            jax.ShapeDtypeStruct((total, self.half), jnp.bfloat16),
            jax.ShapeDtypeStruct((total, both), jnp.float32),
            jax.ShapeDtypeStruct((total, width), jnp.bfloat16),
        ]
        self.out_spaces = [pltpu.HBM, pltpu.HBM, pltpu.HBM]
        self.scratch = [
            pltpu.VMEM((2, self.pair, both), jnp.float32),
            pltpu.SemaphoreType.DMA((3, SIDES)),
            pltpu.VMEM(gate_up_cols.shape, gate_up_cols.dtype),
            pltpu.SemaphoreType.DMA(()),
            pltpu.VMEM((total, self.half), jnp.bfloat16),
        ]

    def begin(self):
        self.load = pltpu.make_async_copy(self.src[0], self.more[2], self.more[3])
        self.load.start()

    def tile(self, k, rows_ref):
        (hidden_out, gate_up, rows_out), (staged, sems, cols, _, hidden) = self.dst, self.more
        if k == 0:
            self.load.wait()
        rows = pl.ds(k * self.pair, self.pair)
        self.keep(pltpu.make_async_copy(rows_ref, rows_out.at[rows], sems.at[0, k]))
        if k >= 2:
            self.last[k - 2].wait()
        value = rows_ref[...]
        for start in range(0, self.half, 256):
            columns = pl.ds(start, 256)
            others = pl.ds(self.half + start, 256)
            gate = jnp.dot(value, cols[:, columns], preferred_element_type=jnp.float32)
            up = jnp.dot(value, cols[:, others], preferred_element_type=jnp.float32)
            staged[k % 2, :, columns] = gate
            staged[k % 2, :, others] = up
            hidden[rows, columns] = (gate * jax.nn.sigmoid(gate) * up).astype(jnp.bfloat16)
        self.keep(pltpu.make_async_copy(hidden.at[rows], hidden_out.at[rows], sems.at[2, k]))
        copy = pltpu.make_async_copy(staged.at[k % 2], gate_up.at[rows], sems.at[1, k])
        copy.start()
        if k == 0:
            self.last = []
        self.last.append(copy)

    def close(self):
        super().close()
        for copy in self.last[-2:]:
            copy.wait()


class FeedBack(Work):
    def __init__(self, down_cols, gate_up_cols, gate_up):
        super().__init__(down_cols, gate_up_cols, gate_up)
        total, both = gate_up.shape
        width = down_cols.shape[0]
        self.half, self.width, self.pair = both // 2, width, 2 * total // MEMBERS
        self.in_spaces = [pltpu.HBM] * 3
        self.outs = [
            jax.ShapeDtypeStruct((total, both), jnp.bfloat16),
            jax.ShapeDtypeStruct((total, width), jnp.bfloat16),
            jax.ShapeDtypeStruct((total, width), jnp.bfloat16),
        ]
        self.out_spaces = [pltpu.HBM, pltpu.VMEM, pltpu.HBM]
        self.scratch = [
            pltpu.VMEM((2, self.pair, both), jnp.float32),
            pltpu.SemaphoreType.DMA((3, SIDES)),
            pltpu.VMEM(down_cols.shape, down_cols.dtype),
            pltpu.VMEM(gate_up_cols.shape, gate_up_cols.dtype),
            pltpu.SemaphoreType.DMA((2,)),
            pltpu.VMEM((total, both), jnp.bfloat16),
        ]

    def fetch(self, k):
        rows = pl.ds(k * self.pair, self.pair)
        return pltpu.make_async_copy(
            self.src[2].at[rows], self.more[0].at[k % 2], self.more[1].at[0, k]
        )

    def begin(self):
        self.loads = [
            pltpu.make_async_copy(self.src[i], self.more[2 + i], self.more[4].at[i])
            for i in range(2)
        ]
        for copy in self.loads:
            copy.start()
        self.fetch(0).start()
        self.fetch(1).start()

    def tile(self, k, rows_ref):
        (grads_out, part, rows_out), (saved, sems, down, cols, _, grads) = self.dst, self.more
        if k == 0:
            for copy in self.loads:
                copy.wait()
        rows = pl.ds(k * self.pair, self.pair)
        self.keep(pltpu.make_async_copy(rows_ref, rows_out.at[rows], sems.at[1, k]))
        self.fetch(k).wait()
        value = rows_ref[...]
        for start in range(0, self.half, 256):
            columns = pl.ds(start, 256)
            others = pl.ds(self.half + start, 256)
            hidden_grad = jnp.dot(value, down[:, columns], preferred_element_type=jnp.float32)
            gate_bf, up_bf = silu_grads(
                hidden_grad, saved[k % 2, :, columns], saved[k % 2, :, others]
            )
            grads[rows, columns] = gate_bf
            grads[rows, others] = up_bf
        if k + 2 < SIDES:
            self.fetch(k + 2).start()
        self.keep(pltpu.make_async_copy(grads.at[rows], grads_out.at[rows], sems.at[2, k]))
        both = grads[rows]
        for start in range(0, self.width, 256):
            columns = pl.ds(start, 256)
            part[rows, columns] = contract_last(both, cols[columns, :]).astype(jnp.bfloat16)


class BranchBack(Work):
    def __init__(self, out_rows, attended):
        super().__init__(out_rows, attended)
        total, width = attended.shape[0], out_rows.shape[1]
        self.width, self.pair = width, 2 * total // MEMBERS
        self.in_spaces = [pltpu.VMEM, pltpu.VMEM]
        self.outs = [
            jax.ShapeDtypeStruct((total, HD), jnp.bfloat16),
            jax.ShapeDtypeStruct((HD, width), jnp.bfloat16),
        ]
        self.out_spaces = [pltpu.VMEM, pltpu.VMEM]
        self.scratch = [pltpu.VMEM((HD, width), jnp.float32)]

    def tile(self, k, rows_ref):
        (out_rows, attended), (grad, _), (total,) = self.src, self.dst, self.more
        rows = pl.ds(k * self.pair, self.pair)
        value = rows_ref[...]
        grad[rows] = contract_last(value, out_rows[...]).astype(jnp.bfloat16)
        for start in range(0, self.width, 512):
            columns = pl.ds(start, 512)
            term = contract_first(attended[rows], rows_ref[:, columns])
            total[:, columns] = term if k == 0 else total[:, columns] + term

    def close(self):
        self.dst[1][...] = self.more[0][...].astype(jnp.bfloat16)


GATHER_STAGES = (0, 1, 2, 3)
NEAR = [("x",), ("zl",), ("y",), ("c",)]


def room_for(*held):
    sizes = [math.prod(s.shape) * jnp.dtype(s.dtype).itemsize for s in held]
    return sum(sizes) + 8 * MIB


def only_vmem(arrays, spaces):
    return [a for a, space in zip(arrays, spaces) if space == pltpu.VMEM]


def in_hbm(value, space):
    return pltpu.with_memory_space_constraint(value, pltpu.HBM) if space == pltpu.HBM else value


def call(body, name, ident, cargo, operands, spaces, outs, out_spaces, scratch):
    cargo_in = [space for load in cargo.loads for space in load.spaces()[0]]
    operands = [in_hbm(v, space) for v, space in zip(operands, spaces)]
    sources = [in_hbm(v, space) for v, space in zip(cargo.sources, cargo_in)]
    cargo_out = [space for load in cargo.loads for space in load.spaces()[1]]
    kept = [
        space(out.shape, out.dtype)
        for out, space in zip(list(outs) + cargo.outs, list(out_spaces) + cargo_out)
    ]
    held = only_vmem(operands, spaces) + only_vmem(outs, out_spaces)
    held += only_vmem(cargo.sources, cargo_in)
    held += [s for s in scratch + cargo.scratch if s.memory_space == pltpu.VMEM]
    return pl.pallas_call(
        functools.partial(body, cargo),
        out_shape=kept,
        in_specs=[pl.BlockSpec(memory_space=s) for s in spaces] + cargo.in_specs,
        out_specs=[pl.BlockSpec(memory_space=s) for s in out_spaces] + cargo.out_specs,
        scratch_shapes=scratch + cargo.scratch,
        compiler_params=pltpu.CompilerParams(
            collective_id=ident, has_side_effects=True, vmem_limit_bytes=room_for(*held)
        ),
        cost_estimate=pl.CostEstimate(flops=0, bytes_accessed=100 * MIB, transcendentals=0),
        name=name,
    )(*operands, *sources)


def take(refs, count):
    taken = refs[:count]
    del refs[:count]
    return taken


def gather_kernel(orders, work, eager, cargo, x_ref, *refs):
    refs = list(refs)
    work_in = take(refs, len(work.sources)) if work else []
    sources = take(refs, len(cargo.sources))
    work_out = take(refs, len(work.outs) if work else 1)
    targets = take(refs, len(cargo.outs))
    send_sem, recv_sem, core_send, core_recv, own_sem = take(refs, 5)
    here = place()
    spans = [pl.ds(r0, size) for _, r0, size in orders]
    orders = [o for o, _, _ in orders]
    pieces = range(len(orders))
    if work:
        (o_ref,) = take(refs, 1)
        work.bind(work_in, work_out, take(refs, len(work.scratch)))
        work.begin()
    else:
        o_ref = work_out[0]
    rows, width = x_ref.shape
    cargo.bind(here, sources, targets, refs)
    cargo.greet(here, NEAR)
    own = pltpu.make_async_copy(x_ref, spots(o_ref, slice(0, 1), rows), own_sem)

    def spot(p, *names):
        return spots(o_ref, slot(*names), rows, spans[p])

    def source(p, mask):
        return spot(p, *subset(orders[p], mask)) if mask else x_ref.at[spans[p]]

    def over(p, mask, k):
        whole = mask | 1 << k
        return pltpu.make_async_remote_copy(
            src_ref=source(p, mask), dst_ref=spot(p, *subset(orders[p], whole)),
            send_sem=send_sem.at[p, whole], recv_sem=recv_sem.at[p, whole],
            device_id=flip(here, orders[p][k]), device_id_type=MESH,
        )

    def across(p, mask):
        return pltpu.make_async_remote_copy(
            src_ref=source(p, mask), dst_ref=spot(p, "c", *subset(orders[p], mask)),
            send_sem=core_send.at[p, mask], recv_sem=core_recv.at[p, mask],
            device_id=flip(here, "c"), device_id_type=MESH,
        )

    sent = []

    def pass_on(mask):
        for p in pieces:
            if mask:
                landing = spot(p, *subset(orders[p], mask))
                pltpu.make_async_copy(landing, landing, recv_sem.at[p, mask]).wait()
            for k in range(mask.bit_length(), 3):
                sent.append(over(p, mask, k))
                sent[-1].start()
        for p in pieces:
            sent.append(across(p, mask))
            sent[-1].start()
        if mask == 0:
            own.start()
        if mask in GATHER_STAGES:
            cargo.start(GATHER_STAGES.index(mask))

    def from_core(*masks):
        for mask in masks:
            for p in pieces:
                landing = spot(p, "c", *subset(orders[p], mask))
                pltpu.make_async_copy(landing, landing, core_recv.at[p, mask]).wait()

    def tiles(*numbers):
        for k in numbers:
            work.tile(k, o_ref.at[pl.ds(2 * rows * k, 2 * rows)])

    if eager:
        pass_on(0)
        own.wait()
        from_core(0)
        tiles(0)
        for mask in (1, 2, 3, 4):
            pass_on(mask)
        from_core(1, 2, 4)
        tiles(1, 2)
        pass_on(5)
        tiles(3)
        pass_on(6)
        from_core(3, 5, 6)
        tiles(4)
        pass_on(7)
        tiles(5, 6)
        from_core(7)
        tiles(7)
    else:
        for mask in range(8):
            pass_on(mask)
        from_core(*range(8))
        own.wait()
        if work:
            tiles(*range(SIDES))
    for copy in sent:
        copy.wait_send()
    if work:
        work.close()
    cargo.finish()


def spots(ref, index, rows, span=None):
    if isinstance(index, slice):
        return ref.at[pl.ds(index.start * rows, rows)]
    if span is None:
        return ref.at[pl.ds(index * rows, rows)]
    return ref.at[pl.ds(index * rows + span.start, span.size)]


def gather_cube(block, ident, loads=(), orders=None, work=None, eager=False):
    rows, width = block.shape
    orders = orders or thirds(rows)
    whole = jax.ShapeDtypeStruct((MEMBERS * rows, width), block.dtype)
    scratch = [pltpu.SemaphoreType.DMA((len(orders), 8))] * 4 + [pltpu.SemaphoreType.DMA(())]
    if work:
        operands, spaces = [block] + work.sources, [pltpu.HBM] + work.in_spaces
        outs, out_spaces = work.outs, work.out_spaces
        scratch += [pltpu.VMEM(whole.shape, whole.dtype)] + work.scratch
    else:
        operands, spaces, outs, out_spaces = [block], [pltpu.HBM], [whole], [pltpu.HBM]
    return call(
        functools.partial(gather_kernel, orders, work, eager),
        "gather_cube", ident, Cargo(list(loads)), operands, spaces, outs, out_spaces, scratch,
    )


def scatter_kernel(orders, cargo, p_ref, *refs):
    n, m = len(cargo.sources), len(cargo.outs)
    sources, o_ref, targets = refs[:n], refs[n], refs[n + 1 : n + 1 + m]
    acc, rcore, came, core_send, core_recv, send_sem, recv_sem = refs[n + m + 1 : n + m + 8]
    here = place()
    spans = [pl.ds(r0, size) for _, r0, size in orders]
    orders = [o for o, _, _ in orders]
    pieces = range(len(orders))
    cargo.bind(here, sources, targets, refs[n + m + 8 :])
    cargo.greet(here, NEAR)

    def away(p, mask):
        return pltpu.make_async_remote_copy(
            src_ref=p_ref.at[slot("c", *subset(orders[p], mask)), spans[p]],
            dst_ref=rcore.at[mask, spans[p]],
            send_sem=core_send.at[p, mask], recv_sem=core_recv.at[p, mask],
            device_id=flip(here, "c"), device_id_type=MESH,
        )

    sequence = [7, 3, 5, 1, 6, 2, 4, 0]
    sent = []
    for mask in sequence:
        for p in pieces:
            sent.append(away(p, mask))
            sent[-1].start()
    cargo.start(0)

    def over(p, mask):
        k = (mask & -mask).bit_length() - 1
        return pltpu.make_async_remote_copy(
            src_ref=acc.at[mask, spans[p]], dst_ref=came.at[mask, spans[p]],
            send_sem=send_sem.at[p, mask], recv_sem=recv_sem.at[p, mask],
            device_id=flip(here, orders[p][k]), device_id_type=MESH,
        )

    for mask in sequence:
        for p in pieces:
            away(p, mask).wait_recv()
            own = slot(*subset(orders[p], mask))
            acc[mask, spans[p]] = p_ref[own, spans[p]] + rcore[mask, spans[p]]
            if mask & 1:
                sent.append(over(p, mask))
                sent[-1].start()
    cargo.start(1)
    for k in range(3):
        low = 1 << k
        for mask in [b for b in (6, 2, 4, 0) if b & (2 * low - 1) == 0]:
            for p in pieces:
                over(p, mask | low).wait_recv()
                if mask == 0 and k == 2:
                    o_ref[spans[p]] = acc[0, spans[p]].astype(jnp.float32) + came[
                        4, spans[p]
                    ].astype(jnp.float32)
                    continue
                acc[mask, spans[p]] = acc[mask, spans[p]] + came[mask | low, spans[p]]
                if mask & (2 * low):
                    sent.append(over(p, mask))
                    sent[-1].start()
        if k < 2:
            cargo.start(2 + k)
        if k == 1:
            cargo.finish(early=True)
    for copy in sent:
        copy.wait_send()
    cargo.finish()


def scatter_cube(partial, ident, loads=(), orders=None):
    total, width = partial.shape
    rows = total // MEMBERS
    orders = orders or thirds(rows)
    return call(
        functools.partial(scatter_kernel, orders),
        "scatter_cube", ident, Cargo(list(loads)),
        [partial.astype(jnp.bfloat16).reshape(MEMBERS, rows, width)], [pltpu.VMEM],
        [jax.ShapeDtypeStruct((rows, width), jnp.float32)], [pltpu.VMEM],
        [pltpu.VMEM((8, rows, width), jnp.bfloat16)] * 3
        + [pltpu.SemaphoreType.DMA((len(orders), 8))] * 4,
    )


def exchange_kernel(v_ref, o_ref, slots, send_sem, recv_sem):
    here = place()
    greet([flip(here, *names) for names in PEERS])
    copies = []
    for names in PEERS:
        k = slot(*names)
        copies.append(pltpu.make_async_remote_copy(
            src_ref=v_ref, dst_ref=slots.at[k], send_sem=send_sem.at[k], recv_sem=recv_sem.at[k],
            device_id=flip(here, *names), device_id_type=MESH,
        ))
        copies[-1].start()
    for copy in copies:
        copy.wait_recv()
    slots[0] = v_ref[...]
    for row in range(v_ref.shape[0]):
        kind, mine = divmod(row, MEMBERS)
        terms = [
            slots[k, pl.ds(kind * MEMBERS + SLOT[SLOTS[mine] ^ SLOTS[k]], 1), :]
            for k in range(MEMBERS)
        ]
        while len(terms) > 1:
            terms = [terms[2 * i] + terms[2 * i + 1] for i in range(len(terms) // 2)]
        o_ref[pl.ds(row, 1), :] = terms[0]
    for copy in copies:
        copy.wait_send()


def sum_cube(values, ident):
    shape = values.shape
    return pl.pallas_call(
        exchange_kernel,
        out_shape=jax.ShapeDtypeStruct(shape, jnp.float32),
        in_specs=[pl.BlockSpec(memory_space=pltpu.VMEM)],
        out_specs=pl.BlockSpec(memory_space=pltpu.VMEM),
        scratch_shapes=[
            pltpu.VMEM((MEMBERS,) + shape, jnp.float32),
            pltpu.SemaphoreType.DMA((MEMBERS,)),
            pltpu.SemaphoreType.DMA((MEMBERS,)),
        ],
        compiler_params=pltpu.CompilerParams(collective_id=ident, has_side_effects=True),
        cost_estimate=pl.CostEstimate(flops=0, bytes_accessed=20 * MIB, transcendentals=0),
        name="sum_cube",
    )(values)


def rope_tables(positions):
    frequency = theta_base ** (-2.0 * jnp.arange(HD // 2).astype(jnp.float32) / HD)
    angles = positions[:, None] * frequency[None, :]
    return (jnp.cos(angles), jnp.sin(angles))


def rotate(values, cos_table, sin_table):
    half_width = values.shape[-1] // 2
    former = values[..., :half_width]
    latter = values[..., half_width:]
    return jnp.concatenate(
        [former * cos_table - latter * sin_table, latter * cos_table + former * sin_table], axis=-1
    )


def normalize(values, scales):
    inverse = lax.rsqrt(jnp.mean(values * values, axis=-1, keepdims=True) + epsilon)
    return (values * inverse * scales, inverse)


def norm_back(upstream, values, inverse, scales):
    unit_rows = values * inverse
    scaled = upstream * scales
    value_grad = inverse * (
        scaled - unit_rows * jnp.mean(scaled * unit_rows, axis=-1, keepdims=True)
    )
    return (value_grad, jnp.sum(upstream * unit_rows, axis=0))


def contract_last(operand, matrix):
    return lax.dot_general(
        operand, matrix, (((1,), (1,)), ((), ())), preferred_element_type=jnp.float32
    )


def contract_first(operand, matrix):
    return lax.dot_general(
        operand, matrix, (((0,), (0,)), ((), ())), preferred_element_type=jnp.float32
    )


def row_sums(pair, ident):
    total = pair[0].shape[0]
    flat = jnp.concatenate([v.reshape(MEMBERS, total // MEMBERS) for v in pair], axis=0)
    summed = sum_cube(flat, ident).reshape(2, total, 1)
    return summed[0], summed[1]


def finish_kernel(parts, *refs):
    *halves_refs, o_ref = refs
    own = pl.program_id(1) == lax.axis_index("x")
    for part in range(parts):

        @pl.when(pl.program_id(0) == part)
        def _(mine_ref=halves_refs[2 * part], came_ref=halves_refs[2 * part + 1]):
            o_ref[...] = jnp.where(own, mine_ref[...], came_ref[...]).astype(jnp.float32)


def whole_rows(*pairs):
    rows, width = pairs[0][0].shape
    parts = len(pairs)
    step = min(2048, width)
    steps = width // step

    def half(part):
        return pl.BlockSpec(
            (rows, step), lambda p, x, k, part=part: (0, jnp.where(p == part, k, 0))
        )

    return pl.pallas_call(
        functools.partial(finish_kernel, parts),
        grid=(parts, 2, steps),
        out_shape=jax.ShapeDtypeStruct((rows, 2 * parts * width), jnp.float32),
        in_specs=[half(part) for part in range(parts) for _ in range(2)],
        out_specs=pl.BlockSpec((rows, step), lambda p, x, k: (0, (2 * p + x) * steps + k)),
        compiler_params=pltpu.CompilerParams(vmem_limit_bytes=32 * MIB),
        cost_estimate=pl.CostEstimate(
            flops=0, bytes_accessed=12 * parts * rows * width, transcendentals=0
        ),
        name="whole_rows",
    )(*[half for pair in pairs for half in pair])


def owners_product(left, right, parts=1, columns=None, **options):
    if left.shape[1] // (lax.axis_size("zh") * SIDES) % 128 == 0:
        return Product(left, right, parts, columns=columns, **options)
    if columns is not None:
        right = right[:, columns[0] : sum(columns)]
    return Owners(contract_first(left, right).astype(jnp.bfloat16), parts, **options)


def heads_are_owners(rows):
    return lax.axis_size("zh") == 2 and rows == HD


def gathered_head_rows(weight):
    full = lax.all_gather(weight, OWNERS, axis=0, tiled=True)
    head = lax.axis_index(("x", "zl", "y", "c"))
    return lax.dynamic_slice_in_dim(full, head * HD, HD, axis=0)


def summed_head_rows(grad_rows, rows):
    head = lax.axis_index(("x", "zl", "y", "c"))
    full = jnp.zeros((MEMBERS * HD, grad_rows.shape[1]), jnp.float32)
    full = lax.dynamic_update_slice_in_dim(full, grad_rows, head * HD, axis=0)
    full = lax.psum(full, EVERY)
    return lax.dynamic_slice_in_dim(full, lax.axis_index(OWNERS) * rows, rows, axis=0)


def silu_grads(hidden_grad, gate_part, up_part):
    sigmoid_gate = jax.nn.sigmoid(gate_part)
    gate_grad = hidden_grad * up_part * sigmoid_gate * (1.0 + gate_part * (1.0 - sigmoid_gate))
    up_grad = hidden_grad * gate_part * sigmoid_gate
    return gate_grad.astype(jnp.bfloat16), up_grad.astype(jnp.bfloat16)


def shards(tokens, w_qkv, w_out, w_gate_up, w_down_t, gains, starts, cotangent):
    count_rows, width = tokens.shape
    owned = gains.shape[0]
    groups = lax.axis_size("zh")
    total = MEMBERS * count_rows
    score_scale = 1.0 / math.sqrt(HD)
    direct = heads_are_owners(owned)
    local_rows = jnp.arange(count_rows, dtype=jnp.int32)
    seq_begin = lax.cummax(jnp.where(starts == 1, local_rows, 0), axis=0)

    gain_part = jnp.pad(gains.astype(jnp.float32).T, ((0, 4), (0, 0)))
    begin_part = jnp.broadcast_to(seq_begin.astype(jnp.float32)[None, :], (8, count_rows))
    loads = [Few(gain_part, False), Few(begin_part, True), Columns(w_qkv, 3)]
    if direct:
        loads.append(Whole(w_out, "zh"))
    tokens_all, gain_all, begin_all, qkv_cols, *out_other = gather_cube(
        tokens, 1, loads, halves(count_rows, "zl", "y", "x")
    )
    same = lax.axis_index("x") == lax.axis_index("zh")
    if direct:
        out_rows = jnp.where(same, w_out, out_other[0])
    else:
        out_rows = gathered_head_rows(w_out)
    gain_rows = gain_all[:, :4].transpose(1, 0, 2).reshape(4, width)
    begin_all = begin_all[:, 0]
    head = lax.axis_index(("x", "zl", "y", "c"))
    head_gains = lax.dynamic_slice_in_dim(gain_rows, head * HD, HD, axis=1)
    rows_f32 = local_rows.astype(jnp.float32)
    positions = (rows_f32[None, :] - begin_all).reshape(total)
    cos_table, sin_table = rope_tables(positions)
    allowed = (rows_f32[None, None, :] <= rows_f32[None, :, None]) & (
        rows_f32[None, None, :] >= begin_all[:, :, None]
    )

    def blocks(values):
        return values.reshape(MEMBERS, count_rows, HD)

    projected = jnp.dot(tokens_all, qkv_cols, preferred_element_type=jnp.float32)
    query_raw = projected[:, :HD]
    key_raw = projected[:, HD : 2 * HD]
    value_bf = blocks(projected[:, 2 * HD :].astype(jnp.bfloat16))
    query_sq, key_sq = row_sums(
        (jnp.sum(query_raw * query_raw, axis=1), jnp.sum(key_raw * key_raw, axis=1)), 2
    )
    query_inv = lax.rsqrt(query_sq / width + epsilon)
    key_inv = lax.rsqrt(key_sq / width + epsilon)
    query_unit = query_raw * query_inv
    key_unit = key_raw * key_inv
    query_bf = blocks(rotate(query_unit * head_gains[0], cos_table, sin_table).astype(jnp.bfloat16))
    key_bf = blocks(rotate(key_unit * head_gains[1], cos_table, sin_table).astype(jnp.bfloat16))
    scores = (
        jnp.einsum("bqd,bkd->bqk", query_bf, key_bf, preferred_element_type=jnp.float32)
        * score_scale
    )
    scores = jnp.where(allowed, scores, -1e30)
    exponent = jnp.exp(scores - jnp.max(scores, axis=-1, keepdims=True))
    attention_f32 = exponent / jnp.sum(exponent, axis=-1, keepdims=True)
    attention = attention_f32.astype(jnp.bfloat16)
    attended = (
        jnp.einsum("bqk,bkd->bqd", attention, value_bf, preferred_element_type=jnp.float32)
        .reshape(total, HD)
        .astype(jnp.bfloat16)
    )
    x_most = halves(count_rows, "x", "y", "zl")
    x_last = halves(count_rows, "zl", "y", "x")
    z_first = (
        (("zl", "x", "y"), 0, count_rows // 2),
        (("zl", "y", "x"), count_rows // 2, count_rows // 2),
    )
    branch, gate_up_cols = scatter_cube(
        jnp.dot(attended, out_rows, preferred_element_type=jnp.float32),
        3, [Columns(w_gate_up, 2, near=1)], x_most,
    )
    branch_norm, branch_inv = normalize(branch, gain_rows[2])
    middle = tokens.astype(jnp.float32) + branch_norm
    hidden_bf, gate_up, middle_all, down_cols = gather_cube(
        middle.astype(jnp.bfloat16), 4, [Columns(w_down_t, far=1, near=3)], x_last,
        FeedForward(gate_up_cols, total), eager=True,
    )
    (feed_out,) = scatter_cube(contract_last(hidden_bf, down_cols), 5)
    feed_norm, feed_inv = normalize(feed_out, gain_rows[3])
    mixed = (middle + feed_norm).astype(jnp.bfloat16)

    upstream = cotangent.astype(jnp.float32)
    feed_grad, gain_feed = norm_back(upstream, feed_out, feed_inv, gain_rows[3])
    gate_up_bf, middle_part, feed_all = gather_cube(
        feed_grad.astype(jnp.bfloat16), 6, work=FeedBack(down_cols, gate_up_cols, gate_up),
        eager=True,
    )
    feed_width = hidden_bf.shape[1]
    middle_sum, gate_sum, gate_other, up_sum = scatter_cube(
        middle_part, 7,
        [
            owners_product(
                middle_all, gate_up_bf, columns=(0, feed_width), near=1, swap=True, early=True
            ),
            owners_product(
                middle_all, gate_up_bf, columns=(feed_width, feed_width), far=1, near=2
            ),
        ], x_most,
    )
    middle_grad = upstream + middle_sum
    branch_grad, gain_branch = norm_back(middle_grad, branch, branch_inv, gain_rows[2])
    attended_grad, out_grad, down_sum, up_other = gather_cube(
        branch_grad.astype(jnp.bfloat16), 8,
        [
            owners_product(feed_all, hidden_bf, far=1, near=3),
            Whole(up_sum, "x", near=3),
        ], z_first, BranchBack(out_rows, attended),
    )
    attended_grad = blocks(attended_grad)
    down_other = lax.ppermute(down_sum, "x", [(0, 1), (1, 0)])
    prob_grad = jnp.einsum(
        "bqd,bkd->bqk", attended_grad, value_bf, preferred_element_type=jnp.float32
    )
    score_bf = (
        attention_f32 * (prob_grad - jnp.sum(attention_f32 * prob_grad, axis=-1, keepdims=True))
    ).astype(jnp.bfloat16)
    value_grad = jnp.einsum(
        "bqk,bqd->bkd", attention, attended_grad, preferred_element_type=jnp.float32
    ).reshape(total, HD)
    query_grad = (
        jnp.einsum("bqk,bkd->bqd", score_bf, key_bf, preferred_element_type=jnp.float32)
        * score_scale
    ).reshape(total, HD)
    key_grad = (
        jnp.einsum("bqk,bqd->bkd", score_bf, query_bf, preferred_element_type=jnp.float32)
        * score_scale
    ).reshape(total, HD)
    query_grad = rotate(query_grad, cos_table, -sin_table)
    key_grad = rotate(key_grad, cos_table, -sin_table)
    query_scaled = query_grad * head_gains[0]
    key_scaled = key_grad * head_gains[1]
    query_dot, key_dot = row_sums(
        (jnp.sum(query_scaled * query_unit, axis=1), jnp.sum(key_scaled * key_unit, axis=1)), 9
    )
    query_raw_grad = query_inv * (query_scaled - query_unit * (query_dot / width))
    key_raw_grad = key_inv * (key_scaled - key_unit * (key_dot / width))
    projected_bf = jnp.concatenate([query_raw_grad, key_raw_grad, value_grad], axis=1).astype(
        jnp.bfloat16
    )

    gain_head = jnp.stack(
        [jnp.sum(query_grad * query_unit, axis=0), jnp.sum(key_grad * key_unit, axis=0)]
    )
    gain_terms = jnp.concatenate(
        [
            lax.dynamic_update_slice_in_dim(
                jnp.zeros((2, width), jnp.float32), gain_head, head * HD, axis=1
            ),
            jnp.stack([gain_branch, gain_feed]),
        ]
    )
    lanes = -(-owned // 128) * 128
    gain_terms = jnp.pad(
        gain_terms.reshape(4, groups * SIDES, owned).transpose(1, 0, 2),
        ((0, 0), (0, 4), (0, lanes - owned)),
    ).reshape(groups * SIDES * 8, lanes)
    loads = [
        owners_product(tokens_all, projected_bf, 3, swap=True, near=1, early=True),
        Owners(gain_terms, swap=True, fold=True, early=True),
    ]
    if direct:
        loads.append(Pair(out_grad, early=True))
    tokens_sum, qkv_sum, qkv_other, gain_sum, gain_other, *out_both = scatter_cube(
        contract_last(projected_bf, qkv_cols), 10, loads, x_most
    )
    grad_tokens = middle_grad + tokens_sum
    if direct:
        grad_out = jnp.where(same, out_both[0], out_both[1]).astype(jnp.float32)
    else:
        grad_out = summed_head_rows(out_grad.astype(jnp.float32), owned)
    third = width // 2
    grad_qkv = whole_rows(
        *[
            (qkv_sum[:, k * third : (k + 1) * third], qkv_other[:, k * third : (k + 1) * third])
            for k in range(3)
        ]
    )
    grad_gate_up = whole_rows((gate_sum, gate_other), (up_sum, up_other))
    grad_down_t = whole_rows((down_sum, down_other))
    grad_gains = (gain_sum + gain_other)[:4, :owned].T
    return (mixed, grad_tokens, grad_qkv, grad_out, grad_gate_up, grad_down_t, grad_gains)


def solution(mesh):
    sizes = dict(mesh.shape)
    groups = sizes["fsdp"] // SIDES
    finer = Mesh(mesh.devices.reshape(2, groups, 2, 2, 2), EVERY)
    return jax.shard_map(
        shards,
        mesh=finer,
        in_specs=(
            P(EVERY, None),
            P(OWNERS, None),
            P(OWNERS, None),
            P(OWNERS, None),
            P(OWNERS, None),
            P(OWNERS, None),
            P(EVERY),
            P(EVERY, None),
        ),
        out_specs=(
            P(EVERY, None),
            P(EVERY, None),
            P(OWNERS, None),
            P(OWNERS, None),
            P(OWNERS, None),
            P(OWNERS, None),
            P(OWNERS, None),
        ),
        check_vma=False,
    )
```

```python
import functools
import math

import jax
import jax.numpy as jnp
from jax import lax
from jax.experimental import pallas as pl
from jax.experimental.pallas import tpu as pltpu
from jax.sharding import Mesh, PartitionSpec as P

HD = 128

epsilon = 1e-06
theta_base = 500000.0

OWNERS = ("zh", "zl", "y", "c")
EVERY = ("x", "zh", "zl", "y", "c")
MEMBERS = 16
SIDES = 8
SIDE_BITS = {"zl": 4, "y": 2, "c": 1}
BITS = {"x": 8, "zl": 4, "y": 2, "c": 1}
SLOTS = [
    frozenset(names + core)
    for names in (
        (), ("x",), ("y",), ("zl",), ("x", "y"), ("x", "zl"), ("y", "zl"), ("x", "y", "zl"),
    )
    for core in ((), ("c",))
]
SLOT = {names: k for k, names in enumerate(SLOTS)}
MESH = pl.DeviceIdType.MESH
MIB = 1 << 20


def thirds(rows):
    unit = rows // 8
    return (
        (("x", "y", "zl"), 0, 3 * unit),
        (("y", "zl", "x"), 3 * unit, 3 * unit),
        (("zl", "x", "y"), 6 * unit, 2 * unit),
    )


def halves(rows, *order):
    return ((order, 0, rows // 2), (order, rows // 2, rows // 2))


PEERS = [tuple(n for n in BITS if m & BITS[n]) for m in range(1, MEMBERS)]
SIDE_PEERS = [tuple(n for n in SIDE_BITS if m & SIDE_BITS[n]) for m in range(SIDES)]


def slot(*names):
    return SLOT[frozenset(names)]


def place():
    return {name: lax.axis_index(name) for name in EVERY}


def flip(here, *names):
    return {name: 1 - here[name] for name in names}


def with_bits(here, names, bits):
    index = 0
    for name, bit in bits.items():
        index = index + bit * ((1 - here[name]) if name in names else here[name])
    return index


def subset(order, mask):
    return tuple(name for k, name in enumerate(order) if mask >> k & 1)


def greet(devices):
    barrier = pltpu.get_barrier_semaphore()
    for device in devices:
        pl.semaphore_signal(barrier, inc=1, device_id=device, device_id_type=MESH)
    pl.semaphore_wait(barrier, len(devices))


def owner_at(here, groups, step, names):
    device = flip(here, *names)
    if step:
        device["zh"] = lax.rem(here["zh"] + step, groups)
    return device


def at(start, size):
    return pl.ds(pl.multiple_of(start, size), size)


class Load:
    space = pltpu.HBM
    parts = 1

    def __init__(self, source, far=0, near=0, early=False):
        self.sources = [source]
        self.stages = (near, far)
        self.early = early
        self.groups = lax.axis_size("zh")

    def spaces(self):
        return [self.space] * len(self.sources), [self.space] * len(self.outs)

    def semaphores(self):
        count = len(self.moves())
        return [pltpu.SemaphoreType.DMA((count,)), pltpu.SemaphoreType.DMA((count,))]

    def scratch(self):
        return self.semaphores()

    def moves(self):
        return [
            ((step, names), part)
            for step in range(self.groups)
            for names in SIDE_PEERS
            for part in range(self.parts)
        ]

    def reached(self):
        return {peer for peer, _ in self.moves() if peer != (0, ())}

    def around(self, here, step, names):
        there = lax.rem(here["zh"] + step, self.groups)
        whence = lax.rem(here["zh"] + self.groups - step, self.groups)
        mine, other = with_bits(here, (), SIDE_BITS), with_bits(here, names, SIDE_BITS)
        return mine, other, there, whence

    def bind(self, here, sources, targets, scratch):
        self.here, self.src, self.dst = here, sources, targets
        self.send, self.recv, *self.more = scratch
        self.copies = []
        for index, ((step, names), part) in enumerate(self.moves()):
            source, target, landing = self.views(here, step, names, part)
            stage = self.stages[1 if step else 0]
            if not step and not names:
                copy = pltpu.make_async_copy(source, target, self.send.at[index])
                self.copies.append((stage, copy, None, (step, names)))
                continue
            copy = pltpu.make_async_remote_copy(
                src_ref=source, dst_ref=target,
                send_sem=self.send.at[index], recv_sem=self.recv.at[index],
                device_id=owner_at(here, self.groups, step, names), device_id_type=MESH,
            )
            landed = pltpu.make_async_copy(landing, landing, self.recv.at[index])
            self.copies.append((stage, copy, landed, (step, names)))

    def start(self, stage):
        for when, copy, _, _ in self.copies:
            if when == stage:
                copy.start()

    def land(self):
        for _, copy, landed, _ in self.copies:
            (copy if landed is None else landed).wait()

    def finish(self):
        pass

    def leave(self):
        for _, copy, landed, _ in self.copies:
            if landed is not None:
                copy.wait_send()


class Columns(Load):
    def __init__(self, source, parts=1, **stages):
        super().__init__(source, **stages)
        self.parts = parts
        self.rows = source.shape[0]
        self.piece = source.shape[1] // (parts * MEMBERS)
        shape = (self.groups * SIDES * self.rows, parts * self.piece)
        self.outs = [jax.ShapeDtypeStruct(shape, source.dtype)]

    def views(self, here, step, names, part):
        mine, other, _, whence = self.around(here, step, names)
        first = part * MEMBERS + here["x"] * SIDES + other
        columns = pl.ds(part * self.piece, self.piece)
        return (
            self.src[0].at[:, at(first * self.piece, self.piece)],
            self.dst[0].at[at((here["zh"] * SIDES + mine) * self.rows, self.rows), columns],
            self.dst[0].at[at((whence * SIDES + other) * self.rows, self.rows), columns],
        )


class Few(Load):
    space = pltpu.VMEM

    def __init__(self, source, cube):
        super().__init__(source)
        self.cube = cube
        count = MEMBERS if cube else self.groups * SIDES
        self.outs = [jax.ShapeDtypeStruct((count,) + source.shape, source.dtype)]

    def moves(self):
        if self.cube:
            return [((0, names), 0) for names in [()] + PEERS]
        return super().moves()

    def views(self, here, step, names, part):
        if self.cube:
            spot = self.dst[0].at[slot(*names)]
            return self.src[0], spot, spot
        mine, other, _, whence = self.around(here, step, names)
        return (
            self.src[0],
            self.dst[0].at[here["zh"] * SIDES + mine],
            self.dst[0].at[whence * SIDES + other],
        )


class Whole(Load):
    def __init__(self, source, axis, **stages):
        super().__init__(source, **stages)
        self.axis = axis
        self.outs = [jax.ShapeDtypeStruct(source.shape, source.dtype)]

    def moves(self):
        return [((0, ("x",)) if self.axis == "x" else (1, ()), 0)]

    def views(self, here, step, names, part):
        return self.src[0], self.dst[0], self.dst[0]


class Swap:
    def swap_scratch(self):
        return [pltpu.SemaphoreType.DMA((3,))]

    def give(self, total, sems):
        self.kept = pltpu.make_async_copy(total, self.dst[0], sems.at[0])
        self.kept.start()
        self.given = None
        if len(self.outs) > 1:
            self.given = pltpu.make_async_remote_copy(
                src_ref=total, dst_ref=self.dst[1], send_sem=sems.at[1], recv_sem=sems.at[2],
                device_id=flip(self.here, "x"), device_id_type=MESH,
            )
            self.given.start()

    def given_wait(self):
        self.kept.wait()
        if self.given is not None:
            self.given.wait()


class Owners(Load, Swap):
    def __init__(self, source, parts=1, swap=False, fold=False, **stages):
        super().__init__(source, **stages)
        self.setup(source.shape[0], source.shape[1], source.dtype, parts, swap, fold)

    def setup(self, depth, width, kind, parts, swap, fold):
        self.parts = parts
        self.fold = fold
        self.kind = kind
        self.rows = depth // (self.groups * SIDES)
        self.piece = width // parts
        self.wide = parts * SIDES * self.piece
        total = (self.rows, self.piece if fold else self.wide)
        self.total = total
        self.outs = [jax.ShapeDtypeStruct(total, kind)] * (1 + swap)
        self.swap = swap

    def reached(self):
        return super().reached() | ({(0, ("x",))} if self.swap else set())

    def spaces(self):
        return [pltpu.VMEM if self.fold else pltpu.HBM] * len(self.sources), [pltpu.HBM] * len(self.outs)

    def scratch(self):
        return self.semaphores() + self.swap_scratch() + [
            pltpu.VMEM((self.groups, self.rows, self.wide), self.kind),
            pltpu.VMEM(self.total, self.kind),
        ]

    def views(self, here, step, names, part):
        mine, other, there, whence = self.around(here, step, names)
        terms = self.more[1]
        return (
            self.slice_of(there * SIDES + other, part),
            terms.at[here["zh"], :, at((part * SIDES + mine) * self.piece, self.piece)],
            terms.at[whence, :, at((part * SIDES + other) * self.piece, self.piece)],
        )

    def slice_of(self, target, part):
        return self.src[0].at[
            at(target * self.rows, self.rows), pl.ds(part * self.piece, self.piece)
        ]

    def finish(self):
        sems, terms, total = self.more[:3]
        step = self.piece if self.fold else min(512, self.wide)

        def add(start):
            value = terms[0, :, pl.ds(start, step)].astype(jnp.float32)
            for group in range(1, self.groups):
                value = value + terms[group, :, pl.ds(start, step)].astype(jnp.float32)
            return value

        if self.fold:
            value = add(0)
            for side in range(1, SIDES):
                value = value + add(side * step)
            total[...] = value
        else:

            @pl.loop(0, self.wide // step)
            def _(k):
                start = pl.multiple_of(k * step, step)
                total[:, pl.ds(start, step)] = add(start).astype(total.dtype)

        self.give(total, sems)

    def leave(self):
        super().leave()
        self.given_wait()


class Product(Owners):
    def __init__(self, left, right, parts=1, swap=False, columns=None, **stages):
        Load.__init__(self, left, **stages)
        self.sources = [left, right]
        self.columns = columns or (0, right.shape[1])
        self.setup(left.shape[1], self.columns[1], jnp.bfloat16, parts, swap, False)

    def scratch(self):
        depth, width = self.sources[0].shape[0], self.columns[1]
        return super().scratch() + [
            pltpu.VMEM((2, depth, 2 * self.rows), jnp.bfloat16),
            pltpu.VMEM((depth, width), jnp.bfloat16),
            pltpu.VMEM((self.groups * SIDES * self.rows, width), jnp.bfloat16),
            pltpu.SemaphoreType.DMA((3,)),
        ]

    def slice_of(self, target, part):
        return self.more[5].at[
            at(target * self.rows, self.rows), pl.ds(part * self.piece, self.piece)
        ]

    def tiles(self):
        order = [
            (step, names)
            for step in reversed(range(self.groups))
            for names in SIDE_PEERS
            if "c" not in names
        ]
        return order

    def first_row(self, step, names):
        _, other, there, _ = self.around(self.here, step, names)
        return (there * SIDES + (other // 2) * 2) * self.rows

    def fetch(self, k):
        step, names = self.tiles()[k]
        left = self.src[0].at[:, at(self.first_row(step, names), 2 * self.rows)]
        return pltpu.make_async_copy(left, self.more[3].at[k % 2], self.more[6].at[k % 2])

    def begin(self):
        right = self.src[1].at[:, pl.ds(*self.columns)]
        self.right = pltpu.make_async_copy(right, self.more[4], self.more[6].at[2])
        self.right.start()
        self.fetch(0).start()
        self.fetch(1).start()

    def start(self, stage):
        tiles = self.tiles()
        _, _, _, lefts, right, result, _ = self.more
        for k, (step, names) in enumerate(tiles):
            if self.stages[1 if step else 0] != stage:
                continue
            if k == 0:
                self.right.wait()
            self.fetch(k).wait()
            rows = at(self.first_row(step, names), 2 * self.rows)
            width = self.columns[1]
            left = lefts[k % 2]
            for column in range(0, width, 256):
                columns = pl.ds(column, min(256, width - column))
                result[rows, columns] = lax.dot_general(
                    left, right[:, columns], (((0,), (0,)), ((), ())),
                    preferred_element_type=jnp.float32,
                ).astype(jnp.bfloat16)
            if k + 2 < len(tiles):
                self.fetch(k + 2).start()
            for _, copy, _, peer in self.copies:
                if peer in ((step, names), (step, names + ("c",))):
                    copy.start()


class HeadRows(Load):
    def __init__(self, source):
        super().__init__(source)
        self.outs = [jax.ShapeDtypeStruct(source.shape, source.dtype)]

    def moves(self):
        return [((1, ()), 0), ((1, ("x",)), 0)]

    def bind(self, here, sources, targets, scratch):
        (source,), (target,), (send, recv) = sources, targets, scratch
        half = source.shape[0] // 2
        self.home = here["x"] == here["zh"]
        mine = jnp.where(self.home, 0, 1)
        rows = at(mine * half, half)
        self.copy = pltpu.make_async_remote_copy(
            src_ref=source.at[rows], dst_ref=target.at[rows],
            send_sem=send.at[0], recv_sem=recv.at[mine],
            device_id={"x": here["zh"], "zh": 1 - here["zh"]}, device_id_type=MESH,
        )
        spots_here = [target.at[pl.ds(k * half, half)] for k in range(2)]
        self.landed = [
            pltpu.make_async_copy(spot, spot, recv.at[k]) for k, spot in enumerate(spots_here)
        ]

    def start(self, stage):
        if stage == 0:
            self.copy.start()

    def land(self):
        @pl.when(jnp.logical_not(self.home))
        def _():
            for landed in self.landed:
                landed.wait()

    def leave(self):
        self.copy.wait_send()


class FinalRows(Load):
    def __init__(self, *pairs, near=4):
        super().__init__(None, near=near)
        self.sources = [half for pair in pairs for half in pair]
        rows, self.width = pairs[0][0].shape
        self.step = min(2048, self.width)
        self.outs = [jax.ShapeDtypeStruct((rows, len(self.sources) * self.width), jnp.float32)]

    def moves(self):
        return []

    def scratch(self):
        rows = self.outs[0].shape[0]
        return [
            pltpu.VMEM((2, rows, self.step), jnp.bfloat16),
            pltpu.VMEM((2, rows, self.step), jnp.float32),
            pltpu.SemaphoreType.DMA((4,)),
        ]

    def bind(self, here, sources, targets, scratch):
        self.here, self.src, self.dst = here, sources, targets
        self.halves, self.wholes, self.sems = scratch

    def start(self, stage):
        if stage != self.stages[0]:
            return
        x = self.here["x"]
        steps = [
            (k, start) for k in range(len(self.sources)) for start in range(0, self.width, self.step)
        ]

        def fetch(n):
            k, start = steps[n]
            return pltpu.make_async_copy(
                self.src[k].at[:, pl.ds(start, self.step)], self.halves.at[n % 2],
                self.sems.at[n % 2],
            )

        def store(n):
            k, start = steps[n]
            half = x if k % 2 == 0 else 1 - x
            first = (2 * (k // 2) + half) * self.width + start
            return pltpu.make_async_copy(
                self.wholes.at[n % 2], self.dst[0].at[:, at(first, self.step)],
                self.sems.at[2 + n % 2],
            )

        fetch(0).start()
        for n in range(len(steps)):
            if n + 1 < len(steps):
                fetch(n + 1).start()
            fetch(n).wait()
            if n >= 2:
                store(n - 2).wait()
            self.wholes[n % 2] = self.halves[n % 2].astype(jnp.float32)
            store(n).start()
        for n in range(max(0, len(steps) - 2), len(steps)):
            store(n).wait()

    def land(self):
        pass

    def leave(self):
        pass


class Cargo:
    def __init__(self, loads):
        self.loads = loads
        self.sources = [s for load in loads for s in load.sources]
        self.outs = [o for load in loads for o in load.outs]
        self.in_specs = [pl.BlockSpec(memory_space=s) for load in loads for s in load.spaces()[0]]
        self.out_specs = [pl.BlockSpec(memory_space=s) for load in loads for s in load.spaces()[1]]
        self.scratch = [s for load in loads for s in load.scratch()]

    def bind(self, here, sources, targets, scratch):
        sources, targets, scratch = list(sources), list(targets), list(scratch)

        def take(refs, count):
            taken = refs[:count]
            del refs[:count]
            return taken

        for load in self.loads:
            load.bind(
                here,
                take(sources, len(load.sources)),
                take(targets, len(load.outs)),
                take(scratch, len(load.scratch())),
            )
            if hasattr(load, "begin"):
                load.begin()

    def greet(self, here, names):
        reached = {(0, n) for n in names}
        for load in self.loads:
            reached |= load.reached()
        groups = lax.axis_size("zh")
        greet([owner_at(here, groups, step, n) for step, n in sorted(reached)])

    def start(self, stage):
        for load in self.loads:
            load.start(stage)

    def finish(self, early=False):
        for load in self.loads:
            if load.early == early:
                load.land()
                load.finish()
        if not early:
            for load in self.loads:
                load.leave()


class Work:
    operands = ()

    def __init__(self, *sources):
        self.sources = list(sources)

    def bind(self, sources, targets, scratch):
        self.src, self.dst, self.more = list(sources), list(targets), list(scratch)
        self.copies = []

    def begin(self):
        pass

    def keep(self, copy):
        self.copies.append(copy)
        copy.start()

    def close(self):
        for copy in self.copies:
            copy.wait()


class FeedForward(Work):
    def __init__(self, gate_up_cols, total):
        super().__init__(gate_up_cols)
        width, both = gate_up_cols.shape
        self.half, self.pair = both // 2, 2 * total // MEMBERS
        self.in_spaces = [pltpu.HBM]
        self.outs = [
            jax.ShapeDtypeStruct((total, self.half), jnp.bfloat16),
            jax.ShapeDtypeStruct((total, both), jnp.float32),
            jax.ShapeDtypeStruct((total, width), jnp.bfloat16),
        ]
        self.out_spaces = [pltpu.HBM, pltpu.HBM, pltpu.HBM]
        self.scratch = [
            pltpu.VMEM((2, self.pair, both), jnp.float32),
            pltpu.SemaphoreType.DMA((3, SIDES)),
            pltpu.VMEM(gate_up_cols.shape, gate_up_cols.dtype),
            pltpu.SemaphoreType.DMA(()),
            pltpu.VMEM((total, self.half), jnp.bfloat16),
        ]

    def begin(self):
        self.load = pltpu.make_async_copy(self.src[0], self.more[2], self.more[3])
        self.load.start()

    def tile(self, k, rows_ref):
        (hidden_out, gate_up, rows_out), (staged, sems, cols, _, hidden) = self.dst, self.more
        if k == 0:
            self.load.wait()
        rows = pl.ds(k * self.pair, self.pair)
        self.keep(pltpu.make_async_copy(rows_ref, rows_out.at[rows], sems.at[0, k]))
        if k >= 2:
            self.last[k - 2].wait()
        value = rows_ref[...]
        for start in range(0, self.half, 256):
            columns = pl.ds(start, 256)
            others = pl.ds(self.half + start, 256)
            gate = jnp.dot(value, cols[:, columns], preferred_element_type=jnp.float32)
            up = jnp.dot(value, cols[:, others], preferred_element_type=jnp.float32)
            staged[k % 2, :, columns] = gate
            staged[k % 2, :, others] = up
            hidden[rows, columns] = (gate * jax.nn.sigmoid(gate) * up).astype(jnp.bfloat16)
        self.keep(pltpu.make_async_copy(hidden.at[rows], hidden_out.at[rows], sems.at[2, k]))
        copy = pltpu.make_async_copy(staged.at[k % 2], gate_up.at[rows], sems.at[1, k])
        copy.start()
        if k == 0:
            self.last = []
        self.last.append(copy)

    def close(self):
        super().close()
        for copy in self.last[-2:]:
            copy.wait()


class FeedBack(Work):
    def __init__(self, down_cols, gate_up_cols, gate_up):
        super().__init__(down_cols, gate_up_cols, gate_up)
        total, both = gate_up.shape
        width = down_cols.shape[0]
        self.half, self.width, self.pair = both // 2, width, 2 * total // MEMBERS
        self.in_spaces = [pltpu.HBM] * 3
        self.outs = [
            jax.ShapeDtypeStruct((total, both), jnp.bfloat16),
            jax.ShapeDtypeStruct((total, width), jnp.bfloat16),
            jax.ShapeDtypeStruct((total, width), jnp.bfloat16),
        ]
        self.out_spaces = [pltpu.HBM, pltpu.HBM, pltpu.HBM]
        self.scratch = [
            pltpu.VMEM((2, self.pair, both), jnp.float32),
            pltpu.SemaphoreType.DMA((4, SIDES)),
            pltpu.VMEM(down_cols.shape, down_cols.dtype),
            pltpu.VMEM(gate_up_cols.shape, gate_up_cols.dtype),
            pltpu.SemaphoreType.DMA((2,)),
            pltpu.VMEM((total, both), jnp.bfloat16),
            pltpu.VMEM((total, width), jnp.bfloat16),
        ]

    def fetch(self, k):
        rows = pl.ds(k * self.pair, self.pair)
        return pltpu.make_async_copy(
            self.src[2].at[rows], self.more[0].at[k % 2], self.more[1].at[0, k]
        )

    def begin(self):
        self.loads = [
            pltpu.make_async_copy(self.src[i], self.more[2 + i], self.more[4].at[i])
            for i in range(2)
        ]
        for copy in self.loads:
            copy.start()
        self.fetch(0).start()
        self.fetch(1).start()

    def tile(self, k, rows_ref):
        grads_out, part_out, rows_out = self.dst
        saved, sems, down, cols, _, grads, part = self.more
        if k == 0:
            for copy in self.loads:
                copy.wait()
        rows = pl.ds(k * self.pair, self.pair)
        self.keep(pltpu.make_async_copy(rows_ref, rows_out.at[rows], sems.at[1, k]))
        self.fetch(k).wait()
        value = rows_ref[...]
        for start in range(0, self.half, 256):
            columns = pl.ds(start, 256)
            others = pl.ds(self.half + start, 256)
            hidden_grad = jnp.dot(value, down[:, columns], preferred_element_type=jnp.float32)
            gate_bf, up_bf = silu_grads(
                hidden_grad, saved[k % 2, :, columns], saved[k % 2, :, others]
            )
            grads[rows, columns] = gate_bf
            grads[rows, others] = up_bf
        if k + 2 < SIDES:
            self.fetch(k + 2).start()
        self.keep(pltpu.make_async_copy(grads.at[rows], grads_out.at[rows], sems.at[2, k]))
        both = grads[rows]
        for start in range(0, self.width, 256):
            columns = pl.ds(start, 256)
            part[rows, columns] = contract_last(both, cols[columns, :]).astype(jnp.bfloat16)
        self.keep(pltpu.make_async_copy(part.at[rows], part_out.at[rows], sems.at[3, k]))


class BranchBack(Work):
    def __init__(self, out_rows, attended):
        super().__init__(out_rows, attended)
        total, width = attended.shape[0], out_rows.shape[1]
        self.width, self.pair = width, 2 * total // MEMBERS
        self.in_spaces = [pltpu.VMEM, pltpu.VMEM]
        self.outs = [
            jax.ShapeDtypeStruct((total, HD), jnp.bfloat16),
            jax.ShapeDtypeStruct((HD, width), jnp.bfloat16),
        ]
        self.out_spaces = [pltpu.VMEM, pltpu.VMEM]
        self.scratch = [pltpu.VMEM((HD, width), jnp.float32)]

    def tile(self, k, rows_ref):
        (out_rows, attended), (grad, _), (total,) = self.src, self.dst, self.more
        rows = pl.ds(k * self.pair, self.pair)
        value = rows_ref[...]
        grad[rows] = contract_last(value, out_rows[...]).astype(jnp.bfloat16)
        for start in range(0, self.width, 512):
            columns = pl.ds(start, 512)
            term = contract_first(attended[rows], rows_ref[:, columns])
            total[:, columns] = term if k == 0 else total[:, columns] + term

    def close(self):
        self.dst[1][...] = self.more[0][...].astype(jnp.bfloat16)


GATHER_STAGES = (0, 1, 2, 3)
NEAR = [("x",), ("zl",), ("y",), ("c",)]


def room_for(*held):
    sizes = [math.prod(s.shape) * jnp.dtype(s.dtype).itemsize for s in held]
    return sum(sizes) + 8 * MIB


def only_vmem(arrays, spaces):
    return [a for a, space in zip(arrays, spaces) if space == pltpu.VMEM]


def in_hbm(value, space):
    return pltpu.with_memory_space_constraint(value, pltpu.HBM) if space == pltpu.HBM else value


def call(body, name, ident, cargo, operands, spaces, outs, out_spaces, scratch):
    cargo_in = [space for load in cargo.loads for space in load.spaces()[0]]
    operands = [in_hbm(v, space) for v, space in zip(operands, spaces)]
    sources = [in_hbm(v, space) for v, space in zip(cargo.sources, cargo_in)]
    cargo_out = [space for load in cargo.loads for space in load.spaces()[1]]
    kept = [
        space(out.shape, out.dtype)
        for out, space in zip(list(outs) + cargo.outs, list(out_spaces) + cargo_out)
    ]
    held = only_vmem(operands, spaces) + only_vmem(outs, out_spaces)
    held += only_vmem(cargo.sources, cargo_in)
    held += [s for s in scratch + cargo.scratch if s.memory_space == pltpu.VMEM]
    return pl.pallas_call(
        functools.partial(body, cargo),
        out_shape=kept,
        in_specs=[pl.BlockSpec(memory_space=s) for s in spaces] + cargo.in_specs,
        out_specs=[pl.BlockSpec(memory_space=s) for s in out_spaces] + cargo.out_specs,
        scratch_shapes=scratch + cargo.scratch,
        compiler_params=pltpu.CompilerParams(
            collective_id=ident, has_side_effects=True, vmem_limit_bytes=room_for(*held)
        ),
        cost_estimate=pl.CostEstimate(flops=0, bytes_accessed=100 * MIB, transcendentals=0),
        name=name,
    )(*operands, *sources)


def take(refs, count):
    taken = refs[:count]
    del refs[:count]
    return taken


def gather_kernel(orders, work, eager, cargo, x_ref, *refs):
    refs = list(refs)
    work_in = take(refs, len(work.sources)) if work else []
    sources = take(refs, len(cargo.sources))
    work_out = take(refs, len(work.outs) if work else 1)
    targets = take(refs, len(cargo.outs))
    send_sem, recv_sem, core_send, core_recv, own_sem = take(refs, 5)
    here = place()
    spans = [pl.ds(r0, size) for _, r0, size in orders]
    orders = [o for o, _, _ in orders]
    pieces = range(len(orders))
    if work:
        (o_ref,) = take(refs, 1)
        work.bind(work_in, work_out, take(refs, len(work.scratch)))
        work.begin()
    else:
        o_ref = work_out[0]
    rows, width = x_ref.shape
    cargo.bind(here, sources, targets, refs)
    cargo.greet(here, NEAR)
    own = pltpu.make_async_copy(x_ref, spots(o_ref, slice(0, 1), rows), own_sem)

    def spot(p, *names):
        return spots(o_ref, slot(*names), rows, spans[p])

    def source(p, mask):
        return spot(p, *subset(orders[p], mask)) if mask else x_ref.at[spans[p]]

    def over(p, mask, k):
        whole = mask | 1 << k
        return pltpu.make_async_remote_copy(
            src_ref=source(p, mask), dst_ref=spot(p, *subset(orders[p], whole)),
            send_sem=send_sem.at[p, whole], recv_sem=recv_sem.at[p, whole],
            device_id=flip(here, orders[p][k]), device_id_type=MESH,
        )

    def across(p, mask):
        return pltpu.make_async_remote_copy(
            src_ref=source(p, mask), dst_ref=spot(p, "c", *subset(orders[p], mask)),
            send_sem=core_send.at[p, mask], recv_sem=core_recv.at[p, mask],
            device_id=flip(here, "c"), device_id_type=MESH,
        )

    sent = []

    def pass_on(mask):
        for p in pieces:
            if mask:
                landing = spot(p, *subset(orders[p], mask))
                pltpu.make_async_copy(landing, landing, recv_sem.at[p, mask]).wait()
            for k in range(mask.bit_length(), 3):
                sent.append(over(p, mask, k))
                sent[-1].start()
        for p in pieces:
            sent.append(across(p, mask))
            sent[-1].start()
        if mask == 0:
            own.start()
        if mask in GATHER_STAGES:
            cargo.start(GATHER_STAGES.index(mask))

    def from_core(*masks):
        for mask in masks:
            for p in pieces:
                landing = spot(p, "c", *subset(orders[p], mask))
                pltpu.make_async_copy(landing, landing, core_recv.at[p, mask]).wait()

    def tiles(*numbers):
        for k in numbers:
            work.tile(k, o_ref.at[pl.ds(2 * rows * k, 2 * rows)])

    if eager:
        pass_on(0)
        own.wait()
        from_core(0)
        tiles(0)
        for mask in (1, 2, 3, 4):
            pass_on(mask)
        from_core(1, 2, 4)
        tiles(1, 2)
        pass_on(5)
        tiles(3)
        pass_on(6)
        from_core(3, 5, 6)
        tiles(4)
        pass_on(7)
        tiles(5, 6)
        from_core(7)
        tiles(7)
    else:
        for mask in range(8):
            pass_on(mask)
        from_core(*range(8))
        own.wait()
        if work:
            tiles(*range(SIDES))
    for copy in sent:
        copy.wait_send()
    if work:
        work.close()
    cargo.finish()


def spots(ref, index, rows, span=None):
    if isinstance(index, slice):
        return ref.at[pl.ds(index.start * rows, rows)]
    if span is None:
        return ref.at[pl.ds(index * rows, rows)]
    return ref.at[pl.ds(index * rows + span.start, span.size)]


def gather_cube(block, ident, loads=(), orders=None, work=None, eager=False):
    rows, width = block.shape
    orders = orders or thirds(rows)
    whole = jax.ShapeDtypeStruct((MEMBERS * rows, width), block.dtype)
    scratch = [pltpu.SemaphoreType.DMA((len(orders), 8))] * 4 + [pltpu.SemaphoreType.DMA(())]
    if work:
        operands, spaces = [block] + work.sources, [pltpu.HBM] + work.in_spaces
        outs, out_spaces = work.outs, work.out_spaces
        scratch += [pltpu.VMEM(whole.shape, whole.dtype)] + work.scratch
    else:
        operands, spaces, outs, out_spaces = [block], [pltpu.HBM], [whole], [pltpu.HBM]
    return call(
        functools.partial(gather_kernel, orders, work, eager),
        "gather_cube", ident, Cargo(list(loads)), operands, spaces, outs, out_spaces, scratch,
    )


class Partial:
    def __init__(self, left, right, last=True):
        self.sources = [left, right]
        self.last = last
        self.pair = 2 * left.shape[0] // MEMBERS
        self.width = right.shape[0 if last else 1]
        self.scratch = [
            pltpu.VMEM(left.shape, left.dtype),
            pltpu.VMEM(right.shape, right.dtype),
            pltpu.SemaphoreType.DMA((2,)),
            pltpu.VMEM((left.shape[0], self.width), jnp.bfloat16),
        ]

    def begin(self, sources, scratch):
        self.left, self.right, sems, self.made = scratch
        self.loads = [
            pltpu.make_async_copy(source, held, sems.at[k])
            for k, (source, held) in enumerate(zip(sources, (self.left, self.right)))
        ]
        for copy in self.loads:
            copy.start()

    def wait(self):
        for copy in self.loads:
            copy.wait()

    def tile(self, k):
        rows = pl.ds(k * self.pair, self.pair)
        for start in range(0, self.width, 512):
            columns = pl.ds(start, 512)
            if self.last:
                value = contract_last(self.left[rows], self.right[columns, :])
            else:
                value = jnp.dot(
                    self.left[rows], self.right[:, columns], preferred_element_type=jnp.float32
                )
            self.made[rows, columns] = value.astype(jnp.bfloat16)


def scatter_kernel(orders, maker, cargo, *refs):
    refs = list(refs)
    heads = take(refs, len(maker.sources) if maker else 1)
    sources = take(refs, len(cargo.sources))
    (o_ref,) = take(refs, 1)
    targets = take(refs, len(cargo.outs))
    acc, rcore, came, core_send, core_recv, send_sem, recv_sem = take(refs, 7)
    here = place()
    rows = o_ref.shape[0]
    spans = [pl.ds(r0, size) for _, r0, size in orders]
    orders = [o for o, _, _ in orders]
    pieces = range(len(orders))
    if maker:
        maker.begin(heads, take(refs, len(maker.scratch)))
        p_ref = maker.made
    else:
        p_ref = heads[0]
        (load_sem,) = take(refs, 1)
    cargo.bind(here, sources, targets, refs)
    cargo.greet(here, NEAR)

    def away(p, mask):
        return pltpu.make_async_remote_copy(
            src_ref=spots(p_ref, slot("c", *subset(orders[p], mask)), rows, spans[p]),
            dst_ref=rcore.at[mask, spans[p]],
            send_sem=core_send.at[p, mask], recv_sem=core_recv.at[p, mask],
            device_id=flip(here, "c"), device_id_type=MESH,
        )

    def mine(p, mask):
        return spots(p_ref, slot(*subset(orders[p], mask)), rows, spans[p])

    def fetch(p, mask):
        return pltpu.make_async_copy(mine(p, mask), acc.at[mask, spans[p]], load_sem.at[p, mask])

    sent = []

    def hand_over(*masks):
        for mask in masks:
            for p in pieces:
                sent.append(away(p, mask))
                sent[-1].start()
                if not maker:
                    fetch(p, mask).start()

    sequence = [7, 3, 5, 1, 6, 2, 4, 0]
    if maker:
        cargo.start(0)
        maker.wait()
        for pairs, masks in (((7,), (7,)), ((4, 5, 6), (3, 5, 6)), ((1, 2, 3), (1, 2, 4)), ((0,), (0,))):
            for k in pairs:
                maker.tile(k)
            hand_over(*masks)
    else:
        hand_over(*sequence)
        cargo.start(0)

    def over(p, mask):
        k = (mask & -mask).bit_length() - 1
        return pltpu.make_async_remote_copy(
            src_ref=acc.at[mask, spans[p]], dst_ref=came.at[mask, spans[p]],
            send_sem=send_sem.at[p, mask], recv_sem=recv_sem.at[p, mask],
            device_id=flip(here, orders[p][k]), device_id_type=MESH,
        )

    for mask in sequence:
        for p in pieces:
            away(p, mask).wait_recv()
            if maker:
                acc[mask, spans[p]] = mine(p, mask)[...] + rcore[mask, spans[p]]
            else:
                fetch(p, mask).wait()
                acc[mask, spans[p]] = acc[mask, spans[p]] + rcore[mask, spans[p]]
            if mask & 1:
                sent.append(over(p, mask))
                sent[-1].start()
    cargo.start(1)
    for k in range(3):
        low = 1 << k
        for mask in [b for b in (6, 2, 4, 0) if b & (2 * low - 1) == 0]:
            for p in pieces:
                over(p, mask | low).wait_recv()
                if mask == 0 and k == 2:
                    o_ref[spans[p]] = acc[0, spans[p]].astype(jnp.float32) + came[
                        4, spans[p]
                    ].astype(jnp.float32)
                    continue
                acc[mask, spans[p]] = acc[mask, spans[p]] + came[mask | low, spans[p]]
                if mask & (2 * low):
                    sent.append(over(p, mask))
                    sent[-1].start()
        if k < 2:
            cargo.start(2 + k)
        if k == 1:
            cargo.finish(early=True)
            cargo.start(4)
    for copy in sent:
        copy.wait_send()
    cargo.finish()


def scatter_cube(partial, ident, loads=(), orders=None):
    maker = partial if isinstance(partial, Partial) else None
    total, width = (maker.sources[0].shape[0], maker.width) if maker else partial.shape
    rows = total // MEMBERS
    orders = orders or thirds(rows)
    operands = maker.sources if maker else [partial]
    semaphores = pltpu.SemaphoreType.DMA((len(orders), 8))
    return call(
        functools.partial(scatter_kernel, orders, maker),
        "scatter_cube", ident, Cargo(list(loads)), operands, [pltpu.HBM] * len(operands),
        [jax.ShapeDtypeStruct((rows, width), jnp.float32)], [pltpu.VMEM],
        [pltpu.VMEM((8, rows, width), jnp.bfloat16)] * 3 + [semaphores] * 4
        + (maker.scratch if maker else [semaphores]),
    )


def exchange_kernel(v_ref, o_ref, slots, send_sem, recv_sem):
    here = place()
    greet([flip(here, *names) for names in PEERS])
    copies = []
    for names in PEERS:
        k = slot(*names)
        copies.append(pltpu.make_async_remote_copy(
            src_ref=v_ref, dst_ref=slots.at[k], send_sem=send_sem.at[k], recv_sem=recv_sem.at[k],
            device_id=flip(here, *names), device_id_type=MESH,
        ))
        copies[-1].start()
    for copy in copies:
        copy.wait_recv()
    slots[0] = v_ref[...]
    for row in range(v_ref.shape[0]):
        kind, mine = divmod(row, MEMBERS)
        terms = [
            slots[k, pl.ds(kind * MEMBERS + SLOT[SLOTS[mine] ^ SLOTS[k]], 1), :]
            for k in range(MEMBERS)
        ]
        while len(terms) > 1:
            terms = [terms[2 * i] + terms[2 * i + 1] for i in range(len(terms) // 2)]
        o_ref[pl.ds(row, 1), :] = terms[0]
    for copy in copies:
        copy.wait_send()


def sum_cube(values, ident):
    shape = values.shape
    return pl.pallas_call(
        exchange_kernel,
        out_shape=jax.ShapeDtypeStruct(shape, jnp.float32),
        in_specs=[pl.BlockSpec(memory_space=pltpu.VMEM)],
        out_specs=pl.BlockSpec(memory_space=pltpu.VMEM),
        scratch_shapes=[
            pltpu.VMEM((MEMBERS,) + shape, jnp.float32),
            pltpu.SemaphoreType.DMA((MEMBERS,)),
            pltpu.SemaphoreType.DMA((MEMBERS,)),
        ],
        compiler_params=pltpu.CompilerParams(collective_id=ident, has_side_effects=True),
        cost_estimate=pl.CostEstimate(flops=0, bytes_accessed=20 * MIB, transcendentals=0),
        name="sum_cube",
    )(values)


def rope_tables(positions):
    frequency = theta_base ** (-2.0 * jnp.arange(HD // 2).astype(jnp.float32) / HD)
    angles = positions[:, None] * frequency[None, :]
    return (jnp.cos(angles), jnp.sin(angles))


def rotate(values, cos_table, sin_table):
    half_width = values.shape[-1] // 2
    former = values[..., :half_width]
    latter = values[..., half_width:]
    return jnp.concatenate(
        [former * cos_table - latter * sin_table, latter * cos_table + former * sin_table], axis=-1
    )


def normalize(values, scales):
    inverse = lax.rsqrt(jnp.mean(values * values, axis=-1, keepdims=True) + epsilon)
    return (values * inverse * scales, inverse)


def norm_back(upstream, values, inverse, scales):
    unit_rows = values * inverse
    scaled = upstream * scales
    value_grad = inverse * (
        scaled - unit_rows * jnp.mean(scaled * unit_rows, axis=-1, keepdims=True)
    )
    return (value_grad, jnp.sum(upstream * unit_rows, axis=0))


def contract_last(operand, matrix):
    return lax.dot_general(
        operand, matrix, (((1,), (1,)), ((), ())), preferred_element_type=jnp.float32
    )


def contract_first(operand, matrix):
    return lax.dot_general(
        operand, matrix, (((0,), (0,)), ((), ())), preferred_element_type=jnp.float32
    )


def row_sums(pair, ident):
    total = pair[0].shape[0]
    flat = jnp.concatenate([v.reshape(MEMBERS, total // MEMBERS) for v in pair], axis=0)
    summed = sum_cube(flat, ident).reshape(2, total, 1)
    return summed[0], summed[1]


def finish_kernel(mine_ref, came_ref, o_ref):
    own = pl.program_id(1) == lax.axis_index("x")
    o_ref[...] = jnp.where(own, mine_ref[...], came_ref[...]).astype(jnp.float32)


def whole_rows(mine, came, parts):
    rows, width = mine.shape
    step = width // parts
    half = pl.BlockSpec((rows, step), lambda p, x: (0, p))
    return pl.pallas_call(
        finish_kernel,
        grid=(parts, 2),
        out_shape=jax.ShapeDtypeStruct((rows, 2 * width), jnp.float32),
        in_specs=[half, half],
        out_specs=pl.BlockSpec((rows, step), lambda p, x: (0, 2 * p + x)),
        compiler_params=pltpu.CompilerParams(vmem_limit_bytes=32 * MIB),
        cost_estimate=pl.CostEstimate(
            flops=0, bytes_accessed=12 * rows * width, transcendentals=0
        ),
        name="whole_rows",
    )(mine, came)


def owners_product(left, right, parts=1, columns=None, **options):
    if left.shape[1] // (lax.axis_size("zh") * SIDES) % 128 == 0:
        return Product(left, right, parts, columns=columns, **options)
    if columns is not None:
        right = right[:, columns[0] : sum(columns)]
    return Owners(contract_first(left, right).astype(jnp.bfloat16), parts, **options)


def heads_are_owners(rows):
    return lax.axis_size("zh") == 2 and rows == HD


def gathered_head_rows(weight):
    full = lax.all_gather(weight, OWNERS, axis=0, tiled=True)
    head = lax.axis_index(("x", "zl", "y", "c"))
    return lax.dynamic_slice_in_dim(full, head * HD, HD, axis=0)


def summed_head_rows(grad_rows, rows):
    head = lax.axis_index(("x", "zl", "y", "c"))
    full = jnp.zeros((MEMBERS * HD, grad_rows.shape[1]), jnp.float32)
    full = lax.dynamic_update_slice_in_dim(full, grad_rows, head * HD, axis=0)
    full = lax.psum(full, EVERY)
    return lax.dynamic_slice_in_dim(full, lax.axis_index(OWNERS) * rows, rows, axis=0)


def silu_grads(hidden_grad, gate_part, up_part):
    sigmoid_gate = jax.nn.sigmoid(gate_part)
    gate_grad = hidden_grad * up_part * sigmoid_gate * (1.0 + gate_part * (1.0 - sigmoid_gate))
    up_grad = hidden_grad * gate_part * sigmoid_gate
    return gate_grad.astype(jnp.bfloat16), up_grad.astype(jnp.bfloat16)


def shards(tokens, w_qkv, w_out, w_gate_up, w_down_t, gains, starts, cotangent):
    count_rows, width = tokens.shape
    owned = gains.shape[0]
    groups = lax.axis_size("zh")
    total = MEMBERS * count_rows
    score_scale = 1.0 / math.sqrt(HD)
    direct = heads_are_owners(owned)
    local_rows = jnp.arange(count_rows, dtype=jnp.int32)
    seq_begin = lax.cummax(jnp.where(starts == 1, local_rows, 0), axis=0)

    gain_part = jnp.pad(gains.astype(jnp.float32).T, ((0, 4), (0, 0)))
    begin_part = jnp.broadcast_to(seq_begin.astype(jnp.float32)[None, :], (8, count_rows))
    z_first = (
        (("zl", "x", "y"), 0, count_rows // 2),
        (("zl", "y", "x"), count_rows // 2, count_rows // 2),
    )
    loads = [Few(gain_part, False), Few(begin_part, True), Columns(w_qkv, 3, near=3)]
    if direct:
        loads.append(HeadRows(w_out))
    tokens_all, gain_all, begin_all, qkv_cols, *out_other = gather_cube(
        tokens, 1, loads, z_first
    )
    same = lax.axis_index("x") == lax.axis_index("zh")
    if direct:
        out_rows = jnp.where(same, w_out, out_other[0])
    else:
        out_rows = gathered_head_rows(w_out)
    gain_rows = gain_all[:, :4].transpose(1, 0, 2).reshape(4, width)
    begin_all = begin_all[:, 0]
    head = lax.axis_index(("x", "zl", "y", "c"))
    head_gains = lax.dynamic_slice_in_dim(gain_rows, head * HD, HD, axis=1)
    rows_f32 = local_rows.astype(jnp.float32)
    positions = (rows_f32[None, :] - begin_all).reshape(total)
    cos_table, sin_table = rope_tables(positions)
    allowed = (rows_f32[None, None, :] <= rows_f32[None, :, None]) & (
        rows_f32[None, None, :] >= begin_all[:, :, None]
    )

    def blocks(values):
        return values.reshape(MEMBERS, count_rows, HD)

    projected = jnp.dot(tokens_all, qkv_cols, preferred_element_type=jnp.float32)
    query_raw = projected[:, :HD]
    key_raw = projected[:, HD : 2 * HD]
    value_bf = blocks(projected[:, 2 * HD :].astype(jnp.bfloat16))
    query_sq, key_sq = row_sums(
        (jnp.sum(query_raw * query_raw, axis=1), jnp.sum(key_raw * key_raw, axis=1)), 2
    )
    query_inv = lax.rsqrt(query_sq / width + epsilon)
    key_inv = lax.rsqrt(key_sq / width + epsilon)
    query_unit = query_raw * query_inv
    key_unit = key_raw * key_inv
    query_bf = blocks(rotate(query_unit * head_gains[0], cos_table, sin_table).astype(jnp.bfloat16))
    key_bf = blocks(rotate(key_unit * head_gains[1], cos_table, sin_table).astype(jnp.bfloat16))
    scores = (
        jnp.einsum("bqd,bkd->bqk", query_bf, key_bf, preferred_element_type=jnp.float32)
        * score_scale
    )
    scores = jnp.where(allowed, scores, -1e30)
    exponent = jnp.exp(scores - jnp.max(scores, axis=-1, keepdims=True))
    attention_f32 = exponent / jnp.sum(exponent, axis=-1, keepdims=True)
    attention = attention_f32.astype(jnp.bfloat16)
    attended = (
        jnp.einsum("bqk,bkd->bqd", attention, value_bf, preferred_element_type=jnp.float32)
        .reshape(total, HD)
        .astype(jnp.bfloat16)
    )
    x_most = halves(count_rows, "x", "y", "zl")
    x_or_y = (
        (("x", "y", "zl"), 0, count_rows // 2),
        (("y", "x", "zl"), count_rows // 2, count_rows // 2),
    )
    x_last = halves(count_rows, "zl", "y", "x")
    branch, gate_up_cols = scatter_cube(
        Partial(attended, out_rows, False),
        3, [Columns(w_gate_up, 2, near=1)], x_most,
    )
    branch_norm, branch_inv = normalize(branch, gain_rows[2])
    middle = tokens.astype(jnp.float32) + branch_norm
    hidden_bf, gate_up, middle_all, down_cols = gather_cube(
        middle.astype(jnp.bfloat16), 4, [Columns(w_down_t, far=1, near=3)], x_last,
        FeedForward(gate_up_cols, total), eager=True,
    )
    (feed_out,) = scatter_cube(Partial(hidden_bf, down_cols), 5)
    feed_norm, feed_inv = normalize(feed_out, gain_rows[3])
    mixed = (middle + feed_norm).astype(jnp.bfloat16)

    upstream = cotangent.astype(jnp.float32)
    feed_grad, gain_feed = norm_back(upstream, feed_out, feed_inv, gain_rows[3])
    gate_up_bf, middle_part, feed_all = gather_cube(
        feed_grad.astype(jnp.bfloat16), 6, work=FeedBack(down_cols, gate_up_cols, gate_up),
        eager=True,
    )
    feed_width = hidden_bf.shape[1]
    middle_sum, gate_sum, gate_other, up_sum = scatter_cube(
        middle_part, 7,
        [
            owners_product(
                middle_all, gate_up_bf, columns=(0, feed_width), near=1, swap=True, early=True
            ),
            owners_product(
                middle_all, gate_up_bf, columns=(feed_width, feed_width), far=1, near=2
            ),
        ], x_most,
    )
    middle_grad = upstream + middle_sum
    branch_grad, gain_branch = norm_back(middle_grad, branch, branch_inv, gain_rows[2])
    attended_grad, out_grad, down_sum, up_other = gather_cube(
        branch_grad.astype(jnp.bfloat16), 8,
        [
            owners_product(feed_all, hidden_bf, far=1, near=3),
            Whole(up_sum, "x", near=3),
        ], z_first, BranchBack(out_rows, attended),
    )
    attended_grad = blocks(attended_grad)
    down_other = lax.ppermute(down_sum, "x", [(0, 1), (1, 0)])
    if direct:
        out_came = lax.ppermute(out_grad, "zh", [(0, 1), (1, 0)])
    prob_grad = jnp.einsum(
        "bqd,bkd->bqk", attended_grad, value_bf, preferred_element_type=jnp.float32
    )
    score_bf = (
        attention_f32 * (prob_grad - jnp.sum(attention_f32 * prob_grad, axis=-1, keepdims=True))
    ).astype(jnp.bfloat16)
    value_grad = jnp.einsum(
        "bqk,bqd->bkd", attention, attended_grad, preferred_element_type=jnp.float32
    ).reshape(total, HD)
    query_grad = (
        jnp.einsum("bqk,bkd->bqd", score_bf, key_bf, preferred_element_type=jnp.float32)
        * score_scale
    ).reshape(total, HD)
    key_grad = (
        jnp.einsum("bqk,bqd->bkd", score_bf, query_bf, preferred_element_type=jnp.float32)
        * score_scale
    ).reshape(total, HD)
    query_grad = rotate(query_grad, cos_table, -sin_table)
    key_grad = rotate(key_grad, cos_table, -sin_table)
    query_scaled = query_grad * head_gains[0]
    key_scaled = key_grad * head_gains[1]
    query_dot, key_dot = row_sums(
        (jnp.sum(query_scaled * query_unit, axis=1), jnp.sum(key_scaled * key_unit, axis=1)), 9
    )
    query_raw_grad = query_inv * (query_scaled - query_unit * (query_dot / width))
    key_raw_grad = key_inv * (key_scaled - key_unit * (key_dot / width))
    projected_bf = jnp.concatenate([query_raw_grad, key_raw_grad, value_grad], axis=1).astype(
        jnp.bfloat16
    )

    gain_head = jnp.stack(
        [jnp.sum(query_grad * query_unit, axis=0), jnp.sum(key_grad * key_unit, axis=0)]
    )
    gain_terms = jnp.concatenate(
        [
            lax.dynamic_update_slice_in_dim(
                jnp.zeros((2, width), jnp.float32), gain_head, head * HD, axis=1
            ),
            jnp.stack([gain_branch, gain_feed]),
        ]
    )
    lanes = -(-owned // 128) * 128
    gain_terms = jnp.pad(
        gain_terms.reshape(4, groups * SIDES, owned).transpose(1, 0, 2),
        ((0, 0), (0, 4), (0, lanes - owned)),
    ).reshape(groups * SIDES * 8, lanes)
    loads = [
        owners_product(tokens_all, projected_bf, 3, swap=True, near=1, early=True),
        Owners(gain_terms, swap=True, fold=True, early=True),
        FinalRows((gate_sum, gate_other), (up_sum, up_other)),
        FinalRows((down_sum, down_other)),
    ]
    if direct:
        out_sum = out_grad.astype(jnp.float32) + out_came.astype(jnp.float32)
        out_sum = out_sum.astype(jnp.bfloat16)
        loads.append(Whole(out_sum, "x", near=1))
    (
        tokens_sum, qkv_sum, qkv_other, gain_sum, gain_other, grad_gate_up, grad_down_t, *out_other
    ) = scatter_cube(
        Partial(projected_bf, qkv_cols), 10, loads, x_or_y
    )
    grad_tokens = middle_grad + tokens_sum
    if direct:
        grad_out = jnp.where(same, out_sum, out_other[0]).astype(jnp.float32)
    else:
        grad_out = summed_head_rows(out_grad.astype(jnp.float32), owned)
    grad_qkv = whole_rows(qkv_sum, qkv_other, 3)
    grad_gains = (gain_sum + gain_other)[:4, :owned].T
    return (mixed, grad_tokens, grad_qkv, grad_out, grad_gate_up, grad_down_t, grad_gains)


def solution(mesh):
    sizes = dict(mesh.shape)
    groups = sizes["fsdp"] // SIDES
    finer = Mesh(mesh.devices.reshape(2, groups, 2, 2, 2), EVERY)
    return jax.shard_map(
        shards,
        mesh=finer,
        in_specs=(
            P(EVERY, None),
            P(OWNERS, None),
            P(OWNERS, None),
            P(OWNERS, None),
            P(OWNERS, None),
            P(OWNERS, None),
            P(EVERY),
            P(EVERY, None),
        ),
        out_specs=(
            P(EVERY, None),
            P(EVERY, None),
            P(OWNERS, None),
            P(OWNERS, None),
            P(OWNERS, None),
            P(OWNERS, None),
            P(OWNERS, None),
        ),
        check_vma=False,
    )
```

```python
import functools
import math

import jax
import jax.numpy as jnp
from jax import lax
from jax.experimental import pallas as pl
from jax.experimental.pallas import tpu as pltpu
from jax.sharding import Mesh, PartitionSpec as P

HD = 128

epsilon = 1e-06
theta_base = 500000.0

OWNERS = ("zh", "zl", "y", "c")
EVERY = ("x", "zh", "zl", "y", "c")
MEMBERS = 16
SIDES = 8
SIDE_BITS = {"zl": 4, "y": 2, "c": 1}
BITS = {"x": 8, "zl": 4, "y": 2, "c": 1}
SLOTS = [
    frozenset(names + core)
    for names in (
        (), ("x",), ("y",), ("zl",), ("x", "y"), ("x", "zl"), ("y", "zl"), ("x", "y", "zl"),
    )
    for core in ((), ("c",))
]
SLOT = {names: k for k, names in enumerate(SLOTS)}
MESH = pl.DeviceIdType.MESH
MIB = 1 << 20


def thirds(rows):
    unit = rows // 8
    return (
        (("x", "y", "zl"), 0, 3 * unit),
        (("y", "zl", "x"), 3 * unit, 3 * unit),
        (("zl", "x", "y"), 6 * unit, 2 * unit),
    )


def halves(rows, *order):
    return ((order, 0, rows // 2), (order, rows // 2, rows // 2))


PEERS = [tuple(n for n in BITS if m & BITS[n]) for m in range(1, MEMBERS)]
SIDE_PEERS = [tuple(n for n in SIDE_BITS if m & SIDE_BITS[n]) for m in range(SIDES)]


def slot(*names):
    return SLOT[frozenset(names)]


def place():
    return {name: lax.axis_index(name) for name in EVERY}


def flip(here, *names):
    return {name: 1 - here[name] for name in names}


def with_bits(here, names, bits):
    index = 0
    for name, bit in bits.items():
        index = index + bit * ((1 - here[name]) if name in names else here[name])
    return index


def subset(order, mask):
    return tuple(name for k, name in enumerate(order) if mask >> k & 1)


def greet(devices):
    barrier = pltpu.get_barrier_semaphore()
    for device in devices:
        pl.semaphore_signal(barrier, inc=1, device_id=device, device_id_type=MESH)
    pl.semaphore_wait(barrier, len(devices))


def owner_at(here, groups, step, names):
    device = flip(here, *names)
    if step:
        device["zh"] = lax.rem(here["zh"] + step, groups)
    return device


def at(start, size):
    return pl.ds(pl.multiple_of(start, size), size)


class Load:
    space = pltpu.HBM
    parts = 1

    def __init__(self, source, far=0, near=0, early=False):
        self.sources = [source]
        self.stages = (near, far)
        self.early = early
        self.groups = lax.axis_size("zh")

    def spaces(self):
        return [self.space] * len(self.sources), [self.space] * len(self.outs)

    def semaphores(self):
        count = len(self.moves())
        return [pltpu.SemaphoreType.DMA((count,)), pltpu.SemaphoreType.DMA((count,))]

    def scratch(self):
        return self.semaphores()

    def moves(self):
        return [
            ((step, names), part)
            for step in range(self.groups)
            for names in SIDE_PEERS
            for part in range(self.parts)
        ]

    def reached(self):
        return {peer for peer, _ in self.moves() if peer != (0, ())}

    def around(self, here, step, names):
        there = lax.rem(here["zh"] + step, self.groups)
        whence = lax.rem(here["zh"] + self.groups - step, self.groups)
        mine, other = with_bits(here, (), SIDE_BITS), with_bits(here, names, SIDE_BITS)
        return mine, other, there, whence

    def bind(self, here, sources, targets, scratch):
        self.here, self.src, self.dst = here, sources, targets
        self.send, self.recv, *self.more = scratch
        self.copies = []
        for index, ((step, names), part) in enumerate(self.moves()):
            source, target, landing = self.views(here, step, names, part)
            stage = self.stages[1 if step else 0]
            if not step and not names:
                copy = pltpu.make_async_copy(source, target, self.send.at[index])
                self.copies.append((stage, copy, None, (step, names)))
                continue
            copy = pltpu.make_async_remote_copy(
                src_ref=source, dst_ref=target,
                send_sem=self.send.at[index], recv_sem=self.recv.at[index],
                device_id=owner_at(here, self.groups, step, names), device_id_type=MESH,
            )
            landed = pltpu.make_async_copy(landing, landing, self.recv.at[index])
            self.copies.append((stage, copy, landed, (step, names)))

    def start(self, stage):
        for when, copy, _, _ in self.copies:
            if when == stage:
                copy.start()

    def land(self):
        for _, copy, landed, _ in self.copies:
            (copy if landed is None else landed).wait()

    def finish(self):
        pass

    def leave(self):
        for _, copy, landed, _ in self.copies:
            if landed is not None:
                copy.wait_send()


class Columns(Load):
    def __init__(self, source, parts=1, **stages):
        super().__init__(source, **stages)
        self.parts = parts
        self.rows = source.shape[0]
        self.piece = source.shape[1] // (parts * MEMBERS)
        shape = (self.groups * SIDES * self.rows, parts * self.piece)
        self.outs = [jax.ShapeDtypeStruct(shape, source.dtype)]

    def views(self, here, step, names, part):
        mine, other, _, whence = self.around(here, step, names)
        first = part * MEMBERS + here["x"] * SIDES + other
        columns = pl.ds(part * self.piece, self.piece)
        return (
            self.src[0].at[:, at(first * self.piece, self.piece)],
            self.dst[0].at[at((here["zh"] * SIDES + mine) * self.rows, self.rows), columns],
            self.dst[0].at[at((whence * SIDES + other) * self.rows, self.rows), columns],
        )


class Few(Load):
    space = pltpu.VMEM

    def __init__(self, source, cube):
        super().__init__(source)
        self.cube = cube
        count = MEMBERS if cube else self.groups * SIDES
        self.outs = [jax.ShapeDtypeStruct((count,) + source.shape, source.dtype)]

    def moves(self):
        if self.cube:
            return [((0, names), 0) for names in [()] + PEERS]
        return super().moves()

    def views(self, here, step, names, part):
        if self.cube:
            spot = self.dst[0].at[slot(*names)]
            return self.src[0], spot, spot
        mine, other, _, whence = self.around(here, step, names)
        return (
            self.src[0],
            self.dst[0].at[here["zh"] * SIDES + mine],
            self.dst[0].at[whence * SIDES + other],
        )


class Whole(Load):
    def __init__(self, source, axis, **stages):
        super().__init__(source, **stages)
        self.axis = axis
        self.outs = [jax.ShapeDtypeStruct(source.shape, source.dtype)]

    def moves(self):
        return [((0, ("x",)) if self.axis == "x" else (1, ()), 0)]

    def views(self, here, step, names, part):
        return self.src[0], self.dst[0], self.dst[0]


class Swap:
    def swap_scratch(self):
        return [pltpu.SemaphoreType.DMA((3,))]

    def give(self, total, sems):
        self.kept = pltpu.make_async_copy(total, self.dst[0], sems.at[0])
        self.kept.start()
        self.given = None
        if len(self.outs) > 1:
            self.given = pltpu.make_async_remote_copy(
                src_ref=total, dst_ref=self.dst[1], send_sem=sems.at[1], recv_sem=sems.at[2],
                device_id=flip(self.here, "x"), device_id_type=MESH,
            )
            self.given.start()

    def given_wait(self):
        self.kept.wait()
        if self.given is not None:
            self.given.wait()


class Owners(Load, Swap):
    def __init__(self, source, parts=1, swap=False, fold=False, **stages):
        super().__init__(source, **stages)
        self.setup(source.shape[0], source.shape[1], source.dtype, parts, swap, fold)

    def setup(self, depth, width, kind, parts, swap, fold):
        self.parts = parts
        self.fold = fold
        self.kind = kind
        self.rows = depth // (self.groups * SIDES)
        self.piece = width // parts
        self.wide = parts * SIDES * self.piece
        total = (self.rows, self.piece if fold else self.wide)
        self.total = total
        self.outs = [jax.ShapeDtypeStruct(total, kind)] * (1 + swap)
        self.swap = swap

    def reached(self):
        return super().reached() | ({(0, ("x",))} if self.swap else set())

    def spaces(self):
        return [pltpu.VMEM if self.fold else pltpu.HBM] * len(self.sources), [pltpu.HBM] * len(self.outs)

    def scratch(self):
        return self.semaphores() + self.swap_scratch() + [
            pltpu.VMEM((self.groups, self.rows, self.wide), self.kind),
            pltpu.VMEM(self.total, self.kind),
        ]

    def views(self, here, step, names, part):
        mine, other, there, whence = self.around(here, step, names)
        terms = self.more[1]
        return (
            self.slice_of(there * SIDES + other, part),
            terms.at[here["zh"], :, at((part * SIDES + mine) * self.piece, self.piece)],
            terms.at[whence, :, at((part * SIDES + other) * self.piece, self.piece)],
        )

    def slice_of(self, target, part):
        return self.src[0].at[
            at(target * self.rows, self.rows), pl.ds(part * self.piece, self.piece)
        ]

    def finish(self):
        sems, terms, total = self.more[:3]
        step = self.piece if self.fold else min(512, self.wide)

        def add(start):
            value = terms[0, :, pl.ds(start, step)].astype(jnp.float32)
            for group in range(1, self.groups):
                value = value + terms[group, :, pl.ds(start, step)].astype(jnp.float32)
            return value

        if self.fold:
            value = add(0)
            for side in range(1, SIDES):
                value = value + add(side * step)
            total[...] = value
        else:

            @pl.loop(0, self.wide // step)
            def _(k):
                start = pl.multiple_of(k * step, step)
                total[:, pl.ds(start, step)] = add(start).astype(total.dtype)

        self.give(total, sems)

    def leave(self):
        super().leave()
        self.given_wait()


class Product(Owners):
    def __init__(self, left, right, parts=1, swap=False, columns=None, **stages):
        Load.__init__(self, left, **stages)
        self.sources = [left, right]
        self.columns = columns or (0, right.shape[1])
        self.setup(left.shape[1], self.columns[1], jnp.bfloat16, parts, swap, False)

    def scratch(self):
        depth, width = self.sources[0].shape[0], self.columns[1]
        return super().scratch() + [
            pltpu.VMEM((2, depth, 2 * self.rows), jnp.bfloat16),
            pltpu.VMEM((depth, width), jnp.bfloat16),
            pltpu.VMEM((self.groups * SIDES * self.rows, width), jnp.bfloat16),
            pltpu.SemaphoreType.DMA((3,)),
        ]

    def slice_of(self, target, part):
        return self.more[5].at[
            at(target * self.rows, self.rows), pl.ds(part * self.piece, self.piece)
        ]

    def tiles(self):
        order = [
            (step, names)
            for step in reversed(range(self.groups))
            for names in SIDE_PEERS
            if "c" not in names
        ]
        return order

    def first_row(self, step, names):
        _, other, there, _ = self.around(self.here, step, names)
        return (there * SIDES + (other // 2) * 2) * self.rows

    def fetch(self, k):
        step, names = self.tiles()[k]
        left = self.src[0].at[:, at(self.first_row(step, names), 2 * self.rows)]
        return pltpu.make_async_copy(left, self.more[3].at[k % 2], self.more[6].at[k % 2])

    def begin(self):
        right = self.src[1].at[:, pl.ds(*self.columns)]
        self.right = pltpu.make_async_copy(right, self.more[4], self.more[6].at[2])
        self.right.start()
        self.fetch(0).start()
        self.fetch(1).start()

    def start(self, stage):
        tiles = self.tiles()
        _, _, _, lefts, right, result, _ = self.more
        for k, (step, names) in enumerate(tiles):
            if self.stages[1 if step else 0] != stage:
                continue
            if k == 0:
                self.right.wait()
            self.fetch(k).wait()
            rows = at(self.first_row(step, names), 2 * self.rows)
            width = self.columns[1]
            left = lefts[k % 2]
            for column in range(0, width, 256):
                columns = pl.ds(column, min(256, width - column))
                result[rows, columns] = lax.dot_general(
                    left, right[:, columns], (((0,), (0,)), ((), ())),
                    preferred_element_type=jnp.float32,
                ).astype(jnp.bfloat16)
            if k + 2 < len(tiles):
                self.fetch(k + 2).start()
            for _, copy, _, peer in self.copies:
                if peer in ((step, names), (step, names + ("c",))):
                    copy.start()


class HeadRows(Load):
    def __init__(self, source):
        super().__init__(source)
        self.outs = [jax.ShapeDtypeStruct(source.shape, source.dtype)]

    def moves(self):
        return [((1, ()), 0), ((1, ("x",)), 0)]

    def bind(self, here, sources, targets, scratch):
        (source,), (target,), (send, recv) = sources, targets, scratch
        half = source.shape[0] // 2
        self.home = here["x"] == here["zh"]
        mine = jnp.where(self.home, 0, 1)
        rows = at(mine * half, half)
        self.copy = pltpu.make_async_remote_copy(
            src_ref=source.at[rows], dst_ref=target.at[rows],
            send_sem=send.at[0], recv_sem=recv.at[mine],
            device_id={"x": here["zh"], "zh": 1 - here["zh"]}, device_id_type=MESH,
        )
        spots_here = [target.at[pl.ds(k * half, half)] for k in range(2)]
        self.landed = [
            pltpu.make_async_copy(spot, spot, recv.at[k]) for k, spot in enumerate(spots_here)
        ]

    def start(self, stage):
        if stage == 0:
            self.copy.start()

    def land(self):
        @pl.when(jnp.logical_not(self.home))
        def _():
            for landed in self.landed:
                landed.wait()

    def leave(self):
        self.copy.wait_send()


class HeadSums(Load, Swap):
    def __init__(self, source, **stages):
        super().__init__(source, **stages)
        rows, width = source.shape
        self.half = jax.ShapeDtypeStruct((rows // 2, width), source.dtype)
        self.outs = [self.half] * 2

    def spaces(self):
        return [pltpu.VMEM], [pltpu.HBM] * 2

    def moves(self):
        return [((1, ()), 0), ((0, ("x",)), 0), ((0, ("x",)), 0)]

    def scratch(self):
        return self.semaphores() + self.swap_scratch() + [
            pltpu.VMEM((3,) + self.half.shape, jnp.bfloat16),
            pltpu.VMEM(self.half.shape, jnp.bfloat16),
        ]

    def bind(self, here, sources, targets, scratch):
        self.here, self.dst = here, targets
        (self.source,) = sources
        send, recv, self.sems, self.terms, self.total = scratch
        self.home = here["x"] == here["zh"]
        rows = self.half.shape[0]

        def copy(source, term, k, device):
            return pltpu.make_async_remote_copy(
                src_ref=source, dst_ref=self.terms.at[term],
                send_sem=send.at[k], recv_sem=recv.at[term],
                device_id=device, device_id_type=MESH,
            )

        first, second = (self.source.at[pl.ds(k * rows, rows)] for k in range(2))
        across = {"zh": 1 - here["zh"]}
        self.near = copy(second, 0, 0, flip(here, "x"))
        self.relay = copy(self.terms.at[2], 1, 1, across)
        self.far = copy(first, 1, 1, across)
        self.hand = copy(second, 2, 0, flip(here, "x"))

    def start(self, stage):
        if stage == self.stages[1]:

            @pl.when(self.home)
            def _():
                self.near.start()

            @pl.when(jnp.logical_not(self.home))
            def _():
                self.hand.start()
                self.far.start()

        if stage == self.stages[0]:

            @pl.when(self.home)
            def _():
                self.hand.wait_recv()
                self.relay.start()

    def land(self):
        self.far.wait_recv()

        @pl.when(jnp.logical_not(self.home))
        def _():
            self.near.wait_recv()

    def finish(self):
        rows = self.half.shape[0]

        @pl.when(self.home)
        def _():
            self.terms[0] = self.source[pl.ds(0, rows)]

        self.total[...] = (
            self.terms[0].astype(jnp.float32) + self.terms[1].astype(jnp.float32)
        ).astype(jnp.bfloat16)
        self.give(self.total, self.sems)

    def leave(self):
        self.near.wait_send()
        self.far.wait_send()
        self.given_wait()


class FinalRows(Load):
    def __init__(self, *pairs, near=4):
        super().__init__(None, near=near)
        self.sources = [half for pair in pairs for half in pair]
        rows, self.width = pairs[0][0].shape
        self.step = min(2048, self.width)
        self.outs = [jax.ShapeDtypeStruct((rows, len(self.sources) * self.width), jnp.float32)]

    def moves(self):
        return []

    def scratch(self):
        rows = self.outs[0].shape[0]
        return [
            pltpu.VMEM((2, rows, self.step), jnp.bfloat16),
            pltpu.VMEM((2, rows, self.step), jnp.float32),
            pltpu.SemaphoreType.DMA((4,)),
        ]

    def bind(self, here, sources, targets, scratch):
        self.here, self.src, self.dst = here, sources, targets
        self.halves, self.wholes, self.sems = scratch

    def start(self, stage):
        if stage != self.stages[0]:
            return
        x = self.here["x"]
        steps = [
            (k, start) for k in range(len(self.sources)) for start in range(0, self.width, self.step)
        ]

        def fetch(n):
            k, start = steps[n]
            return pltpu.make_async_copy(
                self.src[k].at[:, pl.ds(start, self.step)], self.halves.at[n % 2],
                self.sems.at[n % 2],
            )

        def store(n):
            k, start = steps[n]
            half = x if k % 2 == 0 else 1 - x
            first = (2 * (k // 2) + half) * self.width + start
            return pltpu.make_async_copy(
                self.wholes.at[n % 2], self.dst[0].at[:, at(first, self.step)],
                self.sems.at[2 + n % 2],
            )

        fetch(0).start()
        for n in range(len(steps)):
            if n + 1 < len(steps):
                fetch(n + 1).start()
            fetch(n).wait()
            if n >= 2:
                store(n - 2).wait()
            self.wholes[n % 2] = self.halves[n % 2].astype(jnp.float32)
            store(n).start()
        for n in range(max(0, len(steps) - 2), len(steps)):
            store(n).wait()

    def land(self):
        pass

    def leave(self):
        pass


class Cargo:
    def __init__(self, loads):
        self.loads = loads
        self.sources = [s for load in loads for s in load.sources]
        self.outs = [o for load in loads for o in load.outs]
        self.in_specs = [pl.BlockSpec(memory_space=s) for load in loads for s in load.spaces()[0]]
        self.out_specs = [pl.BlockSpec(memory_space=s) for load in loads for s in load.spaces()[1]]
        self.scratch = [s for load in loads for s in load.scratch()]

    def bind(self, here, sources, targets, scratch):
        sources, targets, scratch = list(sources), list(targets), list(scratch)

        def take(refs, count):
            taken = refs[:count]
            del refs[:count]
            return taken

        for load in self.loads:
            load.bind(
                here,
                take(sources, len(load.sources)),
                take(targets, len(load.outs)),
                take(scratch, len(load.scratch())),
            )
            if hasattr(load, "begin"):
                load.begin()

    def greet(self, here, names):
        reached = {(0, n) for n in names}
        for load in self.loads:
            reached |= load.reached()
        groups = lax.axis_size("zh")
        greet([owner_at(here, groups, step, n) for step, n in sorted(reached)])

    def start(self, stage):
        for load in self.loads:
            load.start(stage)

    def finish(self, early=False):
        for load in self.loads:
            if load.early == early:
                load.land()
                load.finish()
        if not early:
            for load in self.loads:
                load.leave()


class Work:
    operands = ()

    def __init__(self, *sources):
        self.sources = list(sources)

    def bind(self, sources, targets, scratch):
        self.src, self.dst, self.more = list(sources), list(targets), list(scratch)
        self.copies = []

    def begin(self):
        pass

    def keep(self, copy):
        self.copies.append(copy)
        copy.start()

    def close(self):
        for copy in self.copies:
            copy.wait()


class FeedForward(Work):
    def __init__(self, gate_up_cols, total):
        super().__init__(gate_up_cols)
        width, both = gate_up_cols.shape
        self.half, self.pair = both // 2, 2 * total // MEMBERS
        self.in_spaces = [pltpu.HBM]
        self.outs = [
            jax.ShapeDtypeStruct((total, self.half), jnp.bfloat16),
            jax.ShapeDtypeStruct((total, both), jnp.float32),
            jax.ShapeDtypeStruct((total, width), jnp.bfloat16),
        ]
        self.out_spaces = [pltpu.HBM, pltpu.HBM, pltpu.HBM]
        self.scratch = [
            pltpu.VMEM((2, self.pair, both), jnp.float32),
            pltpu.SemaphoreType.DMA((3, SIDES)),
            pltpu.VMEM(gate_up_cols.shape, gate_up_cols.dtype),
            pltpu.SemaphoreType.DMA(()),
            pltpu.VMEM((total, self.half), jnp.bfloat16),
        ]

    def begin(self):
        self.load = pltpu.make_async_copy(self.src[0], self.more[2], self.more[3])
        self.load.start()

    def tile(self, k, rows_ref):
        (hidden_out, gate_up, rows_out), (staged, sems, cols, _, hidden) = self.dst, self.more
        if k == 0:
            self.load.wait()
        rows = pl.ds(k * self.pair, self.pair)
        self.keep(pltpu.make_async_copy(rows_ref, rows_out.at[rows], sems.at[0, k]))
        if k >= 2:
            self.last[k - 2].wait()
        value = rows_ref[...]
        for start in range(0, self.half, 256):
            columns = pl.ds(start, 256)
            others = pl.ds(self.half + start, 256)
            gate = jnp.dot(value, cols[:, columns], preferred_element_type=jnp.float32)
            up = jnp.dot(value, cols[:, others], preferred_element_type=jnp.float32)
            staged[k % 2, :, columns] = gate
            staged[k % 2, :, others] = up
            hidden[rows, columns] = (gate * jax.nn.sigmoid(gate) * up).astype(jnp.bfloat16)
        self.keep(pltpu.make_async_copy(hidden.at[rows], hidden_out.at[rows], sems.at[2, k]))
        copy = pltpu.make_async_copy(staged.at[k % 2], gate_up.at[rows], sems.at[1, k])
        copy.start()
        if k == 0:
            self.last = []
        self.last.append(copy)

    def close(self):
        super().close()
        for copy in self.last[-2:]:
            copy.wait()


class FeedBack(Work):
    def __init__(self, down_cols, gate_up_cols, gate_up):
        super().__init__(down_cols, gate_up_cols, gate_up)
        total, both = gate_up.shape
        width = down_cols.shape[0]
        self.half, self.width, self.pair = both // 2, width, 2 * total // MEMBERS
        self.in_spaces = [pltpu.HBM] * 3
        self.outs = [
            jax.ShapeDtypeStruct((total, both), jnp.bfloat16),
            jax.ShapeDtypeStruct((total, width), jnp.bfloat16),
            jax.ShapeDtypeStruct((total, width), jnp.bfloat16),
        ]
        self.out_spaces = [pltpu.HBM, pltpu.HBM, pltpu.HBM]
        self.scratch = [
            pltpu.VMEM((2, self.pair, both), jnp.float32),
            pltpu.SemaphoreType.DMA((4, SIDES)),
            pltpu.VMEM(down_cols.shape, down_cols.dtype),
            pltpu.VMEM(gate_up_cols.shape, gate_up_cols.dtype),
            pltpu.SemaphoreType.DMA((2,)),
            pltpu.VMEM((total, both), jnp.bfloat16),
            pltpu.VMEM((total, width), jnp.bfloat16),
        ]

    def fetch(self, k):
        rows = pl.ds(k * self.pair, self.pair)
        return pltpu.make_async_copy(
            self.src[2].at[rows], self.more[0].at[k % 2], self.more[1].at[0, k]
        )

    def begin(self):
        self.loads = [
            pltpu.make_async_copy(self.src[i], self.more[2 + i], self.more[4].at[i])
            for i in range(2)
        ]
        for copy in self.loads:
            copy.start()
        self.fetch(0).start()
        self.fetch(1).start()

    def tile(self, k, rows_ref):
        grads_out, part_out, rows_out = self.dst
        saved, sems, down, cols, _, grads, part = self.more
        if k == 0:
            for copy in self.loads:
                copy.wait()
        rows = pl.ds(k * self.pair, self.pair)
        self.keep(pltpu.make_async_copy(rows_ref, rows_out.at[rows], sems.at[1, k]))
        self.fetch(k).wait()
        value = rows_ref[...]
        for start in range(0, self.half, 256):
            columns = pl.ds(start, 256)
            others = pl.ds(self.half + start, 256)
            hidden_grad = jnp.dot(value, down[:, columns], preferred_element_type=jnp.float32)
            gate_bf, up_bf = silu_grads(
                hidden_grad, saved[k % 2, :, columns], saved[k % 2, :, others]
            )
            grads[rows, columns] = gate_bf
            grads[rows, others] = up_bf
        if k + 2 < SIDES:
            self.fetch(k + 2).start()
        self.keep(pltpu.make_async_copy(grads.at[rows], grads_out.at[rows], sems.at[2, k]))
        both = grads[rows]
        for start in range(0, self.width, 256):
            columns = pl.ds(start, 256)
            part[rows, columns] = contract_last(both, cols[columns, :]).astype(jnp.bfloat16)
        self.keep(pltpu.make_async_copy(part.at[rows], part_out.at[rows], sems.at[3, k]))


class BranchBack(Work):
    def __init__(self, out_rows, attended):
        super().__init__(out_rows, attended)
        total, width = attended.shape[0], out_rows.shape[1]
        self.width, self.pair = width, 2 * total // MEMBERS
        self.in_spaces = [pltpu.VMEM, pltpu.VMEM]
        self.outs = [
            jax.ShapeDtypeStruct((total, HD), jnp.bfloat16),
            jax.ShapeDtypeStruct((HD, width), jnp.bfloat16),
        ]
        self.out_spaces = [pltpu.VMEM, pltpu.VMEM]
        self.scratch = [pltpu.VMEM((HD, width), jnp.float32)]

    def tile(self, k, rows_ref):
        (out_rows, attended), (grad, _), (total,) = self.src, self.dst, self.more
        rows = pl.ds(k * self.pair, self.pair)
        value = rows_ref[...]
        grad[rows] = contract_last(value, out_rows[...]).astype(jnp.bfloat16)
        for start in range(0, self.width, 512):
            columns = pl.ds(start, 512)
            term = contract_first(attended[rows], rows_ref[:, columns])
            total[:, columns] = term if k == 0 else total[:, columns] + term

    def close(self):
        self.dst[1][...] = self.more[0][...].astype(jnp.bfloat16)


GATHER_STAGES = (0, 1, 2, 3)
NEAR = [("x",), ("zl",), ("y",), ("c",)]


def room_for(*held):
    sizes = [math.prod(s.shape) * jnp.dtype(s.dtype).itemsize for s in held]
    return sum(sizes) + 8 * MIB


def only_vmem(arrays, spaces):
    return [a for a, space in zip(arrays, spaces) if space == pltpu.VMEM]


def in_hbm(value, space):
    return pltpu.with_memory_space_constraint(value, pltpu.HBM) if space == pltpu.HBM else value


def call(body, name, ident, cargo, operands, spaces, outs, out_spaces, scratch):
    cargo_in = [space for load in cargo.loads for space in load.spaces()[0]]
    operands = [in_hbm(v, space) for v, space in zip(operands, spaces)]
    sources = [in_hbm(v, space) for v, space in zip(cargo.sources, cargo_in)]
    cargo_out = [space for load in cargo.loads for space in load.spaces()[1]]
    kept = [
        space(out.shape, out.dtype)
        for out, space in zip(list(outs) + cargo.outs, list(out_spaces) + cargo_out)
    ]
    held = only_vmem(operands, spaces) + only_vmem(outs, out_spaces)
    held += only_vmem(cargo.sources, cargo_in)
    held += [s for s in scratch + cargo.scratch if s.memory_space == pltpu.VMEM]
    return pl.pallas_call(
        functools.partial(body, cargo),
        out_shape=kept,
        in_specs=[pl.BlockSpec(memory_space=s) for s in spaces] + cargo.in_specs,
        out_specs=[pl.BlockSpec(memory_space=s) for s in out_spaces] + cargo.out_specs,
        scratch_shapes=scratch + cargo.scratch,
        compiler_params=pltpu.CompilerParams(
            collective_id=ident, has_side_effects=True, vmem_limit_bytes=room_for(*held)
        ),
        cost_estimate=pl.CostEstimate(flops=0, bytes_accessed=100 * MIB, transcendentals=0),
        name=name,
    )(*operands, *sources)


def take(refs, count):
    taken = refs[:count]
    del refs[:count]
    return taken


def gather_kernel(orders, work, eager, cargo, x_ref, *refs):
    refs = list(refs)
    work_in = take(refs, len(work.sources)) if work else []
    sources = take(refs, len(cargo.sources))
    work_out = take(refs, len(work.outs) if work else 1)
    targets = take(refs, len(cargo.outs))
    send_sem, recv_sem, core_send, core_recv, own_sem = take(refs, 5)
    here = place()
    spans = [pl.ds(r0, size) for _, r0, size in orders]
    orders = [o for o, _, _ in orders]
    pieces = range(len(orders))
    if work:
        (o_ref,) = take(refs, 1)
        work.bind(work_in, work_out, take(refs, len(work.scratch)))
        work.begin()
    else:
        o_ref = work_out[0]
    rows, width = x_ref.shape
    cargo.bind(here, sources, targets, refs)
    cargo.greet(here, NEAR)
    own = pltpu.make_async_copy(x_ref, spots(o_ref, slice(0, 1), rows), own_sem)

    def spot(p, *names):
        return spots(o_ref, slot(*names), rows, spans[p])

    def source(p, mask):
        return spot(p, *subset(orders[p], mask)) if mask else x_ref.at[spans[p]]

    def over(p, mask, k):
        whole = mask | 1 << k
        return pltpu.make_async_remote_copy(
            src_ref=source(p, mask), dst_ref=spot(p, *subset(orders[p], whole)),
            send_sem=send_sem.at[p, whole], recv_sem=recv_sem.at[p, whole],
            device_id=flip(here, orders[p][k]), device_id_type=MESH,
        )

    def across(p, mask):
        return pltpu.make_async_remote_copy(
            src_ref=source(p, mask), dst_ref=spot(p, "c", *subset(orders[p], mask)),
            send_sem=core_send.at[p, mask], recv_sem=core_recv.at[p, mask],
            device_id=flip(here, "c"), device_id_type=MESH,
        )

    sent = []

    def pass_on(mask):
        for p in pieces:
            if mask:
                landing = spot(p, *subset(orders[p], mask))
                pltpu.make_async_copy(landing, landing, recv_sem.at[p, mask]).wait()
            for k in range(mask.bit_length(), 3):
                sent.append(over(p, mask, k))
                sent[-1].start()
        for p in pieces:
            sent.append(across(p, mask))
            sent[-1].start()
        if mask == 0:
            own.start()
        if mask in GATHER_STAGES:
            cargo.start(GATHER_STAGES.index(mask))

    def from_core(*masks):
        for mask in masks:
            for p in pieces:
                landing = spot(p, "c", *subset(orders[p], mask))
                pltpu.make_async_copy(landing, landing, core_recv.at[p, mask]).wait()

    def tiles(*numbers):
        for k in numbers:
            work.tile(k, o_ref.at[pl.ds(2 * rows * k, 2 * rows)])

    if eager:
        pass_on(0)
        own.wait()
        from_core(0)
        tiles(0)
        for mask in (1, 2, 3, 4):
            pass_on(mask)
        from_core(1, 2, 4)
        tiles(1, 2)
        pass_on(5)
        tiles(3)
        pass_on(6)
        from_core(3, 5, 6)
        tiles(4)
        pass_on(7)
        tiles(5, 6)
        from_core(7)
        tiles(7)
    else:
        for mask in range(8):
            pass_on(mask)
        from_core(*range(8))
        own.wait()
        if work:
            tiles(*range(SIDES))
    for copy in sent:
        copy.wait_send()
    if work:
        work.close()
    cargo.finish()


def spots(ref, index, rows, span=None):
    if isinstance(index, slice):
        return ref.at[pl.ds(index.start * rows, rows)]
    if span is None:
        return ref.at[pl.ds(index * rows, rows)]
    return ref.at[pl.ds(index * rows + span.start, span.size)]


def gather_cube(block, ident, loads=(), orders=None, work=None, eager=False):
    rows, width = block.shape
    orders = orders or thirds(rows)
    whole = jax.ShapeDtypeStruct((MEMBERS * rows, width), block.dtype)
    scratch = [pltpu.SemaphoreType.DMA((len(orders), 8))] * 4 + [pltpu.SemaphoreType.DMA(())]
    if work:
        operands, spaces = [block] + work.sources, [pltpu.HBM] + work.in_spaces
        outs, out_spaces = work.outs, work.out_spaces
        scratch += [pltpu.VMEM(whole.shape, whole.dtype)] + work.scratch
    else:
        operands, spaces, outs, out_spaces = [block], [pltpu.HBM], [whole], [pltpu.HBM]
    return call(
        functools.partial(gather_kernel, orders, work, eager),
        "gather_cube", ident, Cargo(list(loads)), operands, spaces, outs, out_spaces, scratch,
    )


class Partial:
    def __init__(self, left, right, last=True):
        self.sources = [left, right]
        self.last = last
        self.pair = 2 * left.shape[0] // MEMBERS
        self.width = right.shape[0 if last else 1]
        self.scratch = [
            pltpu.VMEM(left.shape, left.dtype),
            pltpu.VMEM(right.shape, right.dtype),
            pltpu.SemaphoreType.DMA((2,)),
            pltpu.VMEM((left.shape[0], self.width), jnp.bfloat16),
        ]

    def begin(self, sources, scratch):
        self.left, self.right, sems, self.made = scratch
        self.loads = [
            pltpu.make_async_copy(source, held, sems.at[k])
            for k, (source, held) in enumerate(zip(sources, (self.left, self.right)))
        ]
        for copy in self.loads:
            copy.start()

    def wait(self):
        for copy in self.loads:
            copy.wait()

    def tile(self, k):
        rows = pl.ds(k * self.pair, self.pair)
        for start in range(0, self.width, 512):
            columns = pl.ds(start, 512)
            if self.last:
                value = contract_last(self.left[rows], self.right[columns, :])
            else:
                value = jnp.dot(
                    self.left[rows], self.right[:, columns], preferred_element_type=jnp.float32
                )
            self.made[rows, columns] = value.astype(jnp.bfloat16)


def scatter_kernel(orders, maker, cargo, *refs):
    refs = list(refs)
    heads = take(refs, len(maker.sources) if maker else 1)
    sources = take(refs, len(cargo.sources))
    (o_ref,) = take(refs, 1)
    targets = take(refs, len(cargo.outs))
    acc, rcore, came, core_send, core_recv, send_sem, recv_sem = take(refs, 7)
    here = place()
    rows = o_ref.shape[0]
    spans = [pl.ds(r0, size) for _, r0, size in orders]
    orders = [o for o, _, _ in orders]
    pieces = range(len(orders))
    if maker:
        maker.begin(heads, take(refs, len(maker.scratch)))
        p_ref = maker.made
    else:
        p_ref = heads[0]
        (load_sem,) = take(refs, 1)
    cargo.bind(here, sources, targets, refs)
    cargo.greet(here, NEAR)

    def away(p, mask):
        return pltpu.make_async_remote_copy(
            src_ref=spots(p_ref, slot("c", *subset(orders[p], mask)), rows, spans[p]),
            dst_ref=rcore.at[mask, spans[p]],
            send_sem=core_send.at[p, mask], recv_sem=core_recv.at[p, mask],
            device_id=flip(here, "c"), device_id_type=MESH,
        )

    def mine(p, mask):
        return spots(p_ref, slot(*subset(orders[p], mask)), rows, spans[p])

    def fetch(p, mask):
        return pltpu.make_async_copy(mine(p, mask), acc.at[mask, spans[p]], load_sem.at[p, mask])

    sent = []

    def hand_over(*masks):
        for mask in masks:
            for p in pieces:
                sent.append(away(p, mask))
                sent[-1].start()
                if not maker:
                    fetch(p, mask).start()

    sequence = [7, 3, 5, 1, 6, 2, 4, 0]
    if maker:
        cargo.start(0)
        maker.wait()
        for pairs, masks in (((7,), (7,)), ((4, 5, 6), (3, 5, 6)), ((1, 2, 3), (1, 2, 4)), ((0,), (0,))):
            for k in pairs:
                maker.tile(k)
            hand_over(*masks)
    else:
        hand_over(*sequence)
        cargo.start(0)

    def over(p, mask):
        k = (mask & -mask).bit_length() - 1
        return pltpu.make_async_remote_copy(
            src_ref=acc.at[mask, spans[p]], dst_ref=came.at[mask, spans[p]],
            send_sem=send_sem.at[p, mask], recv_sem=recv_sem.at[p, mask],
            device_id=flip(here, orders[p][k]), device_id_type=MESH,
        )

    for mask in sequence:
        for p in pieces:
            away(p, mask).wait_recv()
            if maker:
                acc[mask, spans[p]] = mine(p, mask)[...] + rcore[mask, spans[p]]
            else:
                fetch(p, mask).wait()
                acc[mask, spans[p]] = acc[mask, spans[p]] + rcore[mask, spans[p]]
            if mask & 1:
                sent.append(over(p, mask))
                sent[-1].start()
    cargo.start(1)
    for k in range(3):
        low = 1 << k
        for mask in [b for b in (6, 2, 4, 0) if b & (2 * low - 1) == 0]:
            for p in pieces:
                over(p, mask | low).wait_recv()
                if mask == 0 and k == 2:
                    o_ref[spans[p]] = acc[0, spans[p]].astype(jnp.float32) + came[
                        4, spans[p]
                    ].astype(jnp.float32)
                    continue
                acc[mask, spans[p]] = acc[mask, spans[p]] + came[mask | low, spans[p]]
                if mask & (2 * low):
                    sent.append(over(p, mask))
                    sent[-1].start()
        if k < 2:
            cargo.start(2 + k)
        if k == 1:
            cargo.finish(early=True)
            cargo.start(4)
    for copy in sent:
        copy.wait_send()
    cargo.finish()


def scatter_cube(partial, ident, loads=(), orders=None):
    maker = partial if isinstance(partial, Partial) else None
    total, width = (maker.sources[0].shape[0], maker.width) if maker else partial.shape
    rows = total // MEMBERS
    orders = orders or thirds(rows)
    operands = maker.sources if maker else [partial]
    semaphores = pltpu.SemaphoreType.DMA((len(orders), 8))
    return call(
        functools.partial(scatter_kernel, orders, maker),
        "scatter_cube", ident, Cargo(list(loads)), operands, [pltpu.HBM] * len(operands),
        [jax.ShapeDtypeStruct((rows, width), jnp.float32)], [pltpu.VMEM],
        [pltpu.VMEM((8, rows, width), jnp.bfloat16)] * 3 + [semaphores] * 4
        + (maker.scratch if maker else [semaphores]),
    )


def exchange_kernel(v_ref, o_ref, slots, send_sem, recv_sem):
    here = place()
    greet([flip(here, *names) for names in PEERS])
    copies = []
    for names in PEERS:
        k = slot(*names)
        copies.append(pltpu.make_async_remote_copy(
            src_ref=v_ref, dst_ref=slots.at[k], send_sem=send_sem.at[k], recv_sem=recv_sem.at[k],
            device_id=flip(here, *names), device_id_type=MESH,
        ))
        copies[-1].start()
    for copy in copies:
        copy.wait_recv()
    slots[0] = v_ref[...]
    o_ref[...] = jnp.zeros_like(o_ref)
    for row in range(v_ref.shape[0]):
        kind, mine = divmod(row, MEMBERS)
        terms = [
            slots[k, pl.ds(kind * MEMBERS + SLOT[SLOTS[mine] ^ SLOTS[k]], 1), :]
            for k in range(MEMBERS)
        ]
        while len(terms) > 1:
            terms = [terms[2 * i] + terms[2 * i + 1] for i in range(len(terms) // 2)]
        o_ref[mine, pl.ds(kind, 1), :] = terms[0]
    for copy in copies:
        copy.wait_send()


def sum_cube(values, ident):
    shape = values.shape
    return pl.pallas_call(
        exchange_kernel,
        out_shape=jax.ShapeDtypeStruct((MEMBERS, 8, shape[1]), jnp.float32),
        in_specs=[pl.BlockSpec(memory_space=pltpu.VMEM)],
        out_specs=pl.BlockSpec(memory_space=pltpu.VMEM),
        scratch_shapes=[
            pltpu.VMEM((MEMBERS,) + shape, jnp.float32),
            pltpu.SemaphoreType.DMA((MEMBERS,)),
            pltpu.SemaphoreType.DMA((MEMBERS,)),
        ],
        compiler_params=pltpu.CompilerParams(collective_id=ident, has_side_effects=True),
        cost_estimate=pl.CostEstimate(flops=0, bytes_accessed=20 * MIB, transcendentals=0),
        name="sum_cube",
    )(values)


def rope_tables(positions):
    frequency = theta_base ** (-2.0 * jnp.arange(HD // 2).astype(jnp.float32) / HD)
    angles = positions[:, None] * frequency[None, :]
    cosines, sines = jnp.cos(angles), jnp.sin(angles)
    return jnp.concatenate([cosines, cosines, -sines, sines], axis=1)


def normalize(values, scales):
    inverse = lax.rsqrt(jnp.mean(values * values, axis=-1, keepdims=True) + epsilon)
    return (values * inverse * scales, inverse)


def norm_back(upstream, values, inverse, scales):
    unit_rows = values * inverse
    scaled = upstream * scales
    value_grad = inverse * (
        scaled - unit_rows * jnp.mean(scaled * unit_rows, axis=-1, keepdims=True)
    )
    return (value_grad, jnp.sum(upstream * unit_rows, axis=0))


def contract_last(operand, matrix):
    return lax.dot_general(
        operand, matrix, (((1,), (1,)), ((), ())), preferred_element_type=jnp.float32
    )


def contract_first(operand, matrix):
    return lax.dot_general(
        operand, matrix, (((0,), (0,)), ((), ())), preferred_element_type=jnp.float32
    )


TOGETHER = 8


def turn(values, cos_table, sin_table):
    return values * cos_table + pltpu.roll(values, HD // 2, 1) * sin_table


def project_kernel(x_ref, w_ref, o_ref, sums_out):
    value = jnp.dot(x_ref[...], w_ref[...], preferred_element_type=jnp.float32)
    o_ref[...] = value
    rows = x_ref.shape[0] // TOGETHER
    for block in range(TOGETHER):
        for kind in range(2):
            part = value[block * rows : (block + 1) * rows, kind * HD : (kind + 1) * HD]
            sums_out[pl.ds(kind * MEMBERS + pl.program_id(0) * TOGETHER + block, 1)] = jnp.sum(
                (part * part).T, axis=0, keepdims=True
            )


def rope_of(positions, table):
    place_of = lax.broadcasted_iota(jnp.int32, (positions.shape[0], table.shape[0]), 1)
    chosen = (place_of.astype(jnp.float32) == positions).astype(jnp.float32)
    found = jnp.dot(
        chosen, table, preferred_element_type=jnp.float32, precision=lax.Precision.HIGHEST
    )
    return found[:, :HD], found[:, HD:]


def attend_kernel(width, p_ref, s_ref, b_ref, t_ref, g_ref, *outs):
    q_out, k_out, v_out, qu_out, ku_out, a_out, o_out = outs
    rows = p_ref.shape[0] // TOGETHER
    for block in range(TOGETHER):
        span = pl.ds(block * rows, rows)
        scales = lax.rsqrt(s_ref[block].T / width + epsilon)
        begin = b_ref[block].T[:, 0:1]
        row = lax.broadcasted_iota(jnp.int32, (rows, 1), 0).astype(jnp.float32)
        cos_table, sin_table = rope_of(row - begin, t_ref[...])
        query_unit = p_ref[span, 0:HD] * scales[:, 0:1]
        key_unit = p_ref[span, HD : 2 * HD] * scales[:, 1:2]
        values = p_ref[span, 2 * HD : 3 * HD].astype(jnp.bfloat16)
        queries = turn(query_unit * g_ref[0:1], cos_table, sin_table).astype(jnp.bfloat16)
        keys = turn(key_unit * g_ref[1:2], cos_table, sin_table).astype(jnp.bfloat16)
        scores = contract_last(queries, keys) * (1.0 / math.sqrt(HD))
        column = lax.broadcasted_iota(jnp.int32, scores.shape, 1).astype(jnp.float32)
        scores = jnp.where((column <= row) & (column >= begin), scores, -1e30)
        exponent = jnp.exp(scores - jnp.max(scores, axis=1, keepdims=True))
        attention = exponent / jnp.sum(exponent, axis=1, keepdims=True)
        q_out[span] = queries
        k_out[span] = keys
        v_out[span] = values
        qu_out[span] = query_unit
        ku_out[span] = key_unit
        a_out[span] = attention
        o_out[span] = jnp.dot(
            attention.astype(jnp.bfloat16), values, preferred_element_type=jnp.float32
        ).astype(jnp.bfloat16)


def attend_back_kernel(
    d_ref, q_ref, k_ref, v_ref, qu_ref, ku_ref, a_ref, b_ref, t_ref, g_ref, *outs
):
    qs_out, ks_out, vg_out, dots_out, gains_out = outs
    rows = d_ref.shape[0] // TOGETHER
    step = pl.program_id(0)
    scale = 1.0 / math.sqrt(HD)

    @pl.when(step == 0)
    def _():
        gains_out[...] = jnp.zeros_like(gains_out)

    for block in range(TOGETHER):
        span = pl.ds(block * rows, rows)
        grad, attention = d_ref[span], a_ref[span]
        prob_grad = contract_last(grad, v_ref[span])
        weighed = jnp.sum(attention * prob_grad, axis=1, keepdims=True)
        score_grad = (attention * (prob_grad - weighed)).astype(jnp.bfloat16)
        vg_out[span] = contract_first(attention.astype(jnp.bfloat16), grad).astype(jnp.bfloat16)
        query_grad = jnp.dot(score_grad, k_ref[span], preferred_element_type=jnp.float32) * scale
        key_grad = contract_first(score_grad, q_ref[span]) * scale
        row = lax.broadcasted_iota(jnp.int32, (rows, 1), 0).astype(jnp.float32)
        cos_table, sin_table = rope_of(row - b_ref[block].T[:, 0:1], t_ref[...])
        sin_table = -sin_table
        query_grad = turn(query_grad, cos_table, sin_table)
        key_grad = turn(key_grad, cos_table, sin_table)
        query_unit, key_unit = qu_ref[span], ku_ref[span]
        gains_out[0:1] += jnp.sum(query_grad * query_unit, axis=0, keepdims=True)
        gains_out[1:2] += jnp.sum(key_grad * key_unit, axis=0, keepdims=True)
        query_grad = query_grad * g_ref[0:1]
        key_grad = key_grad * g_ref[1:2]
        qs_out[span] = query_grad
        ks_out[span] = key_grad
        query_dot = jnp.sum((query_grad * query_unit).T, axis=0, keepdims=True)
        key_dot = jnp.sum((key_grad * key_unit).T, axis=0, keepdims=True)
        dots_out[pl.ds(step * TOGETHER + block, 1)] = query_dot
        dots_out[pl.ds(MEMBERS + step * TOGETHER + block, 1)] = key_dot


def project_back_kernel(width, s_ref, t_ref, qu_ref, ku_ref, qs_ref, ks_ref, vg_ref, o_ref):
    rows = qu_ref.shape[0] // TOGETHER
    for block in range(TOGETHER):
        span = pl.ds(block * rows, rows)
        scales = lax.rsqrt(s_ref[block].T / width + epsilon)
        means = t_ref[block].T / width
        query_grad = scales[:, 0:1] * (qs_ref[span] - qu_ref[span] * means[:, 0:1])
        key_grad = scales[:, 1:2] * (ks_ref[span] - ku_ref[span] * means[:, 1:2])
        o_ref[span, 0:HD] = query_grad.astype(jnp.bfloat16)
        o_ref[span, HD : 2 * HD] = key_grad.astype(jnp.bfloat16)
        o_ref[span, 2 * HD : 3 * HD] = vg_ref[span]


def by_blocks(body, name, operands, outs, whole=()):
    total = operands[0].shape[0]
    if operands[0].ndim == 3:
        total = total * operands[0].shape[2]
    span = total // MEMBERS * TOGETHER

    def spec(array):
        shape = array.shape
        if len(shape) == 3:
            return pl.BlockSpec((TOGETHER,) + shape[1:], lambda k: (k, 0, 0))
        if shape[0] == total:
            return pl.BlockSpec((span, shape[1]), lambda k: (k, 0))
        return pl.BlockSpec(shape, lambda k: (0, 0))

    return pl.pallas_call(
        body,
        grid=(MEMBERS // TOGETHER,),
        out_shape=[pltpu.HBM(v.shape, v.dtype) for v in outs],
        in_specs=[
            pl.BlockSpec(v.shape, lambda k: (0, 0)) if n in whole else spec(v)
            for n, v in enumerate(operands)
        ],
        out_specs=[spec(v) for v in outs],
        compiler_params=pltpu.CompilerParams(vmem_limit_bytes=24 * MIB),
        cost_estimate=pl.CostEstimate(
            flops=4 * total * HD * HD, bytes_accessed=8 * MIB, transcendentals=total * HD
        ),
        name=name,
    )(*[in_hbm(v, pltpu.HBM) for v in operands])


def finish_kernel(mine_ref, came_ref, o_ref):
    own = pl.program_id(1) == lax.axis_index("x")
    o_ref[...] = jnp.where(own, mine_ref[...], came_ref[...]).astype(jnp.float32)


def whole_rows(mine, came, parts):
    rows, width = mine.shape
    step = width // parts
    half = pl.BlockSpec((rows, step), lambda p, x: (0, p))
    return pl.pallas_call(
        finish_kernel,
        grid=(parts, 2),
        out_shape=jax.ShapeDtypeStruct((rows, 2 * width), jnp.float32),
        in_specs=[half, half],
        out_specs=pl.BlockSpec((rows, step), lambda p, x: (0, 2 * p + x)),
        compiler_params=pltpu.CompilerParams(vmem_limit_bytes=32 * MIB),
        cost_estimate=pl.CostEstimate(
            flops=0, bytes_accessed=12 * rows * width, transcendentals=0
        ),
        name="whole_rows",
    )(mine, came)


def owners_product(left, right, parts=1, columns=None, **options):
    if left.shape[1] // (lax.axis_size("zh") * SIDES) % 128 == 0:
        return Product(left, right, parts, columns=columns, **options)
    if columns is not None:
        right = right[:, columns[0] : sum(columns)]
    return Owners(contract_first(left, right).astype(jnp.bfloat16), parts, **options)


def heads_are_owners(rows):
    return lax.axis_size("zh") == 2 and rows == HD


def gathered_head_rows(weight):
    full = lax.all_gather(weight, OWNERS, axis=0, tiled=True)
    head = lax.axis_index(("x", "zl", "y", "c"))
    return lax.dynamic_slice_in_dim(full, head * HD, HD, axis=0)


def summed_head_rows(grad_rows, rows):
    head = lax.axis_index(("x", "zl", "y", "c"))
    full = jnp.zeros((MEMBERS * HD, grad_rows.shape[1]), jnp.float32)
    full = lax.dynamic_update_slice_in_dim(full, grad_rows, head * HD, axis=0)
    full = lax.psum(full, EVERY)
    return lax.dynamic_slice_in_dim(full, lax.axis_index(OWNERS) * rows, rows, axis=0)


def silu_grads(hidden_grad, gate_part, up_part):
    sigmoid_gate = jax.nn.sigmoid(gate_part)
    gate_grad = hidden_grad * up_part * sigmoid_gate * (1.0 + gate_part * (1.0 - sigmoid_gate))
    up_grad = hidden_grad * gate_part * sigmoid_gate
    return gate_grad.astype(jnp.bfloat16), up_grad.astype(jnp.bfloat16)


def shards(tokens, w_qkv, w_out, w_gate_up, w_down_t, gains, starts, cotangent):
    count_rows, width = tokens.shape
    owned = gains.shape[0]
    groups = lax.axis_size("zh")
    total = MEMBERS * count_rows
    direct = heads_are_owners(owned)
    local_rows = jnp.arange(count_rows, dtype=jnp.int32)
    seq_begin = lax.cummax(jnp.where(starts == 1, local_rows, 0), axis=0)

    rope_table = rope_tables(local_rows.astype(jnp.float32))
    gain_part = jnp.pad(gains.astype(jnp.float32).T, ((0, 4), (0, 0)))
    begin_part = jnp.broadcast_to(seq_begin.astype(jnp.float32)[None, :], (8, count_rows))
    z_first = (
        (("zl", "x", "y"), 0, count_rows // 2),
        (("zl", "y", "x"), count_rows // 2, count_rows // 2),
    )
    loads = [Few(gain_part, False), Few(begin_part, True), Columns(w_qkv, 3, near=3)]
    if direct:
        loads.append(HeadRows(w_out))
    tokens_all, gain_all, begin_all, qkv_cols, *out_other = gather_cube(
        tokens, 1, loads, z_first
    )
    same = lax.axis_index("x") == lax.axis_index("zh")
    if direct:
        out_rows = jnp.where(same, w_out, out_other[0])
    else:
        out_rows = gathered_head_rows(w_out)
    gain_rows = gain_all[:, :4].transpose(1, 0, 2).reshape(4, width)
    head = lax.axis_index(("x", "zl", "y", "c"))
    head_gains = lax.dynamic_slice_in_dim(gain_rows, head * HD, HD, axis=1)
    def of(width, kind):
        return jax.ShapeDtypeStruct((total, width), kind)

    narrow, wide = of(HD, jnp.bfloat16), of(HD, jnp.float32)
    sums = jax.ShapeDtypeStruct((2 * MEMBERS, count_rows), jnp.float32)
    projected, squares = by_blocks(
        project_kernel, "project", [tokens_all, qkv_cols], [of(3 * HD, jnp.float32), sums],
        whole=(1,),
    )
    squares = sum_cube(squares, 2)
    query_bf, key_bf, value_bf, query_unit, key_unit, attention, attended = by_blocks(
        functools.partial(attend_kernel, width), "attend",
        [projected, squares, begin_all, rope_table, head_gains],
        [narrow, narrow, narrow, wide, wide, wide, narrow],
    )
    x_most = halves(count_rows, "x", "y", "zl")
    x_or_y = (
        (("x", "y", "zl"), 0, count_rows // 2),
        (("y", "x", "zl"), count_rows // 2, count_rows // 2),
    )
    x_last = halves(count_rows, "zl", "y", "x")
    branch, gate_up_cols = scatter_cube(
        Partial(attended, out_rows, False),
        3, [Columns(w_gate_up, 2, near=1)], x_most,
    )
    branch_norm, branch_inv = normalize(branch, gain_rows[2])
    middle = tokens.astype(jnp.float32) + branch_norm
    hidden_bf, gate_up, middle_all, down_cols = gather_cube(
        middle.astype(jnp.bfloat16), 4, [Columns(w_down_t, far=1, near=3)], x_last,
        FeedForward(gate_up_cols, total), eager=True,
    )
    (feed_out,) = scatter_cube(Partial(hidden_bf, down_cols), 5)
    feed_norm, feed_inv = normalize(feed_out, gain_rows[3])
    mixed = (middle + feed_norm).astype(jnp.bfloat16)

    upstream = cotangent.astype(jnp.float32)
    feed_grad, gain_feed = norm_back(upstream, feed_out, feed_inv, gain_rows[3])
    gate_up_bf, middle_part, feed_all = gather_cube(
        feed_grad.astype(jnp.bfloat16), 6, work=FeedBack(down_cols, gate_up_cols, gate_up),
        eager=True,
    )
    feed_width = hidden_bf.shape[1]
    middle_sum, gate_sum, gate_other, up_sum = scatter_cube(
        middle_part, 7,
        [
            owners_product(
                middle_all, gate_up_bf, columns=(0, feed_width), near=1, swap=True, early=True
            ),
            owners_product(
                middle_all, gate_up_bf, columns=(feed_width, feed_width), far=1, near=2
            ),
        ], x_most,
    )
    middle_grad = upstream + middle_sum
    branch_grad, gain_branch = norm_back(middle_grad, branch, branch_inv, gain_rows[2])
    attended_grad, out_grad, down_sum, up_other = gather_cube(
        branch_grad.astype(jnp.bfloat16), 8,
        [
            owners_product(feed_all, hidden_bf, far=1, near=3),
            Whole(up_sum, "x", near=3),
        ], z_first, BranchBack(out_rows, attended),
    )
    query_scaled, key_scaled, value_grad, dots, gain_head = by_blocks(
        attend_back_kernel, "attend_back",
        [
            attended_grad, query_bf, key_bf, value_bf, query_unit, key_unit, attention,
            begin_all, rope_table, head_gains,
        ],
        [
            wide, wide, narrow,
            sums,
            jax.ShapeDtypeStruct((8, HD), jnp.float32),
        ],
    )
    dots = sum_cube(dots, 9)
    (projected_bf,) = by_blocks(
        functools.partial(project_back_kernel, width), "project_back",
        [squares, dots, query_unit, key_unit, query_scaled, key_scaled, value_grad],
        [of(3 * HD, jnp.bfloat16)],
    )

    gain_terms = jnp.concatenate(
        [
            lax.dynamic_update_slice_in_dim(
                jnp.zeros((2, width), jnp.float32), gain_head[:2], head * HD, axis=1
            ),
            jnp.stack([gain_branch, gain_feed]),
        ]
    )
    lanes = -(-owned // 128) * 128
    gain_terms = jnp.pad(
        gain_terms.reshape(4, groups * SIDES, owned).transpose(1, 0, 2),
        ((0, 0), (0, 4), (0, lanes - owned)),
    ).reshape(groups * SIDES * 8, lanes)
    loads = [
        owners_product(tokens_all, projected_bf, 3, swap=True, near=1, early=True),
        Owners(gain_terms, swap=True, fold=True, early=True),
        FinalRows((gate_sum, gate_other), (up_sum, up_other)),
        Whole(down_sum, "x", near=1),
    ]
    if direct:
        loads.append(HeadSums(out_grad, near=1, early=True))
    (
        tokens_sum, qkv_sum, qkv_other, gain_sum, gain_other, grad_gate_up, down_other, *out_both
    ) = scatter_cube(
        Partial(projected_bf, qkv_cols), 10, loads, x_or_y
    )
    grad_tokens = middle_grad + tokens_sum
    if direct:
        first, second = (jnp.where(same, out_both[k], out_both[1 - k]) for k in range(2))
        grad_out = jnp.concatenate([first, second], axis=0).astype(jnp.float32)
    else:
        grad_out = summed_head_rows(out_grad.astype(jnp.float32), owned)
    grad_qkv = whole_rows(qkv_sum, qkv_other, 3)
    grad_down_t = whole_rows(down_sum, down_other, 1)
    grad_gains = (gain_sum + gain_other)[:4, :owned].T
    return (mixed, grad_tokens, grad_qkv, grad_out, grad_gate_up, grad_down_t, grad_gains)


def solution(mesh):
    sizes = dict(mesh.shape)
    groups = sizes["fsdp"] // SIDES
    finer = Mesh(mesh.devices.reshape(2, groups, 2, 2, 2), EVERY)
    return jax.shard_map(
        shards,
        mesh=finer,
        in_specs=(
            P(EVERY, None),
            P(OWNERS, None),
            P(OWNERS, None),
            P(OWNERS, None),
            P(OWNERS, None),
            P(OWNERS, None),
            P(EVERY),
            P(EVERY, None),
        ),
        out_specs=(
            P(EVERY, None),
            P(EVERY, None),
            P(OWNERS, None),
            P(OWNERS, None),
            P(OWNERS, None),
            P(OWNERS, None),
            P(OWNERS, None),
        ),
        check_vma=False,
    )
```

```python
import functools
import math

import jax
import jax.numpy as jnp
from jax import lax
from jax.experimental import pallas as pl
from jax.experimental.pallas import tpu as pltpu
from jax.sharding import Mesh, PartitionSpec as P

HD = 128

epsilon = 1e-06
theta_base = 500000.0

OWNERS = ("zh", "zl", "y", "c")
EVERY = ("x", "zh", "zl", "y", "c")
MEMBERS = 16
SIDES = 8
SIDE_BITS = {"zl": 4, "y": 2, "c": 1}
BITS = {"x": 8, "zl": 4, "y": 2, "c": 1}
SLOTS = [
    frozenset(names + core)
    for names in (
        (), ("x",), ("y",), ("zl",), ("x", "y"), ("x", "zl"), ("y", "zl"), ("x", "y", "zl"),
    )
    for core in ((), ("c",))
]
SLOT = {names: k for k, names in enumerate(SLOTS)}
MESH = pl.DeviceIdType.MESH
MIB = 1 << 20


def thirds(rows):
    unit = rows // 8
    return (
        (("x", "y", "zl"), 0, 3 * unit),
        (("y", "zl", "x"), 3 * unit, 3 * unit),
        (("zl", "x", "y"), 6 * unit, 2 * unit),
    )


def halves(rows, *order):
    return ((order, 0, rows // 2), (order, rows // 2, rows // 2))


PEERS = [tuple(n for n in BITS if m & BITS[n]) for m in range(1, MEMBERS)]
SIDE_PEERS = [tuple(n for n in SIDE_BITS if m & SIDE_BITS[n]) for m in range(SIDES)]


def slot(*names):
    return SLOT[frozenset(names)]


def place():
    return {name: lax.axis_index(name) for name in EVERY}


def flip(here, *names):
    return {name: 1 - here[name] for name in names}


def with_bits(here, names, bits):
    index = 0
    for name, bit in bits.items():
        index = index + bit * ((1 - here[name]) if name in names else here[name])
    return index


def subset(order, mask):
    return tuple(name for k, name in enumerate(order) if mask >> k & 1)


def greet(devices):
    barrier = pltpu.get_barrier_semaphore()
    for device in devices:
        pl.semaphore_signal(barrier, inc=1, device_id=device, device_id_type=MESH)
    pl.semaphore_wait(barrier, len(devices))


def owner_at(here, groups, step, names):
    device = flip(here, *names)
    if step:
        device["zh"] = lax.rem(here["zh"] + step, groups)
    return device


def at(start, size):
    return pl.ds(pl.multiple_of(start, size), size)


class Load:
    space = pltpu.HBM
    parts = 1

    def __init__(self, source, far=0, near=0, early=False):
        self.sources = [source]
        self.stages = (near, far)
        self.early = early
        self.groups = lax.axis_size("zh")

    def spaces(self):
        return [self.space] * len(self.sources), [self.space] * len(self.outs)

    def semaphores(self):
        count = len(self.moves())
        return [pltpu.SemaphoreType.DMA((count,)), pltpu.SemaphoreType.DMA((count,))]

    def scratch(self):
        return self.semaphores()

    def moves(self):
        return [
            ((step, names), part)
            for step in range(self.groups)
            for names in SIDE_PEERS
            for part in range(self.parts)
        ]

    def reached(self):
        return {peer for peer, _ in self.moves() if peer != (0, ())}

    def around(self, here, step, names):
        there = lax.rem(here["zh"] + step, self.groups)
        whence = lax.rem(here["zh"] + self.groups - step, self.groups)
        mine, other = with_bits(here, (), SIDE_BITS), with_bits(here, names, SIDE_BITS)
        return mine, other, there, whence

    def bind(self, here, sources, targets, scratch):
        self.here, self.src, self.dst = here, sources, targets
        self.send, self.recv, *self.more = scratch
        self.copies = []
        for index, ((step, names), part) in enumerate(self.moves()):
            source, target, landing = self.views(here, step, names, part)
            stage = self.stages[1 if step else 0]
            if not step and not names:
                copy = pltpu.make_async_copy(source, target, self.send.at[index])
                self.copies.append((stage, copy, None, (step, names)))
                continue
            copy = pltpu.make_async_remote_copy(
                src_ref=source, dst_ref=target,
                send_sem=self.send.at[index], recv_sem=self.recv.at[index],
                device_id=owner_at(here, self.groups, step, names), device_id_type=MESH,
            )
            landed = pltpu.make_async_copy(landing, landing, self.recv.at[index])
            self.copies.append((stage, copy, landed, (step, names)))

    def start(self, stage):
        for when, copy, _, _ in self.copies:
            if when == stage:
                copy.start()

    def land(self):
        for _, copy, landed, _ in self.copies:
            (copy if landed is None else landed).wait()

    def finish(self):
        pass

    def leave(self):
        for _, copy, landed, _ in self.copies:
            if landed is not None:
                copy.wait_send()


class Columns(Load):
    def __init__(self, source, parts=1, **stages):
        super().__init__(source, **stages)
        self.parts = parts
        self.rows = source.shape[0]
        self.piece = source.shape[1] // (parts * MEMBERS)
        shape = (self.groups * SIDES * self.rows, parts * self.piece)
        self.outs = [jax.ShapeDtypeStruct(shape, source.dtype)]

    def views(self, here, step, names, part):
        mine, other, _, whence = self.around(here, step, names)
        first = part * MEMBERS + here["x"] * SIDES + other
        columns = pl.ds(part * self.piece, self.piece)
        return (
            self.src[0].at[:, at(first * self.piece, self.piece)],
            self.dst[0].at[at((here["zh"] * SIDES + mine) * self.rows, self.rows), columns],
            self.dst[0].at[at((whence * SIDES + other) * self.rows, self.rows), columns],
        )


class Few(Load):
    space = pltpu.VMEM

    def __init__(self, source, cube):
        super().__init__(source)
        self.cube = cube
        count = MEMBERS if cube else self.groups * SIDES
        self.outs = [jax.ShapeDtypeStruct((count,) + source.shape, source.dtype)]

    def moves(self):
        if self.cube:
            return [((0, names), 0) for names in [()] + PEERS]
        return super().moves()

    def views(self, here, step, names, part):
        if self.cube:
            spot = self.dst[0].at[slot(*names)]
            return self.src[0], spot, spot
        mine, other, _, whence = self.around(here, step, names)
        return (
            self.src[0],
            self.dst[0].at[here["zh"] * SIDES + mine],
            self.dst[0].at[whence * SIDES + other],
        )


class Whole(Load):
    def __init__(self, source, axis, **stages):
        super().__init__(source, **stages)
        self.axis = axis
        self.outs = [jax.ShapeDtypeStruct(source.shape, source.dtype)]

    def moves(self):
        return [((0, ("x",)) if self.axis == "x" else (1, ()), 0)]

    def views(self, here, step, names, part):
        return self.src[0], self.dst[0], self.dst[0]


class Swap:
    def swap_scratch(self):
        return [pltpu.SemaphoreType.DMA((3,))]

    def give(self, total, sems):
        self.kept = pltpu.make_async_copy(total, self.dst[0], sems.at[0])
        self.kept.start()
        self.given = None
        if len(self.outs) > 1:
            self.given = pltpu.make_async_remote_copy(
                src_ref=total, dst_ref=self.dst[1], send_sem=sems.at[1], recv_sem=sems.at[2],
                device_id=flip(self.here, "x"), device_id_type=MESH,
            )
            self.given.start()

    def given_wait(self):
        self.kept.wait()
        if self.given is not None:
            self.given.wait()


class Owners(Load, Swap):
    def __init__(self, source, parts=1, swap=False, fold=False, **stages):
        super().__init__(source, **stages)
        self.setup(source.shape[0], source.shape[1], source.dtype, parts, swap, fold)

    def setup(self, depth, width, kind, parts, swap, fold):
        self.parts = parts
        self.fold = fold
        self.kind = kind
        self.rows = depth // (self.groups * SIDES)
        self.piece = width // parts
        self.wide = parts * SIDES * self.piece
        total = (self.rows, self.piece if fold else self.wide)
        self.total = total
        self.outs = [jax.ShapeDtypeStruct(total, kind)] * (1 + swap)
        self.swap = swap

    def reached(self):
        return super().reached() | ({(0, ("x",))} if self.swap else set())

    def spaces(self):
        return [pltpu.VMEM if self.fold else pltpu.HBM] * len(self.sources), [pltpu.HBM] * len(self.outs)

    def scratch(self):
        return self.semaphores() + self.swap_scratch() + [
            pltpu.VMEM((self.groups, self.rows, self.wide), self.kind),
            pltpu.VMEM(self.total, self.kind),
        ]

    def views(self, here, step, names, part):
        mine, other, there, whence = self.around(here, step, names)
        terms = self.more[1]
        return (
            self.slice_of(there * SIDES + other, part),
            terms.at[here["zh"], :, at((part * SIDES + mine) * self.piece, self.piece)],
            terms.at[whence, :, at((part * SIDES + other) * self.piece, self.piece)],
        )

    def slice_of(self, target, part):
        return self.src[0].at[
            at(target * self.rows, self.rows), pl.ds(part * self.piece, self.piece)
        ]

    def finish(self):
        sems, terms, total = self.more[:3]
        step = self.piece if self.fold else min(512, self.wide)

        def add(start):
            value = terms[0, :, pl.ds(start, step)].astype(jnp.float32)
            for group in range(1, self.groups):
                value = value + terms[group, :, pl.ds(start, step)].astype(jnp.float32)
            return value

        if self.fold:
            value = add(0)
            for side in range(1, SIDES):
                value = value + add(side * step)
            total[...] = value
        else:

            @pl.loop(0, self.wide // step)
            def _(k):
                start = pl.multiple_of(k * step, step)
                total[:, pl.ds(start, step)] = add(start).astype(total.dtype)

        self.give(total, sems)

    def leave(self):
        super().leave()
        self.given_wait()


class Product(Owners):
    def __init__(self, left, right, parts=1, swap=False, columns=None, **stages):
        Load.__init__(self, left, **stages)
        self.sources = [left, right]
        self.columns = columns or (0, right.shape[1])
        self.setup(left.shape[1], self.columns[1], jnp.bfloat16, parts, swap, False)

    def scratch(self):
        depth, width = self.sources[0].shape[0], self.columns[1]
        return super().scratch() + [
            pltpu.VMEM((2, depth, 2 * self.rows), jnp.bfloat16),
            pltpu.VMEM((depth, width), jnp.bfloat16),
            pltpu.VMEM((self.groups * SIDES * self.rows, width), jnp.bfloat16),
            pltpu.SemaphoreType.DMA((3,)),
        ]

    def slice_of(self, target, part):
        return self.more[5].at[
            at(target * self.rows, self.rows), pl.ds(part * self.piece, self.piece)
        ]

    def tiles(self):
        order = [
            (step, names)
            for step in reversed(range(self.groups))
            for names in SIDE_PEERS
            if "c" not in names
        ]
        return order

    def first_row(self, step, names):
        _, other, there, _ = self.around(self.here, step, names)
        return (there * SIDES + (other // 2) * 2) * self.rows

    def fetch(self, k):
        step, names = self.tiles()[k]
        left = self.src[0].at[:, at(self.first_row(step, names), 2 * self.rows)]
        return pltpu.make_async_copy(left, self.more[3].at[k % 2], self.more[6].at[k % 2])

    def begin(self):
        right = self.src[1].at[:, pl.ds(*self.columns)]
        self.right = pltpu.make_async_copy(right, self.more[4], self.more[6].at[2])
        self.right.start()
        self.fetch(0).start()
        self.fetch(1).start()

    def start(self, stage):
        tiles = self.tiles()
        _, _, _, lefts, right, result, _ = self.more
        for k, (step, names) in enumerate(tiles):
            if self.stages[1 if step else 0] != stage:
                continue
            if k == 0:
                self.right.wait()
            self.fetch(k).wait()
            rows = at(self.first_row(step, names), 2 * self.rows)
            width = self.columns[1]
            left = lefts[k % 2]
            for column in range(0, width, 256):
                columns = pl.ds(column, min(256, width - column))
                result[rows, columns] = lax.dot_general(
                    left, right[:, columns], (((0,), (0,)), ((), ())),
                    preferred_element_type=jnp.float32,
                ).astype(jnp.bfloat16)
            if k + 2 < len(tiles):
                self.fetch(k + 2).start()
            for _, copy, _, peer in self.copies:
                if peer in ((step, names), (step, names + ("c",))):
                    copy.start()


class HeadRows(Load):
    def __init__(self, source):
        super().__init__(source)
        self.outs = [jax.ShapeDtypeStruct(source.shape, source.dtype)]

    def moves(self):
        return [((1, ()), 0), ((1, ("x",)), 0)]

    def bind(self, here, sources, targets, scratch):
        (source,), (target,), (send, recv) = sources, targets, scratch
        half = source.shape[0] // 2
        self.home = here["x"] == here["zh"]
        mine = jnp.where(self.home, 0, 1)
        rows = at(mine * half, half)
        self.copy = pltpu.make_async_remote_copy(
            src_ref=source.at[rows], dst_ref=target.at[rows],
            send_sem=send.at[0], recv_sem=recv.at[mine],
            device_id={"x": here["zh"], "zh": 1 - here["zh"]}, device_id_type=MESH,
        )
        spots_here = [target.at[pl.ds(k * half, half)] for k in range(2)]
        self.landed = [
            pltpu.make_async_copy(spot, spot, recv.at[k]) for k, spot in enumerate(spots_here)
        ]

    def start(self, stage):
        if stage == 0:
            self.copy.start()

    def land(self):
        @pl.when(jnp.logical_not(self.home))
        def _():
            for landed in self.landed:
                landed.wait()

    def leave(self):
        self.copy.wait_send()


class HeadSums(Load, Swap):
    def __init__(self, source, **stages):
        super().__init__(source, **stages)
        rows, width = source.shape
        self.half = jax.ShapeDtypeStruct((rows // 2, width), source.dtype)
        self.outs = [self.half] * 2

    def spaces(self):
        return [pltpu.VMEM], [pltpu.HBM] * 2

    def moves(self):
        return [((1, ()), 0), ((0, ("x",)), 0), ((0, ("x",)), 0)]

    def scratch(self):
        return self.semaphores() + self.swap_scratch() + [
            pltpu.VMEM((3,) + self.half.shape, jnp.bfloat16),
            pltpu.VMEM(self.half.shape, jnp.bfloat16),
        ]

    def bind(self, here, sources, targets, scratch):
        self.here, self.dst = here, targets
        (self.source,) = sources
        send, recv, self.sems, self.terms, self.total = scratch
        self.home = here["x"] == here["zh"]
        rows = self.half.shape[0]

        def copy(source, term, k, device):
            return pltpu.make_async_remote_copy(
                src_ref=source, dst_ref=self.terms.at[term],
                send_sem=send.at[k], recv_sem=recv.at[term],
                device_id=device, device_id_type=MESH,
            )

        first, second = (self.source.at[pl.ds(k * rows, rows)] for k in range(2))
        across = {"zh": 1 - here["zh"]}
        self.near = copy(second, 0, 0, flip(here, "x"))
        self.relay = copy(self.terms.at[2], 1, 1, across)
        self.far = copy(first, 1, 1, across)
        self.hand = copy(second, 2, 0, flip(here, "x"))

    def start(self, stage):
        if stage == self.stages[1]:

            @pl.when(self.home)
            def _():
                self.near.start()

            @pl.when(jnp.logical_not(self.home))
            def _():
                self.hand.start()
                self.far.start()

        if stage == self.stages[0]:

            @pl.when(self.home)
            def _():
                self.hand.wait_recv()
                self.relay.start()

    def land(self):
        self.far.wait_recv()

        @pl.when(jnp.logical_not(self.home))
        def _():
            self.near.wait_recv()

    def finish(self):
        rows = self.half.shape[0]

        @pl.when(self.home)
        def _():
            self.terms[0] = self.source[pl.ds(0, rows)]

        self.total[...] = (
            self.terms[0].astype(jnp.float32) + self.terms[1].astype(jnp.float32)
        ).astype(jnp.bfloat16)
        self.give(self.total, self.sems)

    def leave(self):
        self.near.wait_send()
        self.far.wait_send()
        self.given_wait()


class FinalRows(Load):
    def __init__(self, *pairs, near=4):
        super().__init__(None, near=near)
        self.sources = [half for pair in pairs for half in pair]
        rows, self.width = pairs[0][0].shape
        self.step = min(2048, self.width)
        self.outs = [jax.ShapeDtypeStruct((rows, len(self.sources) * self.width), jnp.float32)]

    def moves(self):
        return []

    def scratch(self):
        rows = self.outs[0].shape[0]
        return [
            pltpu.VMEM((2, rows, self.step), jnp.bfloat16),
            pltpu.VMEM((2, rows, self.step), jnp.float32),
            pltpu.SemaphoreType.DMA((4,)),
        ]

    def bind(self, here, sources, targets, scratch):
        self.here, self.src, self.dst = here, sources, targets
        self.halves, self.wholes, self.sems = scratch

    def start(self, stage):
        if stage != self.stages[0]:
            return
        x = self.here["x"]
        steps = [
            (k, start) for k in range(len(self.sources)) for start in range(0, self.width, self.step)
        ]

        def fetch(n):
            k, start = steps[n]
            return pltpu.make_async_copy(
                self.src[k].at[:, pl.ds(start, self.step)], self.halves.at[n % 2],
                self.sems.at[n % 2],
            )

        def store(n):
            k, start = steps[n]
            half = x if k % 2 == 0 else 1 - x
            first = (2 * (k // 2) + half) * self.width + start
            return pltpu.make_async_copy(
                self.wholes.at[n % 2], self.dst[0].at[:, at(first, self.step)],
                self.sems.at[2 + n % 2],
            )

        fetch(0).start()
        for n in range(len(steps)):
            if n + 1 < len(steps):
                fetch(n + 1).start()
            fetch(n).wait()
            if n >= 2:
                store(n - 2).wait()
            self.wholes[n % 2] = self.halves[n % 2].astype(jnp.float32)
            store(n).start()
        for n in range(max(0, len(steps) - 2), len(steps)):
            store(n).wait()

    def land(self):
        pass

    def leave(self):
        pass


class Cargo:
    def __init__(self, loads):
        self.loads = loads
        self.sources = [s for load in loads for s in load.sources]
        self.outs = [o for load in loads for o in load.outs]
        self.in_specs = [pl.BlockSpec(memory_space=s) for load in loads for s in load.spaces()[0]]
        self.out_specs = [pl.BlockSpec(memory_space=s) for load in loads for s in load.spaces()[1]]
        self.scratch = [s for load in loads for s in load.scratch()]

    def bind(self, here, sources, targets, scratch):
        sources, targets, scratch = list(sources), list(targets), list(scratch)

        def take(refs, count):
            taken = refs[:count]
            del refs[:count]
            return taken

        for load in self.loads:
            load.bind(
                here,
                take(sources, len(load.sources)),
                take(targets, len(load.outs)),
                take(scratch, len(load.scratch())),
            )
            if hasattr(load, "begin"):
                load.begin()

    def greet(self, here, names):
        reached = {(0, n) for n in names}
        for load in self.loads:
            reached |= load.reached()
        groups = lax.axis_size("zh")
        greet([owner_at(here, groups, step, n) for step, n in sorted(reached)])

    def start(self, stage):
        for load in self.loads:
            load.start(stage)

    def finish(self, early=False):
        for load in self.loads:
            if load.early == early:
                load.land()
                load.finish()
        if not early:
            for load in self.loads:
                load.leave()


class Work:
    operands = ()

    def __init__(self, *sources):
        self.sources = list(sources)

    def bind(self, sources, targets, scratch):
        self.src, self.dst, self.more = list(sources), list(targets), list(scratch)
        self.copies = []

    def begin(self):
        pass

    def keep(self, copy):
        self.copies.append(copy)
        copy.start()

    def close(self):
        for copy in self.copies:
            copy.wait()


class FeedForward(Work):
    def __init__(self, gate_up_cols, total):
        super().__init__(gate_up_cols)
        width, both = gate_up_cols.shape
        self.half, self.pair = both // 2, 2 * total // MEMBERS
        self.in_spaces = [pltpu.HBM]
        self.outs = [
            jax.ShapeDtypeStruct((total, self.half), jnp.bfloat16),
            jax.ShapeDtypeStruct((total, both), jnp.float32),
            jax.ShapeDtypeStruct((total, width), jnp.bfloat16),
        ]
        self.out_spaces = [pltpu.HBM, pltpu.HBM, pltpu.HBM]
        self.scratch = [
            pltpu.VMEM((2, self.pair, both), jnp.float32),
            pltpu.SemaphoreType.DMA((3, SIDES)),
            pltpu.VMEM(gate_up_cols.shape, gate_up_cols.dtype),
            pltpu.SemaphoreType.DMA(()),
            pltpu.VMEM((total, self.half), jnp.bfloat16),
        ]

    def begin(self):
        self.load = pltpu.make_async_copy(self.src[0], self.more[2], self.more[3])
        self.load.start()

    def tile(self, k, rows_ref):
        (hidden_out, gate_up, rows_out), (staged, sems, cols, _, hidden) = self.dst, self.more
        if k == 0:
            self.load.wait()
        rows = pl.ds(k * self.pair, self.pair)
        self.keep(pltpu.make_async_copy(rows_ref, rows_out.at[rows], sems.at[0, k]))
        if k >= 2:
            self.last[k - 2].wait()
        value = rows_ref[...]
        for start in range(0, self.half, 256):
            columns = pl.ds(start, 256)
            others = pl.ds(self.half + start, 256)
            gate = jnp.dot(value, cols[:, columns], preferred_element_type=jnp.float32)
            up = jnp.dot(value, cols[:, others], preferred_element_type=jnp.float32)
            staged[k % 2, :, columns] = gate
            staged[k % 2, :, others] = up
            hidden[rows, columns] = (gate * jax.nn.sigmoid(gate) * up).astype(jnp.bfloat16)
        self.keep(pltpu.make_async_copy(hidden.at[rows], hidden_out.at[rows], sems.at[2, k]))
        copy = pltpu.make_async_copy(staged.at[k % 2], gate_up.at[rows], sems.at[1, k])
        copy.start()
        if k == 0:
            self.last = []
        self.last.append(copy)

    def close(self):
        super().close()
        for copy in self.last[-2:]:
            copy.wait()


class FeedBack(Work):
    def __init__(self, down_cols, gate_up_cols, gate_up):
        super().__init__(down_cols, gate_up_cols, gate_up)
        total, both = gate_up.shape
        width = down_cols.shape[0]
        self.half, self.width, self.pair = both // 2, width, 2 * total // MEMBERS
        self.in_spaces = [pltpu.HBM] * 3
        self.outs = [
            jax.ShapeDtypeStruct((total, both), jnp.bfloat16),
            jax.ShapeDtypeStruct((total, width), jnp.bfloat16),
            jax.ShapeDtypeStruct((total, width), jnp.bfloat16),
        ]
        self.out_spaces = [pltpu.HBM, pltpu.HBM, pltpu.HBM]
        self.scratch = [
            pltpu.VMEM((2, self.pair, both), jnp.float32),
            pltpu.SemaphoreType.DMA((4, SIDES)),
            pltpu.VMEM(down_cols.shape, down_cols.dtype),
            pltpu.VMEM(gate_up_cols.shape, gate_up_cols.dtype),
            pltpu.SemaphoreType.DMA((2,)),
            pltpu.VMEM((total, both), jnp.bfloat16),
            pltpu.VMEM((total, width), jnp.bfloat16),
        ]

    def fetch(self, k):
        rows = pl.ds(k * self.pair, self.pair)
        return pltpu.make_async_copy(
            self.src[2].at[rows], self.more[0].at[k % 2], self.more[1].at[0, k]
        )

    def begin(self):
        self.loads = [
            pltpu.make_async_copy(self.src[i], self.more[2 + i], self.more[4].at[i])
            for i in range(2)
        ]
        for copy in self.loads:
            copy.start()
        self.fetch(0).start()
        self.fetch(1).start()

    def tile(self, k, rows_ref):
        grads_out, part_out, rows_out = self.dst
        saved, sems, down, cols, _, grads, part = self.more
        if k == 0:
            for copy in self.loads:
                copy.wait()
        rows = pl.ds(k * self.pair, self.pair)
        self.keep(pltpu.make_async_copy(rows_ref, rows_out.at[rows], sems.at[1, k]))
        self.fetch(k).wait()
        value = rows_ref[...]
        for start in range(0, self.half, 256):
            columns = pl.ds(start, 256)
            others = pl.ds(self.half + start, 256)
            hidden_grad = jnp.dot(value, down[:, columns], preferred_element_type=jnp.float32)
            gate_bf, up_bf = silu_grads(
                hidden_grad, saved[k % 2, :, columns], saved[k % 2, :, others]
            )
            grads[rows, columns] = gate_bf
            grads[rows, others] = up_bf
        if k + 2 < SIDES:
            self.fetch(k + 2).start()
        self.keep(pltpu.make_async_copy(grads.at[rows], grads_out.at[rows], sems.at[2, k]))
        both = grads[rows]
        for start in range(0, self.width, 256):
            columns = pl.ds(start, 256)
            part[rows, columns] = contract_last(both, cols[columns, :]).astype(jnp.bfloat16)
        self.keep(pltpu.make_async_copy(part.at[rows], part_out.at[rows], sems.at[3, k]))


class BranchBack(Work):
    def __init__(self, out_rows, attended):
        super().__init__(out_rows, attended)
        total, width = attended.shape[0], out_rows.shape[1]
        self.width, self.pair = width, 2 * total // MEMBERS
        self.in_spaces = [pltpu.VMEM, pltpu.VMEM]
        self.outs = [
            jax.ShapeDtypeStruct((total, HD), jnp.bfloat16),
            jax.ShapeDtypeStruct((HD, width), jnp.bfloat16),
        ]
        self.out_spaces = [pltpu.VMEM, pltpu.VMEM]
        self.scratch = [pltpu.VMEM((HD, width), jnp.float32)]

    def tile(self, k, rows_ref):
        (out_rows, attended), (grad, _), (total,) = self.src, self.dst, self.more
        rows = pl.ds(k * self.pair, self.pair)
        value = rows_ref[...]
        grad[rows] = contract_last(value, out_rows[...]).astype(jnp.bfloat16)
        for start in range(0, self.width, 512):
            columns = pl.ds(start, 512)
            term = contract_first(attended[rows], rows_ref[:, columns])
            total[:, columns] = term if k == 0 else total[:, columns] + term

    def close(self):
        self.dst[1][...] = self.more[0][...].astype(jnp.bfloat16)


GATHER_STAGES = (0, 1, 2, 3)
NEAR = [("x",), ("zl",), ("y",), ("c",)]


def room_for(*held):
    sizes = [math.prod(s.shape) * jnp.dtype(s.dtype).itemsize for s in held]
    return sum(sizes) + 8 * MIB


def only_vmem(arrays, spaces):
    return [a for a, space in zip(arrays, spaces) if space == pltpu.VMEM]


def in_hbm(value, space):
    return pltpu.with_memory_space_constraint(value, pltpu.HBM) if space == pltpu.HBM else value


def call(body, name, ident, cargo, operands, spaces, outs, out_spaces, scratch):
    cargo_in = [space for load in cargo.loads for space in load.spaces()[0]]
    operands = [in_hbm(v, space) for v, space in zip(operands, spaces)]
    sources = [in_hbm(v, space) for v, space in zip(cargo.sources, cargo_in)]
    cargo_out = [space for load in cargo.loads for space in load.spaces()[1]]
    kept = [
        space(out.shape, out.dtype)
        for out, space in zip(list(outs) + cargo.outs, list(out_spaces) + cargo_out)
    ]
    held = only_vmem(operands, spaces) + only_vmem(outs, out_spaces)
    held += only_vmem(cargo.sources, cargo_in)
    held += [s for s in scratch + cargo.scratch if s.memory_space == pltpu.VMEM]
    return pl.pallas_call(
        functools.partial(body, cargo),
        out_shape=kept,
        in_specs=[pl.BlockSpec(memory_space=s) for s in spaces] + cargo.in_specs,
        out_specs=[pl.BlockSpec(memory_space=s) for s in out_spaces] + cargo.out_specs,
        scratch_shapes=scratch + cargo.scratch,
        compiler_params=pltpu.CompilerParams(
            collective_id=ident, has_side_effects=True, vmem_limit_bytes=room_for(*held)
        ),
        cost_estimate=pl.CostEstimate(flops=0, bytes_accessed=100 * MIB, transcendentals=0),
        name=name,
    )(*operands, *sources)


def take(refs, count):
    taken = refs[:count]
    del refs[:count]
    return taken


def gather_kernel(orders, work, eager, cargo, x_ref, *refs):
    refs = list(refs)
    work_in = take(refs, len(work.sources)) if work else []
    sources = take(refs, len(cargo.sources))
    work_out = take(refs, len(work.outs) if work else 1)
    targets = take(refs, len(cargo.outs))
    send_sem, recv_sem, core_send, core_recv, own_sem = take(refs, 5)
    here = place()
    spans = [pl.ds(r0, size) for _, r0, size in orders]
    orders = [o for o, _, _ in orders]
    pieces = range(len(orders))
    if work:
        (o_ref,) = take(refs, 1)
        work.bind(work_in, work_out, take(refs, len(work.scratch)))
        work.begin()
    else:
        o_ref = work_out[0]
    rows, width = x_ref.shape
    cargo.bind(here, sources, targets, refs)
    cargo.greet(here, NEAR)
    own = pltpu.make_async_copy(x_ref, spots(o_ref, slice(0, 1), rows), own_sem)

    def spot(p, *names):
        return spots(o_ref, slot(*names), rows, spans[p])

    def source(p, mask):
        return spot(p, *subset(orders[p], mask)) if mask else x_ref.at[spans[p]]

    def over(p, mask, k):
        whole = mask | 1 << k
        return pltpu.make_async_remote_copy(
            src_ref=source(p, mask), dst_ref=spot(p, *subset(orders[p], whole)),
            send_sem=send_sem.at[p, whole], recv_sem=recv_sem.at[p, whole],
            device_id=flip(here, orders[p][k]), device_id_type=MESH,
        )

    def across(p, mask):
        return pltpu.make_async_remote_copy(
            src_ref=source(p, mask), dst_ref=spot(p, "c", *subset(orders[p], mask)),
            send_sem=core_send.at[p, mask], recv_sem=core_recv.at[p, mask],
            device_id=flip(here, "c"), device_id_type=MESH,
        )

    sent = []

    def pass_on(mask):
        for p in pieces:
            if mask:
                landing = spot(p, *subset(orders[p], mask))
                pltpu.make_async_copy(landing, landing, recv_sem.at[p, mask]).wait()
            for k in range(mask.bit_length(), 3):
                sent.append(over(p, mask, k))
                sent[-1].start()
        for p in pieces:
            sent.append(across(p, mask))
            sent[-1].start()
        if mask == 0:
            own.start()
        if mask in GATHER_STAGES:
            cargo.start(GATHER_STAGES.index(mask))

    def from_core(*masks):
        for mask in masks:
            for p in pieces:
                landing = spot(p, "c", *subset(orders[p], mask))
                pltpu.make_async_copy(landing, landing, core_recv.at[p, mask]).wait()

    def tiles(*numbers):
        for k in numbers:
            work.tile(k, o_ref.at[pl.ds(2 * rows * k, 2 * rows)])

    if eager:
        pass_on(0)
        own.wait()
        from_core(0)
        tiles(0)
        for mask in (1, 2, 3, 4):
            pass_on(mask)
        from_core(1, 2, 4)
        tiles(1, 2)
        pass_on(5)
        tiles(3)
        pass_on(6)
        from_core(3, 5, 6)
        tiles(4)
        pass_on(7)
        tiles(5, 6)
        from_core(7)
        tiles(7)
    else:
        for mask in range(8):
            pass_on(mask)
        from_core(*range(8))
        own.wait()
        if work:
            tiles(*range(SIDES))
    for copy in sent:
        copy.wait_send()
    if work:
        work.close()
    cargo.finish()


def spots(ref, index, rows, span=None):
    if isinstance(index, slice):
        return ref.at[pl.ds(index.start * rows, rows)]
    if span is None:
        return ref.at[pl.ds(index * rows, rows)]
    return ref.at[pl.ds(index * rows + span.start, span.size)]


def gather_cube(block, ident, loads=(), orders=None, work=None, eager=False):
    rows, width = block.shape
    orders = orders or thirds(rows)
    whole = jax.ShapeDtypeStruct((MEMBERS * rows, width), block.dtype)
    scratch = [pltpu.SemaphoreType.DMA((len(orders), 8))] * 4 + [pltpu.SemaphoreType.DMA(())]
    if work:
        operands, spaces = [block] + work.sources, [pltpu.HBM] + work.in_spaces
        outs, out_spaces = work.outs, work.out_spaces
        scratch += [pltpu.VMEM(whole.shape, whole.dtype)] + work.scratch
    else:
        operands, spaces, outs, out_spaces = [block], [pltpu.HBM], [whole], [pltpu.HBM]
    return call(
        functools.partial(gather_kernel, orders, work, eager),
        "gather_cube", ident, Cargo(list(loads)), operands, spaces, outs, out_spaces, scratch,
    )


class Partial:
    def __init__(self, left, right, last=True):
        self.sources = [left, right]
        self.last = last
        self.pair = 2 * left.shape[0] // MEMBERS
        self.width = right.shape[0 if last else 1]
        self.scratch = [
            pltpu.VMEM(left.shape, left.dtype),
            pltpu.VMEM(right.shape, right.dtype),
            pltpu.SemaphoreType.DMA((2,)),
            pltpu.VMEM((left.shape[0], self.width), jnp.bfloat16),
        ]

    def begin(self, sources, scratch):
        self.left, self.right, sems, self.made = scratch
        self.loads = [
            pltpu.make_async_copy(source, held, sems.at[k])
            for k, (source, held) in enumerate(zip(sources, (self.left, self.right)))
        ]
        for copy in self.loads:
            copy.start()

    def wait(self):
        for copy in self.loads:
            copy.wait()

    def tile(self, k):
        rows = pl.ds(k * self.pair, self.pair)
        for start in range(0, self.width, 512):
            columns = pl.ds(start, 512)
            if self.last:
                value = contract_last(self.left[rows], self.right[columns, :])
            else:
                value = jnp.dot(
                    self.left[rows], self.right[:, columns], preferred_element_type=jnp.float32
                )
            self.made[rows, columns] = value.astype(jnp.bfloat16)


def scatter_kernel(orders, maker, cargo, *refs):
    refs = list(refs)
    heads = take(refs, len(maker.sources) if maker else 1)
    sources = take(refs, len(cargo.sources))
    (o_ref,) = take(refs, 1)
    targets = take(refs, len(cargo.outs))
    acc, rcore, came, core_send, core_recv, send_sem, recv_sem = take(refs, 7)
    here = place()
    rows = o_ref.shape[0]
    spans = [pl.ds(r0, size) for _, r0, size in orders]
    orders = [o for o, _, _ in orders]
    pieces = range(len(orders))
    if maker:
        maker.begin(heads, take(refs, len(maker.scratch)))
        p_ref = maker.made
    else:
        p_ref = heads[0]
        (load_sem,) = take(refs, 1)
    cargo.bind(here, sources, targets, refs)
    cargo.greet(here, NEAR)

    def away(p, mask):
        return pltpu.make_async_remote_copy(
            src_ref=spots(p_ref, slot("c", *subset(orders[p], mask)), rows, spans[p]),
            dst_ref=rcore.at[mask, spans[p]],
            send_sem=core_send.at[p, mask], recv_sem=core_recv.at[p, mask],
            device_id=flip(here, "c"), device_id_type=MESH,
        )

    def mine(p, mask):
        return spots(p_ref, slot(*subset(orders[p], mask)), rows, spans[p])

    def fetch(p, mask):
        return pltpu.make_async_copy(mine(p, mask), acc.at[mask, spans[p]], load_sem.at[p, mask])

    sent = []

    def hand_over(*masks):
        for mask in masks:
            for p in pieces:
                sent.append(away(p, mask))
                sent[-1].start()
                if not maker:
                    fetch(p, mask).start()

    sequence = [7, 3, 5, 1, 6, 2, 4, 0]
    if maker:
        cargo.start(0)
        maker.wait()
        for pairs, masks in (((7,), (7,)), ((4, 5, 6), (3, 5, 6)), ((1, 2, 3), (1, 2, 4)), ((0,), (0,))):
            for k in pairs:
                maker.tile(k)
            hand_over(*masks)
    else:
        hand_over(*sequence)
        cargo.start(0)

    def over(p, mask):
        k = (mask & -mask).bit_length() - 1
        return pltpu.make_async_remote_copy(
            src_ref=acc.at[mask, spans[p]], dst_ref=came.at[mask, spans[p]],
            send_sem=send_sem.at[p, mask], recv_sem=recv_sem.at[p, mask],
            device_id=flip(here, orders[p][k]), device_id_type=MESH,
        )

    for mask in sequence:
        for p in pieces:
            away(p, mask).wait_recv()
            if maker:
                acc[mask, spans[p]] = mine(p, mask)[...] + rcore[mask, spans[p]]
            else:
                fetch(p, mask).wait()
                acc[mask, spans[p]] = acc[mask, spans[p]] + rcore[mask, spans[p]]
            if mask & 1:
                sent.append(over(p, mask))
                sent[-1].start()
    cargo.start(1)
    for k in range(3):
        low = 1 << k
        for mask in [b for b in (6, 2, 4, 0) if b & (2 * low - 1) == 0]:
            for p in pieces:
                over(p, mask | low).wait_recv()
                if mask == 0 and k == 2:
                    o_ref[spans[p]] = acc[0, spans[p]].astype(jnp.float32) + came[
                        4, spans[p]
                    ].astype(jnp.float32)
                    continue
                acc[mask, spans[p]] = acc[mask, spans[p]] + came[mask | low, spans[p]]
                if mask & (2 * low):
                    sent.append(over(p, mask))
                    sent[-1].start()
        if k < 2:
            cargo.start(2 + k)
        if k == 1:
            cargo.finish(early=True)
            cargo.start(4)
    for copy in sent:
        copy.wait_send()
    cargo.finish()


def scatter_cube(partial, ident, loads=(), orders=None):
    maker = partial if isinstance(partial, Partial) else None
    total, width = (maker.sources[0].shape[0], maker.width) if maker else partial.shape
    rows = total // MEMBERS
    orders = orders or thirds(rows)
    operands = maker.sources if maker else [partial]
    semaphores = pltpu.SemaphoreType.DMA((len(orders), 8))
    return call(
        functools.partial(scatter_kernel, orders, maker),
        "scatter_cube", ident, Cargo(list(loads)), operands, [pltpu.HBM] * len(operands),
        [jax.ShapeDtypeStruct((rows, width), jnp.float32)], [pltpu.VMEM],
        [pltpu.VMEM((8, rows, width), jnp.bfloat16)] * 3 + [semaphores] * 4
        + (maker.scratch if maker else [semaphores]),
    )


def exchange_kernel(v_ref, o_ref, slots, send_sem, recv_sem):
    here = place()
    greet([flip(here, *names) for names in PEERS])
    copies = []
    for names in PEERS:
        k = slot(*names)
        copies.append(pltpu.make_async_remote_copy(
            src_ref=v_ref, dst_ref=slots.at[k], send_sem=send_sem.at[k], recv_sem=recv_sem.at[k],
            device_id=flip(here, *names), device_id_type=MESH,
        ))
        copies[-1].start()
    for copy in copies:
        copy.wait_recv()
    slots[0] = v_ref[...]
    o_ref[...] = jnp.zeros_like(o_ref)
    for row in range(v_ref.shape[0]):
        kind, mine = divmod(row, MEMBERS)
        terms = [
            slots[k, pl.ds(kind * MEMBERS + SLOT[SLOTS[mine] ^ SLOTS[k]], 1), :]
            for k in range(MEMBERS)
        ]
        while len(terms) > 1:
            terms = [terms[2 * i] + terms[2 * i + 1] for i in range(len(terms) // 2)]
        o_ref[mine, pl.ds(kind, 1), :] = terms[0]
    for copy in copies:
        copy.wait_send()


def sum_cube(values, ident):
    shape = values.shape
    return pl.pallas_call(
        exchange_kernel,
        out_shape=jax.ShapeDtypeStruct((MEMBERS, 8, shape[1]), jnp.float32),
        in_specs=[pl.BlockSpec(memory_space=pltpu.VMEM)],
        out_specs=pl.BlockSpec(memory_space=pltpu.VMEM),
        scratch_shapes=[
            pltpu.VMEM((MEMBERS,) + shape, jnp.float32),
            pltpu.SemaphoreType.DMA((MEMBERS,)),
            pltpu.SemaphoreType.DMA((MEMBERS,)),
        ],
        compiler_params=pltpu.CompilerParams(collective_id=ident, has_side_effects=True),
        cost_estimate=pl.CostEstimate(flops=0, bytes_accessed=20 * MIB, transcendentals=0),
        name="sum_cube",
    )(values)


def rope_tables(positions):
    frequency = theta_base ** (-2.0 * jnp.arange(HD // 2).astype(jnp.float32) / HD)
    angles = positions[:, None] * frequency[None, :]
    cosines, sines = jnp.cos(angles), jnp.sin(angles)
    return jnp.concatenate([cosines, cosines, -sines, sines], axis=1)


def normalize(values, scales):
    inverse = lax.rsqrt(jnp.mean(values * values, axis=-1, keepdims=True) + epsilon)
    return (values * inverse * scales, inverse)


def norm_back(upstream, values, inverse, scales):
    unit_rows = values * inverse
    scaled = upstream * scales
    value_grad = inverse * (
        scaled - unit_rows * jnp.mean(scaled * unit_rows, axis=-1, keepdims=True)
    )
    return (value_grad, jnp.sum(upstream * unit_rows, axis=0))


def contract_last(operand, matrix):
    return lax.dot_general(
        operand, matrix, (((1,), (1,)), ((), ())), preferred_element_type=jnp.float32
    )


def contract_first(operand, matrix):
    return lax.dot_general(
        operand, matrix, (((0,), (0,)), ((), ())), preferred_element_type=jnp.float32
    )


TOGETHER = 8


def turn(values, cos_table, sin_table):
    return values * cos_table + pltpu.roll(values, HD // 2, 1) * sin_table


def project_kernel(x_ref, w_ref, o_ref, sums_out):
    value = jnp.dot(x_ref[...], w_ref[...], preferred_element_type=jnp.float32)
    o_ref[...] = value
    rows = x_ref.shape[0] // TOGETHER
    for block in range(TOGETHER):
        for kind in range(2):
            part = value[block * rows : (block + 1) * rows, kind * HD : (kind + 1) * HD]
            sums_out[pl.ds(kind * MEMBERS + pl.program_id(0) * TOGETHER + block, 1)] = jnp.sum(
                (part * part).T, axis=0, keepdims=True
            )


def rope_of(positions, table):
    place_of = lax.broadcasted_iota(jnp.int32, (positions.shape[0], table.shape[0]), 1)
    chosen = (place_of.astype(jnp.float32) == positions).astype(jnp.float32)
    found = jnp.dot(
        chosen, table, preferred_element_type=jnp.float32, precision=lax.Precision.HIGHEST
    )
    return found[:, :HD], found[:, HD:]


def attend_kernel(width, p_ref, s_ref, b_ref, t_ref, g_ref, *outs):
    q_out, k_out, v_out, qu_out, ku_out, a_out, o_out = outs
    rows = p_ref.shape[0] // TOGETHER
    for block in range(TOGETHER):
        span = pl.ds(block * rows, rows)
        scales = lax.rsqrt(s_ref[block].T / width + epsilon)
        begin = b_ref[block].T[:, 0:1]
        row = lax.broadcasted_iota(jnp.int32, (rows, 1), 0).astype(jnp.float32)
        cos_table, sin_table = rope_of(row - begin, t_ref[...])
        query_unit = p_ref[span, 0:HD] * scales[:, 0:1]
        key_unit = p_ref[span, HD : 2 * HD] * scales[:, 1:2]
        values = p_ref[span, 2 * HD : 3 * HD].astype(jnp.bfloat16)
        queries = turn(query_unit * g_ref[0:1], cos_table, sin_table).astype(jnp.bfloat16)
        keys = turn(key_unit * g_ref[1:2], cos_table, sin_table).astype(jnp.bfloat16)
        scores = contract_last(queries, keys) * (1.0 / math.sqrt(HD))
        column = lax.broadcasted_iota(jnp.int32, scores.shape, 1).astype(jnp.float32)
        scores = jnp.where((column <= row) & (column >= begin), scores, -1e30)
        exponent = jnp.exp(scores - jnp.max(scores, axis=1, keepdims=True))
        attention = exponent / jnp.sum(exponent, axis=1, keepdims=True)
        q_out[span] = queries
        k_out[span] = keys
        v_out[span] = values
        qu_out[span] = query_unit
        ku_out[span] = key_unit
        a_out[span] = attention
        o_out[span] = jnp.dot(
            attention.astype(jnp.bfloat16), values, preferred_element_type=jnp.float32
        ).astype(jnp.bfloat16)


def attend_back_kernel(
    d_ref, q_ref, k_ref, v_ref, qu_ref, ku_ref, a_ref, b_ref, t_ref, g_ref, *outs
):
    qs_out, ks_out, vg_out, dots_out, gains_out = outs
    rows = d_ref.shape[0] // TOGETHER
    step = pl.program_id(0)
    scale = 1.0 / math.sqrt(HD)

    @pl.when(step == 0)
    def _():
        gains_out[...] = jnp.zeros_like(gains_out)

    for block in range(TOGETHER):
        span = pl.ds(block * rows, rows)
        grad, attention = d_ref[span], a_ref[span]
        prob_grad = contract_last(grad, v_ref[span])
        weighed = jnp.sum(attention * prob_grad, axis=1, keepdims=True)
        score_grad = (attention * (prob_grad - weighed)).astype(jnp.bfloat16)
        vg_out[span] = contract_first(attention.astype(jnp.bfloat16), grad).astype(jnp.bfloat16)
        query_grad = jnp.dot(score_grad, k_ref[span], preferred_element_type=jnp.float32) * scale
        key_grad = contract_first(score_grad, q_ref[span]) * scale
        row = lax.broadcasted_iota(jnp.int32, (rows, 1), 0).astype(jnp.float32)
        cos_table, sin_table = rope_of(row - b_ref[block].T[:, 0:1], t_ref[...])
        sin_table = -sin_table
        query_grad = turn(query_grad, cos_table, sin_table)
        key_grad = turn(key_grad, cos_table, sin_table)
        query_unit, key_unit = qu_ref[span], ku_ref[span]
        gains_out[0:1] += jnp.sum(query_grad * query_unit, axis=0, keepdims=True)
        gains_out[1:2] += jnp.sum(key_grad * key_unit, axis=0, keepdims=True)
        query_grad = query_grad * g_ref[0:1]
        key_grad = key_grad * g_ref[1:2]
        qs_out[span] = query_grad
        ks_out[span] = key_grad
        query_dot = jnp.sum((query_grad * query_unit).T, axis=0, keepdims=True)
        key_dot = jnp.sum((key_grad * key_unit).T, axis=0, keepdims=True)
        dots_out[pl.ds(step * TOGETHER + block, 1)] = query_dot
        dots_out[pl.ds(MEMBERS + step * TOGETHER + block, 1)] = key_dot


def project_back_kernel(width, s_ref, t_ref, qu_ref, ku_ref, qs_ref, ks_ref, vg_ref, o_ref):
    rows = qu_ref.shape[0] // TOGETHER
    for block in range(TOGETHER):
        span = pl.ds(block * rows, rows)
        scales = lax.rsqrt(s_ref[block].T / width + epsilon)
        means = t_ref[block].T / width
        query_grad = scales[:, 0:1] * (qs_ref[span] - qu_ref[span] * means[:, 0:1])
        key_grad = scales[:, 1:2] * (ks_ref[span] - ku_ref[span] * means[:, 1:2])
        o_ref[span, 0:HD] = query_grad.astype(jnp.bfloat16)
        o_ref[span, HD : 2 * HD] = key_grad.astype(jnp.bfloat16)
        o_ref[span, 2 * HD : 3 * HD] = vg_ref[span]


def by_blocks(body, name, operands, outs, whole=()):
    total = operands[0].shape[0]
    if operands[0].ndim == 3:
        total = total * operands[0].shape[2]
    span = total // MEMBERS * TOGETHER

    def spec(array):
        shape = array.shape
        if len(shape) == 3:
            return pl.BlockSpec((TOGETHER,) + shape[1:], lambda k: (k, 0, 0))
        if shape[0] == total:
            return pl.BlockSpec((span, shape[1]), lambda k: (k, 0))
        return pl.BlockSpec(shape, lambda k: (0, 0))

    return pl.pallas_call(
        body,
        grid=(MEMBERS // TOGETHER,),
        out_shape=[pltpu.HBM(v.shape, v.dtype) for v in outs],
        in_specs=[
            pl.BlockSpec(v.shape, lambda k: (0, 0)) if n in whole else spec(v)
            for n, v in enumerate(operands)
        ],
        out_specs=[spec(v) for v in outs],
        compiler_params=pltpu.CompilerParams(vmem_limit_bytes=24 * MIB),
        cost_estimate=pl.CostEstimate(
            flops=4 * total * HD * HD, bytes_accessed=8 * MIB, transcendentals=total * HD
        ),
        name=name,
    )(*[in_hbm(v, pltpu.HBM) for v in operands])


def finish_kernel(mine_ref, came_ref, o_ref):
    own = pl.program_id(1) == lax.axis_index("x")
    o_ref[...] = jnp.where(own, mine_ref[...], came_ref[...]).astype(jnp.float32)


def whole_rows(mine, came, parts):
    rows, width = mine.shape
    step = width // parts
    half = pl.BlockSpec((rows, step), lambda p, x: (0, p))
    return pl.pallas_call(
        finish_kernel,
        grid=(parts, 2),
        out_shape=jax.ShapeDtypeStruct((rows, 2 * width), jnp.float32),
        in_specs=[half, half],
        out_specs=pl.BlockSpec((rows, step), lambda p, x: (0, 2 * p + x)),
        compiler_params=pltpu.CompilerParams(vmem_limit_bytes=32 * MIB),
        cost_estimate=pl.CostEstimate(
            flops=0, bytes_accessed=12 * rows * width, transcendentals=0
        ),
        name="whole_rows",
    )(mine, came)


def owners_product(left, right, parts=1, columns=None, **options):
    if left.shape[1] // (lax.axis_size("zh") * SIDES) % 128 == 0:
        return Product(left, right, parts, columns=columns, **options)
    if columns is not None:
        right = right[:, columns[0] : sum(columns)]
    return Owners(contract_first(left, right).astype(jnp.bfloat16), parts, **options)


def heads_are_owners(rows):
    return lax.axis_size("zh") == 2 and rows == HD


def gathered_head_rows(weight):
    full = lax.all_gather(weight, OWNERS, axis=0, tiled=True)
    head = lax.axis_index(("x", "zl", "y", "c"))
    return lax.dynamic_slice_in_dim(full, head * HD, HD, axis=0)


def summed_head_rows(grad_rows, rows):
    head = lax.axis_index(("x", "zl", "y", "c"))
    full = jnp.zeros((MEMBERS * HD, grad_rows.shape[1]), jnp.float32)
    full = lax.dynamic_update_slice_in_dim(full, grad_rows, head * HD, axis=0)
    full = lax.psum(full, EVERY)
    return lax.dynamic_slice_in_dim(full, lax.axis_index(OWNERS) * rows, rows, axis=0)


def silu_grads(hidden_grad, gate_part, up_part):
    sigmoid_gate = jax.nn.sigmoid(gate_part)
    gate_grad = hidden_grad * up_part * sigmoid_gate * (1.0 + gate_part * (1.0 - sigmoid_gate))
    up_grad = hidden_grad * gate_part * sigmoid_gate
    return gate_grad.astype(jnp.bfloat16), up_grad.astype(jnp.bfloat16)


def shards(tokens, w_qkv, w_out, w_gate_up, w_down_t, gains, starts, cotangent):
    count_rows, width = tokens.shape
    owned = gains.shape[0]
    groups = lax.axis_size("zh")
    total = MEMBERS * count_rows
    direct = heads_are_owners(owned)
    local_rows = jnp.arange(count_rows, dtype=jnp.int32)
    seq_begin = lax.cummax(jnp.where(starts == 1, local_rows, 0), axis=0)

    rope_table = rope_tables(local_rows.astype(jnp.float32))
    gain_part = jnp.pad(gains.astype(jnp.float32).T, ((0, 4), (0, 0)))
    begin_part = jnp.broadcast_to(seq_begin.astype(jnp.float32)[None, :], (8, count_rows))
    z_first = (
        (("zl", "x", "y"), 0, count_rows // 2),
        (("zl", "y", "x"), count_rows // 2, count_rows // 2),
    )
    loads = [Few(gain_part, False), Few(begin_part, True), Columns(w_qkv, 3, near=3)]
    if direct:
        loads.append(HeadRows(w_out))
    tokens_all, gain_all, begin_all, qkv_cols, *out_other = gather_cube(
        tokens, 1, loads, z_first
    )
    same = lax.axis_index("x") == lax.axis_index("zh")
    if direct:
        out_rows = jnp.where(same, w_out, out_other[0])
    else:
        out_rows = gathered_head_rows(w_out)
    gain_rows = gain_all[:, :4].transpose(1, 0, 2).reshape(4, width)
    head = lax.axis_index(("x", "zl", "y", "c"))
    head_gains = lax.dynamic_slice_in_dim(gain_rows, head * HD, HD, axis=1)
    def of(width, kind):
        return jax.ShapeDtypeStruct((total, width), kind)

    narrow, wide = of(HD, jnp.bfloat16), of(HD, jnp.float32)
    sums = jax.ShapeDtypeStruct((2 * MEMBERS, count_rows), jnp.float32)
    projected, squares = by_blocks(
        project_kernel, "project", [tokens_all, qkv_cols], [of(3 * HD, jnp.float32), sums],
        whole=(1,),
    )
    squares = sum_cube(squares, 2)
    query_bf, key_bf, value_bf, query_unit, key_unit, attention, attended = by_blocks(
        functools.partial(attend_kernel, width), "attend",
        [projected, squares, begin_all, rope_table, head_gains],
        [narrow, narrow, narrow, wide, wide, wide, narrow],
    )
    x_most = halves(count_rows, "x", "y", "zl")
    x_or_y = (
        (("x", "y", "zl"), 0, count_rows // 2),
        (("y", "x", "zl"), count_rows // 2, count_rows // 2),
    )
    x_last = halves(count_rows, "zl", "y", "x")
    branch, gate_up_cols = scatter_cube(
        Partial(attended, out_rows, False),
        3, [Columns(w_gate_up, 2, near=1)], x_most,
    )
    branch_norm, branch_inv = normalize(branch, gain_rows[2])
    middle = tokens.astype(jnp.float32) + branch_norm
    hidden_bf, gate_up, middle_all, down_cols = gather_cube(
        middle.astype(jnp.bfloat16), 4, [Columns(w_down_t, far=1, near=3)], x_last,
        FeedForward(gate_up_cols, total), eager=True,
    )
    (feed_out,) = scatter_cube(Partial(hidden_bf, down_cols), 5)
    feed_norm, feed_inv = normalize(feed_out, gain_rows[3])
    mixed = (middle + feed_norm).astype(jnp.bfloat16)

    upstream = cotangent.astype(jnp.float32)
    feed_grad, gain_feed = norm_back(upstream, feed_out, feed_inv, gain_rows[3])
    gate_up_bf, middle_part, feed_all = gather_cube(
        feed_grad.astype(jnp.bfloat16), 6, work=FeedBack(down_cols, gate_up_cols, gate_up),
        eager=True,
    )
    feed_width = hidden_bf.shape[1]
    middle_sum, gate_sum, gate_other, up_sum = scatter_cube(
        middle_part, 7,
        [
            owners_product(
                middle_all, gate_up_bf, columns=(0, feed_width), near=1, swap=True, early=True
            ),
            owners_product(
                middle_all, gate_up_bf, columns=(feed_width, feed_width), far=1, near=2
            ),
        ], x_most,
    )
    middle_grad = upstream + middle_sum
    branch_grad, gain_branch = norm_back(middle_grad, branch, branch_inv, gain_rows[2])
    attended_grad, out_grad, down_sum, up_other = gather_cube(
        branch_grad.astype(jnp.bfloat16), 8,
        [
            owners_product(feed_all, hidden_bf, far=1, near=3),
            Whole(up_sum, "x", near=3),
        ], z_first, BranchBack(out_rows, attended),
    )
    half = down_sum.shape[0] // 2
    down_first = lax.ppermute(down_sum[:half], "x", [(0, 1), (1, 0)])
    query_scaled, key_scaled, value_grad, dots, gain_head = by_blocks(
        attend_back_kernel, "attend_back",
        [
            attended_grad, query_bf, key_bf, value_bf, query_unit, key_unit, attention,
            begin_all, rope_table, head_gains,
        ],
        [
            wide, wide, narrow,
            sums,
            jax.ShapeDtypeStruct((8, HD), jnp.float32),
        ],
    )
    dots = sum_cube(dots, 9)
    (projected_bf,) = by_blocks(
        functools.partial(project_back_kernel, width), "project_back",
        [squares, dots, query_unit, key_unit, query_scaled, key_scaled, value_grad],
        [of(3 * HD, jnp.bfloat16)],
    )

    gain_terms = jnp.concatenate(
        [
            lax.dynamic_update_slice_in_dim(
                jnp.zeros((2, width), jnp.float32), gain_head[:2], head * HD, axis=1
            ),
            jnp.stack([gain_branch, gain_feed]),
        ]
    )
    lanes = -(-owned // 128) * 128
    gain_terms = jnp.pad(
        gain_terms.reshape(4, groups * SIDES, owned).transpose(1, 0, 2),
        ((0, 0), (0, 4), (0, lanes - owned)),
    ).reshape(groups * SIDES * 8, lanes)
    loads = [
        owners_product(tokens_all, projected_bf, 3, swap=True, near=1, early=True),
        Owners(gain_terms, swap=True, fold=True, early=True),
        FinalRows((gate_sum, gate_other), (up_sum, up_other)),
        Whole(down_sum[half:], "x", near=1),
    ]
    if direct:
        loads.append(HeadSums(out_grad, near=1, early=True))
    (
        tokens_sum, qkv_sum, qkv_other, gain_sum, gain_other, grad_gate_up, down_other, *out_both
    ) = scatter_cube(
        Partial(projected_bf, qkv_cols), 10, loads, x_or_y
    )
    grad_tokens = middle_grad + tokens_sum
    if direct:
        first, second = (jnp.where(same, out_both[k], out_both[1 - k]) for k in range(2))
        grad_out = jnp.concatenate([first, second], axis=0).astype(jnp.float32)
    else:
        grad_out = summed_head_rows(out_grad.astype(jnp.float32), owned)
    grad_qkv = whole_rows(qkv_sum, qkv_other, 3)
    down_other = jnp.concatenate([down_first, down_other], axis=0)
    grad_down_t = whole_rows(down_sum, down_other, 1)
    grad_gains = (gain_sum + gain_other)[:4, :owned].T
    return (mixed, grad_tokens, grad_qkv, grad_out, grad_gate_up, grad_down_t, grad_gains)


def solution(mesh):
    sizes = dict(mesh.shape)
    groups = sizes["fsdp"] // SIDES
    finer = Mesh(mesh.devices.reshape(2, groups, 2, 2, 2), EVERY)
    return jax.shard_map(
        shards,
        mesh=finer,
        in_specs=(
            P(EVERY, None),
            P(OWNERS, None),
            P(OWNERS, None),
            P(OWNERS, None),
            P(OWNERS, None),
            P(OWNERS, None),
            P(EVERY),
            P(EVERY, None),
        ),
        out_specs=(
            P(EVERY, None),
            P(EVERY, None),
            P(OWNERS, None),
            P(OWNERS, None),
            P(OWNERS, None),
            P(OWNERS, None),
            P(OWNERS, None),
        ),
        check_vma=False,
    )
```
